128 devices in a mesh: ctx: 32 (over y, x, core), chan: 4 (over z).
Axes of the slice: x: 4, y: 4, z: 4, core: 2. Of those that a mesh axis runs over, the one named last changes fastest.
Arguments:
- hyena_q: bfloat16 [4096, 8192], P('ctx', 'chan'), may hold values from -20 to 20
- hyena_k: bfloat16 [4096, 8192], P('ctx', 'chan'), may hold values from -6 to 6
- hyena_v: bfloat16 [4096, 8192], P('ctx', 'chan'), may hold values from -6 to 6
- hyena_grad: bfloat16 [4096, 8192], P('ctx', 'chan'), may hold values from -6 to 6
- pole_rate: float32 [16, 8192], P(None, 'chan'), may hold values from 0.00024414062 to 0.033333335
- residue: float32 [16, 8192], P(None, 'chan'), may hold values from -1.5 to 1.5
- norm_gain: float32 [8192], P('chan'), may hold values from 0.25 to 1.75
- doc_ids: int32 [4096], P('ctx'), may hold values from 0 to 3, never falling along the last dimension, each value on 1 to 2048 neighbouring positions
- attn_q: bfloat16 [4096, 4096], P('ctx', 'chan'), may hold values from -5 to 5
- attn_k: bfloat16 [4096, 4096], P('ctx', 'chan'), may hold values from -5 to 5
- attn_v: bfloat16 [4096, 4096], P('ctx', 'chan'), may hold values from -6 to 6
- attn_grad: bfloat16 [4096, 4096], P('ctx', 'chan'), may hold values from -6 to 6
Outputs:
- grad_hq: bfloat16 [4096, 8192], P('ctx', 'chan')
- grad_hk: bfloat16 [4096, 8192], P('ctx', 'chan')
- grad_hv: bfloat16 [4096, 8192], P('ctx', 'chan')
- grad_residue: float32 [16, 8192], P(None, 'chan')
- grad_gain: float32 [8192], P('chan')
- grad_aq: bfloat16 [4096, 4096], P('ctx', 'chan')
- grad_ak: bfloat16 [4096, 4096], P('ctx', 'chan')
- grad_av: bfloat16 [4096, 4096], P('ctx', 'chan')
The draws below stay inside these ranges and needn't reach their ends.
Inputs may be any that keep to these rules, and one draw needn't show every extreme that they name: doc_ids never falls along the tokens; each of the 4 documents is one contiguous run of tokens, and the longest run holds exactly half of the 4096 tokens.
All inputs are finite; a program needn't handle non-finite values.
Results may differ from the reference program's by a relative error of at most 0.015.
Values may be sent and summed in bfloat16 or wider, within the bound.
No kernel may reach another device: no remote copies, remote signals or barrier semaphores. Data moves between devices by JAX's collectives and lax.ppermute only.
A program may use at most 128 MiB of HBM per device.

```python
import math
import jax
import jax.numpy as jnp
import numpy as np
from jax import lax

D = 8192
HEAD_DIM = 128
POLES = 16
A_HEADS = 32
TOK_DEV = 128
DOCS = 4
TOKENS = 4096
A_WIDTH = 4096


def draw_hyena_q(key, part):
    key = jax.random.fold_in(key, 11)
    row_key, base_key = jax.random.split(key)
    columns = jnp.arange(D, dtype=jnp.float32) / D
    rows = 10.0 ** jax.random.uniform(row_key, (TOKENS, 1))
    base = jax.random.truncated_normal(base_key, -4.0, 4.0, (TOKENS, D))
    return (base * rows * 10.0 ** columns / 20.0).astype(jnp.bfloat16)


def draw_attn_q(key, part):
    key = jax.random.fold_in(key, 21)
    base = jax.random.truncated_normal(key, -4.0, 4.0, (TOKENS, A_HEADS * HEAD_DIM))
    return base.astype(jnp.bfloat16)


def draw_attn_k(key, part):
    key = jax.random.fold_in(key, 22)
    base = jax.random.truncated_normal(key, -4.0, 4.0, (TOKENS, A_HEADS * HEAD_DIM))
    return base.astype(jnp.bfloat16)


def levels(stream_key, shape, cuts, least, high):
    gain, own = 1.0, jax.random.fold_in(stream_key, 6)
    for axis_at, shards_of in cuts:
        steps = jnp.exp(jax.random.uniform(jax.random.fold_in(own, axis_at), (shards_of,), jnp.float32, least / len(cuts), high / len(cuts)))
        gain = gain * jnp.repeat(steps, shape[axis_at] // shards_of).reshape([-1 if axis == axis_at else 1 for axis in range(len(shape))])
    return gain


def profile(count, total, most, slope):
    portions = [(1 << 20) // math.isqrt(standing ** slope) + 1 for standing in range(2, count + 1)]
    spare, holding = total - most - (count - 1), [1] * (count - 1)
    while spare > 0:
        free = [i for i in range(count - 1) if holding[i] < most]
        whole, budget = sum([portions[i] for i in free]), spare
        for i in free:
            addition = min(most - holding[i], max(1, budget * portions[i] // whole), spare)
            holding[i] = holding[i] + addition
            spare = spare - addition
    return np.array([most] + holding)


def uneven(rng, number_of, total, reach, slope):
    if number_of == 2:
        one = jax.random.randint(rng, (), max(1, total - reach), min(reach, total - 1) + 1)
        return jnp.stack([one, total - one])
    lengths = jnp.asarray(profile(number_of, total, reach, slope), jnp.int32)
    twos = (number_of - 1) // 2
    source_of, taker = lengths[1:1 + 2 * twos:2], lengths[2:2 + 2 * twos:2]
    room = jnp.minimum(source_of - 1, reach - taker)
    shifted = jax.random.randint(jax.random.fold_in(rng, 1), (twos,), 0, 1 << 20) % (room + 1)
    lengths = lengths.at[1:1 + 2 * twos:2].set(source_of - shifted).at[2:2 + 2 * twos:2].set(taker + shifted)
    return lengths[jax.random.permutation(jax.random.fold_in(rng, 2), number_of)]


def centred(rng, dims, deviation, reach, shards=(), kind=jnp.bfloat16):
    gain = levels(rng, dims, shards, -0.22, 0.18) if shards else 1.0
    values = jax.random.normal(rng, dims, jnp.float32) * deviation * gain
    return jnp.minimum(jnp.maximum(values, -reach), reach).astype(kind)


def setup_inputs(seed: int = 0) -> dict:
    seeds = jax.random.split(jax.random.key(seed), 13)
    return {
        "hyena_q": draw_hyena_q(jax.random.fold_in(seeds[12], 71), 0),
        "hyena_k": centred(seeds[1], (TOKENS, D), 1.0, 6.0, ((0, 32), (1, 4))),
        "hyena_v": centred(seeds[2], (TOKENS, D), 1.0, 6.0, ((0, 32), (1, 4))),
        "hyena_grad": centred(seeds[3], (TOKENS, D), 1.0, 6.0, ((0, 32), (1, 4))),
        "pole_rate": jnp.clip(jnp.exp(math.log(0.033333335) - 4.9165688 * jax.random.uniform(seeds[4], (POLES, D), jnp.float32) ** levels(seeds[4], (POLES, D), ((1, 4),), -0.2, 0.2)), 0.00024414062, 0.033333335),
        "residue": centred(seeds[5], (POLES, D), POLES ** -0.5, 1.5, ((1, 4),), jnp.float32),
        "norm_gain": jnp.clip(1.0 + 0.15 * jax.random.normal(seeds[6], (D,), jnp.float32), 0.25, 1.75),
        "doc_ids": jnp.searchsorted(jnp.cumsum(uneven(seeds[7], DOCS, TOKENS, TOKENS // 2, 0)), jnp.arange(TOKENS), side="right").astype(jnp.int32),
        "attn_q": draw_attn_q(jax.random.fold_in(seeds[12], 71), 0),
        "attn_k": draw_attn_k(jax.random.fold_in(seeds[12], 71), 0),
        "attn_v": centred(seeds[10], (TOKENS, A_WIDTH), 1.0, 6.0, ((0, 32), (1, 4))),
        "attn_grad": centred(seeds[11], (TOKENS, A_WIDTH), 1.0, 6.0, ((0, 32), (1, 4))),
    }


EPSILON = 1e-06

def reference(hyena_q, hyena_k, hyena_v, hyena_grad, pole_rate, residue, norm_gain, doc_ids, attn_q, attn_k, attn_v, attn_grad):
    decay = jnp.exp(-pole_rate)
    scaling = jnp.sqrt(-jnp.expm1(-2.0 * pole_rate))
    weight = residue * scaling
    mixed = hyena_k.astype(jnp.float32) * hyena_v.astype(jnp.float32)
    joined = (doc_ids[1:] == doc_ids[:-1]).astype(jnp.float32)
    after_prev = jnp.concatenate([jnp.zeros((1,), jnp.float32), joined])
    before_next = jnp.concatenate([joined, jnp.zeros((1,), jnp.float32)])

    def forward_step(states, row):
        keep, source = row
        states = keep * decay * states + source[None, :]
        return (states, lax.optimization_barrier(jnp.sum(weight * states, axis=0)))
    _, filtered = lax.scan(forward_step, jnp.zeros((POLES, D), jnp.float32), (after_prev, mixed))
    query_vals = hyena_q.astype(jnp.float32)
    out_y = query_vals * filtered
    inv_rms = lax.rsqrt(lax.optimization_barrier(jnp.mean(out_y * out_y, axis=1)) + EPSILON)
    scaled_grad = hyena_grad.astype(jnp.float32) * norm_gain
    along = lax.optimization_barrier(jnp.sum(scaled_grad * out_y, axis=1))
    grad_y = inv_rms[:, None] * scaled_grad - out_y * (inv_rms ** 3 * along / D)[:, None]
    grad_hq = (grad_y * filtered).astype(jnp.bfloat16)
    grad_filtered = grad_y * query_vals
    grad_gain = lax.optimization_barrier(jnp.sum(hyena_grad.astype(jnp.float32) * out_y * inv_rms[:, None], axis=0))

    def backward_step(carry, row):
        states, totals = carry
        keep, source, feed = row
        states = keep * decay * states + source[None, :]
        return ((states, totals + states * feed[None, :]), lax.optimization_barrier(jnp.sum(weight * states, axis=0)))
    start = (jnp.zeros((POLES, D), jnp.float32), jnp.zeros((POLES, D), jnp.float32))
    (_, totals), grad_mixed = lax.scan(backward_step, start, (before_next, grad_filtered, mixed), reverse=True)
    grad_hk = (grad_mixed * hyena_v.astype(jnp.float32)).astype(jnp.bfloat16)
    grad_hv = (grad_mixed * hyena_k.astype(jnp.float32)).astype(jnp.bfloat16)
    grad_residue = scaling * totals
    heads = attn_q.shape[1] // HEAD_DIM
    scale = HEAD_DIM ** (-0.5)
    keys = attn_k.astype(jnp.float32).reshape(TOKENS, heads, HEAD_DIM)
    values = attn_v.astype(jnp.float32).reshape(TOKENS, heads, HEAD_DIM)
    positions = jnp.arange(TOKENS, dtype=jnp.int32)

    def one_rank(sums, rank):
        first = rank * TOK_DEV
        queries = lax.dynamic_slice_in_dim(attn_q, first, TOK_DEV, 0).astype(jnp.float32).reshape(TOK_DEV, heads, HEAD_DIM)
        backs = lax.dynamic_slice_in_dim(attn_grad, first, TOK_DEV, 0).astype(jnp.float32).reshape(TOK_DEV, heads, HEAD_DIM)
        row_docs = lax.dynamic_slice_in_dim(doc_ids, first, TOK_DEV, 0)
        row_pos = first + jnp.arange(TOK_DEV, dtype=jnp.int32)
        valid = (positions[None, :] <= row_pos[:, None]) & (doc_ids[None, :] == row_docs[:, None])
        valid = valid[None]
        scores = jnp.einsum('thd,khd->htk', queries, keys) * scale
        peak = lax.optimization_barrier(jnp.max(jnp.where(valid, scores, -jnp.inf), axis=2))
        total = lax.optimization_barrier(jnp.sum(jnp.where(valid, jnp.exp(scores - peak[..., None]), 0.0), axis=2))
        log_total = peak + jnp.log(total)
        probability = jnp.where(valid, jnp.exp(scores - log_total[..., None]), 0.0)
        grad_prob = jnp.einsum('thd,khd->htk', backs, values)
        centre = lax.optimization_barrier(jnp.sum(probability * grad_prob, axis=2))
        dscores = lax.optimization_barrier((probability * (grad_prob - centre[..., None])).astype(jnp.bfloat16)).astype(jnp.float32)
        rounded = lax.optimization_barrier(probability.astype(jnp.bfloat16)).astype(jnp.float32)
        grad_rows = (scale * jnp.einsum('htk,khd->thd', dscores, keys)).astype(jnp.bfloat16)
        key_part = lax.optimization_barrier((scale * jnp.einsum('htk,thd->khd', dscores, queries)).astype(jnp.bfloat16)).astype(jnp.float32)
        value_part = lax.optimization_barrier(jnp.einsum('htk,thd->khd', rounded, backs).astype(jnp.bfloat16)).astype(jnp.float32)
        return ((sums[0] + key_part, sums[1] + value_part), grad_rows)
    zeros = jnp.zeros((TOKENS, heads, HEAD_DIM), jnp.float32)
    ranks = jnp.arange(TOKENS // TOK_DEV, dtype=jnp.int32)
    (key_sum, value_sum), query_rows = lax.scan(one_rank, (zeros, zeros), ranks)
    grad_aq = query_rows.reshape(TOKENS, heads * HEAD_DIM)
    grad_ak = key_sum.astype(jnp.bfloat16).reshape(TOKENS, heads * HEAD_DIM)
    grad_av = value_sum.astype(jnp.bfloat16).reshape(TOKENS, heads * HEAD_DIM)
    return (grad_hq, grad_hk, grad_hv, grad_residue, grad_gain, grad_aq, grad_ak, grad_av)
```

```python
import jax
import jax.numpy as jnp
from jax import lax
from jax.experimental import pallas as pl
from jax.experimental.pallas import tpu as pltpu
from jax.sharding import PartitionSpec as P

D = 8192
HEAD_DIM = 128
EPSILON = 1e-06
FLOOR_SCORE = -1e30

TOK = 128
CH = 2048
POLES = 16
LANES = 128
CHUNKS = CH // LANES
GROUP = 16
HALF = GROUP * TOK
SPAN = 8
SCALE = HEAD_DIM ** (-0.5)
LOG2E = 1.4426950408889634

ROW_LO, ROW_DOC, ROW_K, ROW_V, ROW_Q, ROW_G, ROWS_IN = 16, 32, 48, 112, 176, 240, 304
OUT_RES, OUT_GAIN, OUT_Q, OUT_KV, ROWS_OUT = 32, 64, 80, 144, 272

TILE = 256
N_TILES = 2 * HALF // TILE
Q_TILES = 4

F32 = jnp.float32
BF16 = jnp.bfloat16


def call(kernel, outs, *args, scratch=(), smem=(), flops=0, nbytes=0, vmem=24 << 20, specs=None):
    grid = (1,) if specs else ()
    specs = specs or {}
    ins = [
        pl.BlockSpec(memory_space=pltpu.SMEM) if i in smem
        else specs.get(i, pl.BlockSpec(memory_space=pltpu.VMEM))
        for i in range(len(args))
    ]
    shapes = [jax.ShapeDtypeStruct(shape, kind) for shape, kind in outs]
    return pl.pallas_call(
        kernel,
        out_shape=shapes,
        grid=grid,
        in_specs=ins,
        out_specs=[pl.BlockSpec(memory_space=pltpu.VMEM) for _ in outs],
        scratch_shapes=list(scratch),
        cost_estimate=pl.CostEstimate(flops=flops, bytes_accessed=nbytes, transcendentals=0),
        compiler_params=pltpu.CompilerParams(vmem_limit_bytes=vmem),
    )(*args)


def every(start, size):
    return pl.ds(start, size, stride=CHUNKS)


def lanes(j):
    return slice(LANES * j, LANES * (j + 1))


def split(value):
    high = value.astype(BF16)
    return high, (value - high.astype(F32)).astype(BF16)


def scaling_of(rate):
    y = 2.0 * rate
    series = 1.0 - y / 6.0
    for k in (5.0, 4.0, 3.0, 2.0):
        series = 1.0 - y / k * series
    return jnp.sqrt(y * series)


def forward_groups(docs, step, state):
    def group(i, state):
        first = i * SPAN

        def plain(state):
            for u in range(SPAN):
                state = step(first + u, state)
            return state

        def cut(state):
            for u in range(SPAN):
                t = first + u
                keep = jnp.where(docs[t] == docs[jnp.maximum(t - 1, 0)], 1.0, 0.0)
                state = step(t, tuple(s * keep for s in state))
            return state

        whole = docs[jnp.maximum(first - 1, 0)] == docs[first + SPAN - 1]
        return lax.cond(whole, plain, cut, state)

    return lax.fori_loop(0, TOK // SPAN, group, state)


def backward_groups(docs, step, state, count):
    def group(i, state):
        first = TOK - SPAN - i * SPAN

        def plain(state):
            for u in reversed(range(SPAN)):
                state = step(first + u, state)
            return state

        def cut(state):
            for u in reversed(range(SPAN)):
                t = first + u
                keep = jnp.where(docs[t] == docs[jnp.minimum(t + 1, TOK - 1)], 1.0, 0.0)
                state = tuple(s * keep for s in state[:count]) + tuple(state[count:])
                state = step(t, state)
            return state

        whole = docs[first] == docs[jnp.minimum(first + SPAN, TOK - 1)]
        return lax.cond(whole, plain, cut, state)

    return lax.fori_loop(0, TOK // SPAN, group, state)


def first_kernel(docs, doc_row, hk, hv, rate, res, aq, ak, av, ag, send, m, dec, wgt, ends):
    rates = rate[...]
    decay = jnp.exp(-rates)
    weight = res[...] * scaling_of(rates)
    for j in range(CHUNKS):
        dec[every(j, POLES), :] = decay[:, lanes(j)]
        wgt[every(j, POLES), :] = weight[:, lanes(j)]
    for j in range(CHUNKS):
        m[every(j, TOK), :] = hk[:, lanes(j)].astype(F32) * hv[:, lanes(j)].astype(F32)
    for g in range(2):
        kept = [dec[n * 16 + 8 * g : n * 16 + 8 * g + 8, :] for n in range(POLES)]

        def step(t, state):
            x = m[pl.ds(pl.multiple_of(t * 16 + 8 * g, 8), 8), :]
            return tuple(d * s + x for d, s in zip(kept, state))

        state = forward_groups(docs, step, (jnp.zeros((8, LANES), F32),) * POLES)
        for n in range(POLES):
            ends[n * 16 + 8 * g : n * 16 + 8 * g + 8, :] = state[n]
    ids = jnp.broadcast_to(doc_row[...].astype(F32), (16, LANES)).astype(BF16)
    for p in range(GROUP):
        high, low = split(ends[every(p, POLES), :])
        send[p, 0:ROW_LO, :] = high
        send[p, ROW_LO:ROW_DOC, :] = low
        send[p, ROW_DOC:ROW_K, :] = ids
        head, part = p // 2, p % 2
        for row, ref in ((ROW_K, ak), (ROW_V, av), (ROW_Q, aq), (ROW_G, ag)):
            send[p, row : row + 64, :] = ref[64 * part : 64 * part + 64, lanes(head)]


def block_docs(got):
    return jnp.concatenate([got[b, ROW_DOC:ROW_K, :].astype(F32)[0:1] for b in range(GROUP)], axis=0)


def end_state(got, b):
    return got[b, 0:ROW_LO, :].astype(F32) + got[b, ROW_LO:ROW_DOC, :].astype(F32)


def spread(value):
    return jnp.broadcast_to(value, (POLES, LANES))


def flags_of(ids):
    first, last = ids[:, 0:1], ids[:, LANES - 1 : LANES]
    same = [spread((first[b : b + 1] == last[b : b + 1]).astype(F32)) for b in range(GROUP)]
    join = [
        spread((last[b : b + 1] == first[b + 1 : b + 2]).astype(F32)) for b in range(GROUP - 1)
    ]
    return same, join


def half_state_kernel(got, rate, out):
    ids = block_docs(got)
    same, join = flags_of(ids)
    through = jnp.exp(-float(TOK) * rate[...])
    carry = jnp.zeros((POLES, LANES), F32)
    for b in range(GROUP):
        carry = end_state(got, b) + same[b] * through * carry
        if b < GROUP - 1:
            carry = join[b] * carry
    out[0:16, :] = carry
    out[16:32, :] = ids


def carry_kernel(got, rate, other, out):
    ids = block_docs(got)
    same, join = flags_of(ids)
    through = jnp.exp(-float(TOK) * rate[...])
    late = jnp.where(lax.axis_index("ctx") >= GROUP, 1.0, 0.0)
    met = spread((other[31:32, LANES - 1 : LANES] == ids[0:1, 0:1]).astype(F32))
    carry = other[0:16, :] * met * late
    for b in range(GROUP):
        out[b] = carry
        if b < GROUP - 1:
            carry = join[b] * (end_state(got, b) + same[b] * through * carry)


def forward_kernel(docs, carry, m, dec, wgt, hq, hg, gain, f, sums):
    for g in range(2):
        kept = [dec[n * 16 + 8 * g : n * 16 + 8 * g + 8, :] for n in range(POLES)]
        weights = [wgt[n * 16 + 8 * g : n * 16 + 8 * g + 8, :] for n in range(POLES)]

        def step(t, state):
            at = pl.ds(pl.multiple_of(t * 16 + 8 * g, 8), 8)
            x = m[at, :]
            state = tuple(d * s + x for d, s in zip(kept, state))
            terms = [w * s for w, s in zip(weights, state)]
            while len(terms) > 1:
                terms = [a + b for a, b in zip(terms[::2], terms[1::2])]
            f[at, :] = terms[0]
            return state

        forward_groups(docs, step, tuple(carry[every(8 * g * 16 + n, 8), :] for n in range(POLES)))
    squares = jnp.zeros((TOK, LANES), F32)
    along = jnp.zeros((TOK, LANES), F32)
    for j in range(CHUNKS):
        out_y = hq[:, lanes(j)].astype(F32) * f[every(j, TOK), :]
        squares = squares + out_y * out_y
        along = along + hg[:, lanes(j)].astype(F32) * gain[:, lanes(j)] * out_y
    sums[0:1, :] = jnp.sum(squares.T, axis=0, keepdims=True)
    sums[1:2, :] = jnp.sum(along.T, axis=0, keepdims=True)
    sums[2:8, :] = jnp.zeros((6, LANES), F32)


def backward_kernel(docs, s0, s1, s2, s3, f, m, dec, hq, hg, gain, ghq, gf, send, starts, totals):
    total = s0[...] + s1[...] + s2[...] + s3[...]
    inv = lax.rsqrt(total[0:1, :] / D + EPSILON)
    slope = inv * inv * inv * total[1:2, :] / D
    inv = jnp.broadcast_to(inv, (TOK, LANES)).T
    slope = jnp.broadcast_to(slope, (TOK, LANES)).T
    for j in range(CHUNKS):
        q = hq[:, lanes(j)].astype(F32)
        back = hg[:, lanes(j)].astype(F32)
        row = f[every(j, TOK), :]
        out_y = q * row
        grad_y = inv * (back * gain[:, lanes(j)]) - out_y * slope
        ghq[:, lanes(j)] = (grad_y * row).astype(BF16)
        gf[every(j, TOK), :] = grad_y * q
        send[j, 32:40, :] = jnp.broadcast_to(
            jnp.sum(back * out_y * inv, axis=0, keepdims=True), (8, LANES)
        )
    for g in range(2):
        kept = [dec[n * 16 + 8 * g : n * 16 + 8 * g + 8, :] for n in range(POLES)]

        def step(t, carry):
            at = pl.ds(pl.multiple_of(t * 16 + 8 * g, 8), 8)
            x, feed = gf[at, :], m[at, :]
            state = tuple(d * s + x for d, s in zip(kept, carry[:POLES]))
            return state + tuple(k + feed * s for k, s in zip(carry[POLES:], state))

        zero = (jnp.zeros((8, LANES), F32),) * (2 * POLES)
        carry = backward_groups(docs, step, zero, POLES)
        for n in range(POLES):
            starts[n * 16 + 8 * g : n * 16 + 8 * g + 8, :] = carry[n]
            totals[n * 16 + 8 * g : n * 16 + 8 * g + 8, :] = carry[POLES + n]
    for p in range(GROUP):
        send[p, 0:16, :] = starts[every(p, POLES), :]
        send[p, 16:32, :] = totals[every(p, POLES), :]


def half_adjoint_kernel(got, back, rate, other, out):
    ids = block_docs(got)
    same, join = flags_of(ids)
    rates = rate[...]
    through = jnp.exp(-float(TOK) * rates)
    decay = jnp.exp(-rates)
    early = jnp.where(lax.axis_index("ctx") < GROUP, 1.0, 0.0)
    met = spread((other[16:17, 0:1] == ids[15:16, LANES - 1 : LANES]).astype(F32)) * early
    total = jnp.zeros((POLES, LANES), F32)
    reach = jnp.zeros((POLES, LANES), F32)
    gains = jnp.zeros((8, LANES), F32)
    carry = jnp.zeros((POLES, LANES), F32)
    unit = met
    for b in reversed(range(GROUP)):
        end = decay * end_state(got, b)
        total = total + back[b, 16:32, :] + end * carry
        reach = reach + end * unit
        gains = gains + back[b, 32:40, :]
        carry = back[b, 0:16, :] + same[b] * through * carry
        unit = same[b] * through * unit
        if b > 0:
            carry = join[b - 1] * carry
            unit = join[b - 1] * unit
    out[0:16, :] = carry
    out[16:32, :] = total
    out[32:48, :] = reach
    out[48:56, :] = gains


def last_pack_kernel(got, back, rate, other, mine, theirs, dq, own, own_got, prev_got, send):
    ids = block_docs(got)
    same, join = flags_of(ids)
    rates = rate[...]
    through = jnp.exp(-float(TOK) * rates)
    early = jnp.where(lax.axis_index("ctx") < GROUP, 1.0, 0.0)
    met = spread((other[16:17, 0:1] == ids[15:16, LANES - 1 : LANES]).astype(F32)) * early
    late_start = mine[0:16, :] * (1.0 - early) + theirs[0:16, :] * early
    early_reach = mine[32:48, :] * early + theirs[32:48, :] * (1.0 - early)
    residue = mine[16:32, :] + theirs[16:32, :] + late_start * early_reach
    residue = scaling_of(rates) * residue
    gains = mine[48:56, :] + theirs[48:56, :]
    res_high, res_low = split(residue)
    gain_high, gain_low = split(gains)
    pair = jnp.concatenate([gain_high.astype(F32), gain_low.astype(F32)], axis=0).astype(BF16)
    carry = theirs[0:16, :] * met
    for b in reversed(range(GROUP)):
        high, low = split(carry)
        send[b, 0:16, :] = high
        send[b, 16:32, :] = low
        send[b, OUT_RES : OUT_RES + 16, :] = res_high
        send[b, OUT_RES + 16 : OUT_GAIN, :] = res_low
        send[b, OUT_GAIN:OUT_Q, :] = pair
        send[b, OUT_Q:OUT_KV, :] = dq[b]
        kv = own[b].astype(F32) + own_got[b].astype(F32) + prev_got[b].astype(F32) * early
        send[b, OUT_KV:ROWS_OUT, :] = kv.astype(BF16)
        if b > 0:
            carry = join[b - 1] * (back[b, 0:16, :] + same[b] * through * carry)


def final_kernel(
    docs, got, gf, dec, wgt, hk, hv, ghk, ghv, gres, ggain, gaq, gak, gav, gm, entry
):
    for p in range(GROUP):
        entry[16 * p : 16 * p + 16, :] = got[p, 0:16, :].astype(F32) + got[p, 16:32, :].astype(F32)
        gres[:, lanes(p)] = got[p, OUT_RES : OUT_RES + 16, :].astype(F32) + got[
            p, OUT_RES + 16 : OUT_GAIN, :
        ].astype(F32)
        pair = got[p, OUT_GAIN:OUT_Q, :].astype(F32)
        ggain[:, lanes(p)] = pair[0:1] + pair[8:9]
        rows = slice(64 * (p % 2), 64 * (p % 2) + 64)
        gaq[rows, lanes(p // 2)] = got[p, OUT_Q:OUT_KV, :]
        gak[rows, lanes(p // 2)] = got[p, OUT_KV : OUT_KV + 64, :]
        gav[rows, lanes(p // 2)] = got[p, OUT_KV + 64 : ROWS_OUT, :]
    for g in range(2):
        kept = [dec[n * 16 + 8 * g : n * 16 + 8 * g + 8, :] for n in range(POLES)]
        weights = [wgt[n * 16 + 8 * g : n * 16 + 8 * g + 8, :] for n in range(POLES)]

        def step(t, state):
            at = pl.ds(pl.multiple_of(t * 16 + 8 * g, 8), 8)
            x = gf[at, :]
            state = tuple(d * s + x for d, s in zip(kept, state))
            terms = [w * s for w, s in zip(weights, state)]
            while len(terms) > 1:
                terms = [a + b for a, b in zip(terms[::2], terms[1::2])]
            gm[at, :] = terms[0]
            return state

        start = tuple(entry[every(8 * g * 16 + n, 8), :] for n in range(POLES))
        backward_groups(docs, step, start, POLES)
    for j in range(CHUNKS):
        row = gm[every(j, TOK), :]
        ghk[:, lanes(j)] = (row * hv[:, lanes(j)].astype(F32)).astype(BF16)
        ghv[:, lanes(j)] = (row * hk[:, lanes(j)].astype(F32)).astype(BF16)


def attention_kernel(
    got, kv_core, kv_half, kv_half_core, ids_mine, ids_other,
    dq, own, own_send, prev, prev_send,
    kbuf, vbuf, kturned, scores, products, dk, dv,
):
    me = lax.axis_index("ctx")
    core = lax.rem(me, 2)
    late = me >= GROUP

    def place(base, b, at_core, keys, values):
        at = pl.ds(pl.multiple_of(base + TOK * b + 64 * at_core, 64), 64)
        kbuf[at, :] = keys
        vbuf[at, :] = values

    for b in range(GROUP):
        place(HALF, b, core, got[b, ROW_K:ROW_V, :], got[b, ROW_V:ROW_Q, :])
        place(HALF, b, 1 - core, kv_core[b, 0:64, :], kv_core[b, 64:128, :])

    @pl.when(late)
    def _():
        for b in range(GROUP):
            place(0, b, core, kv_half[b, 0:64, :], kv_half[b, 64:128, :])
            place(0, b, 1 - core, kv_half_core[b, 0:64, :], kv_half_core[b, 64:128, :])

    first_tile = jnp.where(late, 0, N_TILES // 2)

    def prepare(t, _):
        at = pl.ds(pl.multiple_of(t * TILE, TILE), TILE)
        kturned[t] = kbuf[at, :].astype(F32).T.astype(BF16)
        dk[at, :] = jnp.zeros((TILE, HEAD_DIM), F32)
        dv[at, :] = jnp.zeros((TILE, HEAD_DIM), F32)
        return 0

    lax.fori_loop(first_tile, N_TILES, prepare, 0)

    own_ids, other_ids = ids_mine[16:32, :], ids_other[16:32, :]
    base = jnp.where(late, 0, HALF)
    starts = []
    for d in (1, 2, 3):
        before = jnp.sum((own_ids < d).astype(F32)).astype(jnp.int32)
        behind = jnp.sum((other_ids < d).astype(F32)).astype(jnp.int32)
        starts.append(before + jnp.where(late, behind, HALF))

    def start_of(pos):
        result = jnp.where(pos >= starts[0], starts[0], base)
        for start in starts[1:]:
            result = jnp.where(pos >= start, start, result)
        return result

    def query_tile(i, _):
        rows_q = jnp.concatenate([got[4 * i + u, ROW_Q:ROW_G, :] for u in range(4)], axis=0)
        rows_g = jnp.concatenate([got[4 * i + u, ROW_G:ROWS_IN, :] for u in range(4)], axis=0)
        turned_q = rows_q.astype(F32).T.astype(BF16)
        turned_g = rows_g.astype(F32).T.astype(BF16)
        lane = lax.broadcasted_iota(jnp.int32, (1, TILE), 1)
        qpos = HALF + 512 * i + 128 * (lane // 64) + 64 * core + lax.rem(lane, 64)
        qstart = start_of(qpos)
        low = start_of(HALF + 512 * i + 64 * core) // TILE
        high = HALF // TILE + 2 * i + 2

        def first_pass(t, peak):
            at = pl.ds(pl.multiple_of(t * TILE, TILE), TILE)
            kpos = t * TILE + lax.broadcasted_iota(jnp.int32, (TILE, TILE), 0)
            s = jnp.dot(kbuf[at, :], turned_q, preferred_element_type=F32) * (SCALE * LOG2E)
            s = jnp.where((kpos <= qpos) & (kpos >= qstart), s, FLOOR_SCORE)
            scores[t] = s
            products[t] = jnp.dot(vbuf[at, :], turned_g, preferred_element_type=F32)
            return jnp.maximum(peak, jnp.max(s.reshape(TILE // 8, 8, TILE), axis=0))

        peak = lax.fori_loop(low, high, first_pass, jnp.full((8, TILE), FLOOR_SCORE, F32))
        peak = jnp.max(peak, axis=0, keepdims=True)

        def second_pass(t, carry):
            total, weighted = carry
            p = jnp.exp2(scores[t] - peak)
            scores[t] = p
            total = total + jnp.sum(p.reshape(TILE // 8, 8, TILE), axis=0)
            q = p * products[t]
            return total, weighted + jnp.sum(q.reshape(TILE // 8, 8, TILE), axis=0)

        zero = jnp.zeros((8, TILE), F32)
        total, weighted = lax.fori_loop(low, high, second_pass, (zero, zero))
        inv = 1.0 / jnp.sum(total, axis=0, keepdims=True)
        centre = jnp.sum(weighted, axis=0, keepdims=True) * inv

        def third_pass(t, turned_dq):
            at = pl.ds(pl.multiple_of(t * TILE, TILE), TILE)
            p = scores[t] * inv
            ds = (p * (products[t] - centre)).astype(BF16)
            dk[at, :] += jnp.dot(ds, rows_q, preferred_element_type=F32)
            dv[at, :] += jnp.dot(p.astype(BF16), rows_g, preferred_element_type=F32)
            return turned_dq + jnp.dot(kturned[t], ds, preferred_element_type=F32)

        turned_dq = lax.fori_loop(low, high, third_pass, jnp.zeros((HEAD_DIM, TILE), F32))
        rows = (turned_dq * SCALE).T.astype(BF16)
        for u in range(4):
            dq[4 * i + u] = rows[64 * u : 64 * u + 64]
        return 0

    lax.fori_loop(0, Q_TILES, query_tile, 0)

    def leave(base, target, target_send):
        for b in range(GROUP):
            for at_core, ref in ((core, target), (1 - core, target_send)):
                at = pl.ds(pl.multiple_of(base + TOK * b + 64 * at_core, 64), 64)
                ref[b, 0:64, :] = (dk[at, :] * SCALE).astype(BF16)
                ref[b, 64:128, :] = dv[at, :].astype(BF16)

    leave(HALF, own, own_send)

    @pl.when(late)
    def _():
        leave(0, prev, prev_send)

    @pl.when(jnp.logical_not(late))
    def _():
        prev[...] = jnp.zeros(prev.shape, BF16)
        prev_send[...] = jnp.zeros(prev_send.shape, BF16)


def body(
    hyena_q, hyena_k, hyena_v, hyena_grad, pole_rate, residue, norm_gain, doc_ids,
    attn_q, attn_k, attn_v, attn_grad,
):
    count = 2 * GROUP
    halves = [list(range(GROUP)), list(range(GROUP, count))]
    swap_core = [(i, i ^ 1) for i in range(count)]
    swap_half = [(i, (i + GROUP) % count) for i in range(count)]
    up_half = [(i, i + GROUP) for i in range(GROUP)]
    down_half = [(i + GROUP, i) for i in range(GROUP)]

    def exchange(x):
        return lax.all_to_all(x, "ctx", 0, 0, tiled=True, axis_index_groups=halves)

    gain = norm_gain.reshape(1, CH)
    sweep = (TOK * CHUNKS, LANES)
    params = (POLES * CHUNKS, LANES)
    vmem = pltpu.VMEM
    send, m, dec, wgt = call(
        first_kernel,
        [((GROUP, ROWS_IN, LANES), BF16), (sweep, F32), (params, F32), (params, F32)],
        doc_ids, doc_ids.reshape(1, TOK), hyena_k, hyena_v, pole_rate, residue,
        attn_q, attn_k, attn_v, attn_grad,
        smem=(0,), scratch=[vmem(params, F32)], flops=40_000_000, nbytes=6_000_000,
    )
    got = exchange(send)
    slot = lax.rem(lax.axis_index("ctx"), GROUP)
    rate_part = lax.dynamic_slice_in_dim(pole_rate, slot * LANES, LANES, axis=1)
    head_spec = {0: pl.BlockSpec((GROUP, ROW_K, LANES), lambda i: (0, 0, 0))}

    kv = got[:, ROW_K:ROW_Q, :]
    kv_core = lax.ppermute(kv, "ctx", swap_core)
    kv_half = lax.ppermute(kv, "ctx", up_half)
    (mine,) = call(
        half_state_kernel, [((32, LANES), F32)], got, rate_part, specs=head_spec,
        flops=1_000_000, nbytes=300_000,
    )
    other = lax.ppermute(mine, "ctx", swap_half)
    (carry,) = call(
        carry_kernel, [((GROUP, POLES, LANES), F32)], got, rate_part, other, specs=head_spec,
        flops=1_000_000, nbytes=300_000,
    )
    carry = exchange(carry).reshape(params)
    f, sums = call(
        forward_kernel, [(sweep, F32), ((8, LANES), F32)],
        doc_ids, carry, m, dec, wgt, hyena_q, hyena_grad, gain,
        smem=(0,), flops=40_000_000, nbytes=6_000_000,
    )
    shared = [
        lax.ppermute(sums, "chan", [(i, (i + k) % 4) for i in range(4)]) for k in (1, 2, 3)
    ]
    kv_half_core = lax.ppermute(kv_half, "ctx", swap_core)
    part = (GROUP, TOK, HEAD_DIM)
    dq, own, own_send, prev, prev_send = call(
        attention_kernel,
        [((GROUP, 64, HEAD_DIM), BF16)] + [(part, BF16)] * 4,
        got, kv_core, kv_half, kv_half_core, mine, other,
        scratch=[
            vmem((2 * HALF, HEAD_DIM), BF16),
            vmem((2 * HALF, HEAD_DIM), BF16),
            vmem((N_TILES, HEAD_DIM, TILE), BF16),
            vmem((N_TILES, TILE, TILE), F32),
            vmem((N_TILES, TILE, TILE), F32),
            vmem((2 * HALF, HEAD_DIM), F32),
            vmem((2 * HALF, HEAD_DIM), F32),
        ],
        flops=2_000_000_000, nbytes=6_000_000, vmem=40 << 20,
    )
    own_got = lax.ppermute(own_send, "ctx", swap_core)
    prev_got = lax.ppermute(prev_send, "ctx", swap_core)
    prev_sum = (prev.astype(F32) + prev_got.astype(F32)).astype(BF16)
    prev_home = lax.ppermute(prev_sum, "ctx", down_half)

    ghq, gf, back_send = call(
        backward_kernel,
        [((TOK, CH), BF16), (sweep, F32), ((GROUP, 40, LANES), F32)],
        doc_ids, sums, *shared, f, m, dec, hyena_q, hyena_grad, gain,
        smem=(0,), scratch=[vmem(params, F32), vmem(params, F32)],
        flops=40_000_000, nbytes=6_000_000,
    )
    back = exchange(back_send)
    (half_mine,) = call(
        half_adjoint_kernel, [((56, LANES), F32)], got, back, rate_part, other, specs=head_spec,
        flops=1_000_000, nbytes=300_000,
    )
    half_other = lax.ppermute(half_mine, "ctx", swap_half)
    (last_send,) = call(
        last_pack_kernel, [((GROUP, ROWS_OUT, LANES), BF16)],
        got, back, rate_part, other, half_mine, half_other, dq, own, own_got, prev_home,
        specs=head_spec, flops=1_000_000, nbytes=3_000_000,
    )
    last = exchange(last_send)
    ghk, ghv, gres, ggain, gaq, gak, gav = call(
        final_kernel,
        [((TOK, CH), BF16), ((TOK, CH), BF16), ((POLES, CH), F32), ((1, CH), F32)]
        + [((TOK, 1024), BF16)] * 3,
        doc_ids, last, gf, dec, wgt, hyena_k, hyena_v,
        smem=(0,), scratch=[vmem(sweep, F32), vmem(params, F32)],
        flops=40_000_000, nbytes=6_000_000,
    )
    return (ghq, ghk, ghv, gres, ggain.reshape(CH), gaq, gak, gav)


def solution(mesh):
    wide, deep, one = P("ctx", "chan"), P(None, "chan"), P("chan")
    return jax.shard_map(
        body,
        mesh=mesh,
        in_specs=(wide,) * 4 + (deep, deep, one, P("ctx")) + (wide,) * 4,
        out_specs=(wide, wide, wide, deep, one, wide, wide, wide),
        check_vma=False,
    )
```

```python
import jax
import jax.numpy as jnp
from jax import lax
from jax.experimental import pallas as pl
from jax.experimental.pallas import tpu as pltpu
from jax.sharding import PartitionSpec as P

D = 8192
HEAD_DIM = 128
EPSILON = 1e-06
FLOOR_SCORE = -1e30

TOK = 128
CH = 2048
POLES = 16
LANES = 128
CHUNKS = CH // LANES
GROUP = 16
HALF = GROUP * TOK
SPAN = 8
SCALE = HEAD_DIM ** (-0.5)
LOG2E = 1.4426950408889634

ROW_LO, ROW_DOC, ROW_K, ROW_V, ROW_Q, ROW_G, ROWS_IN = 16, 32, 48, 112, 176, 240, 304
OUT_RES, OUT_GAIN, OUT_Q, OUT_KV, ROWS_OUT = 32, 64, 80, 144, 272
ROWS_BACK = 40

ROWS_TILE = 256
KEYS_TILE = 512
N_TILES = 2 * HALF // KEYS_TILE
Q_TILES = 4

F32 = jnp.float32
BF16 = jnp.bfloat16


def call(kernel, outs, *args, scratch=(), smem=(), flops=0, nbytes=0, vmem=24 << 20, specs=None, far=()):
    grid = (1,) if specs else ()
    specs = specs or {}
    ins = [
        pl.BlockSpec(memory_space=pltpu.SMEM) if i in smem
        else specs.get(i, pl.BlockSpec(memory_space=pltpu.VMEM))
        for i in range(len(args))
    ]
    shapes = [jax.ShapeDtypeStruct(shape, kind) for shape, kind in outs]
    return pl.pallas_call(
        kernel,
        out_shape=shapes,
        grid=grid,
        in_specs=ins,
        out_specs=[
            pl.BlockSpec(memory_space=pltpu.HBM if i in far else pltpu.VMEM) for i in range(len(outs))
        ],
        scratch_shapes=list(scratch),
        cost_estimate=pl.CostEstimate(flops=flops, bytes_accessed=nbytes, transcendentals=0),
        compiler_params=pltpu.CompilerParams(vmem_limit_bytes=vmem),
    )(*args)


def every(start, size):
    return pl.ds(start, size, stride=CHUNKS)


def lanes(j):
    return slice(LANES * j, LANES * (j + 1))


def split(value):
    high = value.astype(BF16)
    return high, (value - high.astype(F32)).astype(BF16)


def scaling_of(rate):
    y = 2.0 * rate
    series = 1.0 - y / 6.0
    for k in (5.0, 4.0, 3.0, 2.0):
        series = 1.0 - y / k * series
    return jnp.sqrt(y * series)


def forward_groups(docs, step, state):
    def group(i, state):
        first = i * SPAN

        def plain(state):
            for u in range(SPAN):
                state = step(first + u, state)
            return state

        def cut(state):
            for u in range(SPAN):
                t = first + u
                keep = jnp.where(docs[t] == docs[jnp.maximum(t - 1, 0)], 1.0, 0.0)
                state = step(t, tuple(s * keep for s in state))
            return state

        whole = docs[jnp.maximum(first - 1, 0)] == docs[first + SPAN - 1]
        return lax.cond(whole, plain, cut, state)

    return lax.fori_loop(0, TOK // SPAN, group, state)


def backward_groups(docs, step, state, count):
    def group(i, state):
        first = TOK - SPAN - i * SPAN

        def plain(state):
            for u in reversed(range(SPAN)):
                state = step(first + u, state)
            return state

        def cut(state):
            for u in reversed(range(SPAN)):
                t = first + u
                keep = jnp.where(docs[t] == docs[jnp.minimum(t + 1, TOK - 1)], 1.0, 0.0)
                state = tuple(s * keep for s in state[:count]) + tuple(state[count:])
                state = step(t, state)
            return state

        whole = docs[first] == docs[jnp.minimum(first + SPAN, TOK - 1)]
        return lax.cond(whole, plain, cut, state)

    return lax.fori_loop(0, TOK // SPAN, group, state)


def split(value):
    high = value.astype(BF16)
    return high, (value - high.astype(F32)).astype(BF16)


def joined(ref, index, row):
    return ref[index, row : row + 16, :].astype(F32) + ref[index, row + 16 : row + 32, :].astype(F32)


def first_kernel(
    docs, doc_row, rate_hbm, res_hbm, hk_hbm, hv_hbm, ak_hbm, av_hbm, aq_hbm, ag_hbm,
    send, m, dec, wgt, rate_part, ends, rate, res, hk, hv, ak, av, aq, ag, sems,
):
    pairs = (
        (rate_hbm, rate), (res_hbm, res), (hk_hbm, hk), (hv_hbm, hv),
        (ak_hbm, ak), (av_hbm, av), (aq_hbm, aq), (ag_hbm, ag),
    )
    copies = [
        pltpu.make_async_copy(source, target, sems.at[i])
        for i, (source, target) in enumerate(pairs)
    ]
    for copy in copies:
        copy.start()
    ids = jnp.broadcast_to(doc_row[...].astype(F32), (16, LANES)).astype(BF16)
    for p in range(GROUP):
        send[p, ROW_DOC:ROW_K, :] = ids
    copies[0].wait()
    copies[1].wait()
    rates = rate[...]
    rate_part[...] = rate[:, pl.ds(pl.multiple_of(position() * LANES, LANES), LANES)]
    decay = jnp.exp(-rates)
    weight = res[...] * scaling_of(rates)
    for j in range(CHUNKS):
        dec[every(j, POLES), :] = decay[:, lanes(j)]
        wgt[every(j, POLES), :] = weight[:, lanes(j)]
    copies[2].wait()
    copies[3].wait()
    for j in range(CHUNKS):
        m[every(j, TOK), :] = hk[:, lanes(j)].astype(F32) * hv[:, lanes(j)].astype(F32)
    for g in range(2):
        kept = [dec[n * 16 + 8 * g : n * 16 + 8 * g + 8, :] for n in range(POLES)]

        def step(t, state):
            x = m[pl.ds(pl.multiple_of(t * 16 + 8 * g, 8), 8), :]
            return tuple(d * s + x for d, s in zip(kept, state))

        state = forward_groups(docs, step, (jnp.zeros((8, LANES), F32),) * POLES)
        for n in range(POLES):
            ends[n * 16 + 8 * g : n * 16 + 8 * g + 8, :] = state[n]
    for p in range(GROUP):
        high, low = split(ends[every(p, POLES), :])
        send[p, 0:ROW_LO, :] = high
        send[p, ROW_LO:ROW_DOC, :] = low
    for copy, row, ref in zip(copies[4:], (ROW_K, ROW_V, ROW_Q, ROW_G), (ak, av, aq, ag)):
        copy.wait()
        for p in range(GROUP):
            part = slice(64 * (p % 2), 64 * (p % 2) + 64)
            send[p, row : row + 64, :] = ref[part, lanes(p // 2)]


def is_late():
    return lax.axis_index("ctx") >= GROUP


def block_at(b):
    return lax.rem(b + jnp.where(is_late(), 8, 0), GROUP)


def position():
    return block_at(lax.rem(lax.axis_index("ctx"), GROUP))


def block_docs(got):
    return jnp.concatenate([got[block_at(b), ROW_DOC:ROW_K, :].astype(F32)[0:1] for b in range(GROUP)], axis=0)


def end_state(got, b):
    return joined(got, block_at(b), 0)


def spread(value):
    return jnp.broadcast_to(value, (POLES, LANES))


def flags_of(ids):
    first, last = ids[:, 0:1], ids[:, LANES - 1 : LANES]
    same = [spread((first[b : b + 1] == last[b : b + 1]).astype(F32)) for b in range(GROUP)]
    join = [
        spread((last[b : b + 1] == first[b + 1 : b + 2]).astype(F32)) for b in range(GROUP - 1)
    ]
    return same, join


def half_state_kernel(got, rate, out):
    ids = block_docs(got)
    same, join = flags_of(ids)
    through = jnp.exp(-float(TOK) * rate[...])
    carry = jnp.zeros((POLES, LANES), F32)
    for b in range(GROUP):
        carry = end_state(got, b) + same[b] * through * carry
        if b < GROUP - 1:
            carry = join[b] * carry
    out[0:16, :] = carry
    out[16:32, :] = ids


def carry_kernel(got, rate, other, out):
    ids = block_docs(got)
    same, join = flags_of(ids)
    through = jnp.exp(-float(TOK) * rate[...])
    late = jnp.where(is_late(), 1.0, 0.0)
    met = spread((other[31:32, LANES - 1 : LANES] == ids[0:1, 0:1]).astype(F32))
    carry = other[0:16, :] * met * late
    for b in range(GROUP):
        out[block_at(b)] = carry
        if b < GROUP - 1:
            carry = join[b] * (end_state(got, b) + same[b] * through * carry)


def forward_kernel(docs, carry, m, dec, wgt, hq, hg, gain, f, sums):
    for g in range(2):
        kept = [dec[n * 16 + 8 * g : n * 16 + 8 * g + 8, :] for n in range(POLES)]
        weights = [wgt[n * 16 + 8 * g : n * 16 + 8 * g + 8, :] for n in range(POLES)]

        def step(t, state):
            at = pl.ds(pl.multiple_of(t * 16 + 8 * g, 8), 8)
            x = m[at, :]
            state = tuple(d * s + x for d, s in zip(kept, state))
            terms = [w * s for w, s in zip(weights, state)]
            while len(terms) > 1:
                terms = [a + b for a, b in zip(terms[::2], terms[1::2])]
            f[at, :] = terms[0]
            return state

        forward_groups(docs, step, tuple(carry[every(8 * g * 16 + n, 8), :] for n in range(POLES)))
    squares = jnp.zeros((TOK, LANES), F32)
    along = jnp.zeros((TOK, LANES), F32)
    for j in range(CHUNKS):
        out_y = hq[:, lanes(j)].astype(F32) * f[every(j, TOK), :]
        squares = squares + out_y * out_y
        along = along + hg[:, lanes(j)].astype(F32) * gain[:, lanes(j)] * out_y
    sums[0:1, :] = jnp.sum(squares.T, axis=0, keepdims=True)
    sums[1:2, :] = jnp.sum(along.T, axis=0, keepdims=True)
    sums[2:8, :] = jnp.zeros((6, LANES), F32)


def backward_kernel(docs, s0, s1, s2, s3, f, m, dec, hq, hg, gain, ghq, gf, send, starts, totals):
    total = s0[...] + s1[...] + s2[...] + s3[...]
    inv = lax.rsqrt(total[0:1, :] / D + EPSILON)
    slope = inv * inv * inv * total[1:2, :] / D
    inv = jnp.broadcast_to(inv, (TOK, LANES)).T
    slope = jnp.broadcast_to(slope, (TOK, LANES)).T
    for j in range(CHUNKS):
        q = hq[:, lanes(j)].astype(F32)
        back = hg[:, lanes(j)].astype(F32)
        row = f[every(j, TOK), :]
        out_y = q * row
        grad_y = inv * (back * gain[:, lanes(j)]) - out_y * slope
        ghq[:, lanes(j)] = (grad_y * row).astype(BF16)
        gf[every(j, TOK), :] = grad_y * q
        send[j, 32:40, :] = jnp.broadcast_to(
            jnp.sum(back * out_y * inv, axis=0, keepdims=True), (8, LANES)
        )
    for g in range(2):
        kept = [dec[n * 16 + 8 * g : n * 16 + 8 * g + 8, :] for n in range(POLES)]

        def step(t, carry):
            at = pl.ds(pl.multiple_of(t * 16 + 8 * g, 8), 8)
            x, feed = gf[at, :], m[at, :]
            state = tuple(d * s + x for d, s in zip(kept, carry[:POLES]))
            return state + tuple(k + feed * s for k, s in zip(carry[POLES:], state))

        zero = (jnp.zeros((8, LANES), F32),) * (2 * POLES)
        carry = backward_groups(docs, step, zero, POLES)
        for n in range(POLES):
            starts[n * 16 + 8 * g : n * 16 + 8 * g + 8, :] = carry[n]
            totals[n * 16 + 8 * g : n * 16 + 8 * g + 8, :] = carry[POLES + n]
    for p in range(GROUP):
        send[p, 0:16, :] = starts[every(p, POLES), :]
        send[p, 16:32, :] = totals[every(p, POLES), :]


def half_adjoint_kernel(got, back, rate, other, out):
    ids = block_docs(got)
    same, join = flags_of(ids)
    rates = rate[...]
    through = jnp.exp(-float(TOK) * rates)
    decay = jnp.exp(-rates)
    early = jnp.where(is_late(), 0.0, 1.0)
    met = spread((other[16:17, 0:1] == ids[15:16, LANES - 1 : LANES]).astype(F32)) * early
    total = jnp.zeros((POLES, LANES), F32)
    reach = jnp.zeros((POLES, LANES), F32)
    gains = jnp.zeros((8, LANES), F32)
    carry = jnp.zeros((POLES, LANES), F32)
    unit = met
    for b in reversed(range(GROUP)):
        end = decay * end_state(got, b)
        total = total + back[block_at(b), 16:32, :] + end * carry
        reach = reach + end * unit
        gains = gains + back[block_at(b), 32:40, :]
        carry = back[block_at(b), 0:16, :] + same[b] * through * carry
        unit = same[b] * through * unit
        if b > 0:
            carry = join[b - 1] * carry
            unit = join[b - 1] * unit
    out[0:16, :] = carry
    out[16:32, :] = total
    out[32:48, :] = reach
    out[48:56, :] = gains


def last_pack_kernel(got, back, rate, other, mine, theirs, dq, own, own_got, prev_got, send):
    ids = block_docs(got)
    same, join = flags_of(ids)
    rates = rate[...]
    through = jnp.exp(-float(TOK) * rates)
    early = jnp.where(is_late(), 0.0, 1.0)
    met = spread((other[16:17, 0:1] == ids[15:16, LANES - 1 : LANES]).astype(F32)) * early
    late_start = mine[0:16, :] * (1.0 - early) + theirs[0:16, :] * early
    early_reach = mine[32:48, :] * early + theirs[32:48, :] * (1.0 - early)
    residue = mine[16:32, :] + theirs[16:32, :] + late_start * early_reach
    res_high, res_low = split(scaling_of(rates) * residue)
    gain_high, gain_low = split(mine[48:56, :] + theirs[48:56, :])
    pair = jnp.concatenate([gain_high.astype(F32), gain_low.astype(F32)], axis=0).astype(BF16)
    carry = theirs[0:16, :] * met
    for b in reversed(range(GROUP)):
        at = block_at(b)
        high, low = split(carry)
        send[at, 0:16, :] = high
        send[at, 16:OUT_RES, :] = low
        send[at, OUT_RES : OUT_RES + 16, :] = res_high
        send[at, OUT_RES + 16 : OUT_GAIN, :] = res_low
        send[at, OUT_GAIN:OUT_Q, :] = pair
        send[at, OUT_Q:OUT_KV, :] = dq[at]
        kv = own[at].astype(F32) + own_got[at].astype(F32) + prev_got[at].astype(F32) * early
        send[at, OUT_KV:ROWS_OUT, :] = kv.astype(BF16)
        if b > 0:
            carry = join[b - 1] * (back[at, 0:16, :] + same[b] * through * carry)


def final_kernel(
    docs, got, gf, dec, wgt, hk, hv, ghk, ghv, gres, ggain, gaq, gak, gav, gm, entry
):
    for p in range(GROUP):
        entry[16 * p : 16 * p + 16, :] = joined(got, p, 0)
        gres[:, lanes(p)] = joined(got, p, OUT_RES)
        pair = got[p, OUT_GAIN:OUT_Q, :].astype(F32)
        ggain[:, lanes(p)] = pair[0:1] + pair[8:9]
        rows = slice(64 * (p % 2), 64 * (p % 2) + 64)
        gaq[rows, lanes(p // 2)] = got[p, OUT_Q:OUT_KV, :]
        gak[rows, lanes(p // 2)] = got[p, OUT_KV : OUT_KV + 64, :]
        gav[rows, lanes(p // 2)] = got[p, OUT_KV + 64 : ROWS_OUT, :]
    for g in range(2):
        kept = [dec[n * 16 + 8 * g : n * 16 + 8 * g + 8, :] for n in range(POLES)]
        weights = [wgt[n * 16 + 8 * g : n * 16 + 8 * g + 8, :] for n in range(POLES)]

        def step(t, state):
            at = pl.ds(pl.multiple_of(t * 16 + 8 * g, 8), 8)
            x = gf[at, :]
            state = tuple(d * s + x for d, s in zip(kept, state))
            terms = [w * s for w, s in zip(weights, state)]
            while len(terms) > 1:
                terms = [a + b for a, b in zip(terms[::2], terms[1::2])]
            gm[at, :] = terms[0]
            return state

        start = tuple(entry[every(8 * g * 16 + n, 8), :] for n in range(POLES))
        backward_groups(docs, step, start, POLES)
    for j in range(CHUNKS):
        row = gm[every(j, TOK), :]
        ghk[:, lanes(j)] = (row * hv[:, lanes(j)].astype(F32)).astype(BF16)
        ghv[:, lanes(j)] = (row * hk[:, lanes(j)].astype(F32)).astype(BF16)


def attention_kernel(
    got, kv_core, kv_half, kv_half_core, ids_mine, ids_other, after,
    dq, own, own_send, prev, prev_send,
    kbuf, vbuf, kturned, scores, products, peaks, dk, dv,
):
    core = lax.rem(lax.axis_index("ctx"), 2)
    late = is_late()

    def place(base, b, at_core, keys, values):
        at = pl.ds(pl.multiple_of(base + TOK * b + 64 * at_core, 64), 64)
        kbuf[at, :] = keys
        vbuf[at, :] = values

    for b in range(GROUP):
        s = block_at(b)
        place(HALF, b, core, got[s, ROW_K:ROW_V, :], got[s, ROW_V:ROW_Q, :])
        place(HALF, b, 1 - core, kv_core[s, 0:64, :], kv_core[s, 64:128, :])

    @pl.when(late)
    def _():
        for b in range(GROUP):
            place(0, b, core, kv_half[b, 0:64, :], kv_half[b, 64:128, :])
            place(0, b, 1 - core, kv_half_core[b, 0:64, :], kv_half_core[b, 64:128, :])

    first_tile = jnp.where(late, 0, N_TILES // 2)

    def prepare(t, _):
        at = pl.ds(pl.multiple_of(t * KEYS_TILE, KEYS_TILE), KEYS_TILE)
        kturned[t] = kbuf[at, :].astype(F32).T.astype(BF16)
        dk[at, :] = jnp.zeros((KEYS_TILE, HEAD_DIM), F32)
        dv[at, :] = jnp.zeros((KEYS_TILE, HEAD_DIM), F32)
        return 0

    lax.fori_loop(first_tile, N_TILES, prepare, 0)

    own_ids, other_ids = ids_mine[16:32, :], ids_other[16:32, :]
    base = jnp.where(late, 0, HALF)
    starts = []
    for d in (1, 2, 3):
        before = jnp.sum((own_ids < d).astype(F32)).astype(jnp.int32)
        behind = jnp.sum((other_ids < d).astype(F32)).astype(jnp.int32)
        starts.append(before + jnp.where(late, behind, HALF))

    def start_of(pos):
        result = jnp.where(pos >= starts[0], starts[0], base)
        for start in starts[1:]:
            result = jnp.where(pos >= start, start, result)
        return result

    def query_tile(i, _):
        rows_q = jnp.concatenate([got[block_at(4 * i + u), ROW_Q:ROW_G, :] for u in range(4)], axis=0)
        rows_g = jnp.concatenate([got[block_at(4 * i + u), ROW_G:ROWS_IN, :] for u in range(4)], axis=0)
        turned_q = rows_q.astype(F32).T.astype(BF16)
        turned_g = rows_g.astype(F32).T.astype(BF16)
        lane = lax.broadcasted_iota(jnp.int32, (1, ROWS_TILE), 1)
        qpos = HALF + 512 * i + 128 * (lane // 64) + 64 * core + lax.rem(lane, 64)
        qstart = start_of(qpos)
        low = start_of(HALF + 512 * i + 64 * core) // KEYS_TILE
        high = HALF // KEYS_TILE + i + 1
        row = lax.broadcasted_iota(jnp.int32, (KEYS_TILE, ROWS_TILE), 0)

        def fold(value, by):
            return by(value.reshape(KEYS_TILE // 8, 8, ROWS_TILE), axis=0)

        def first_pass(t, carry):
            peak, total, weighted = carry
            at = pl.ds(pl.multiple_of(t * KEYS_TILE, KEYS_TILE), KEYS_TILE)
            s = jnp.dot(kbuf[at, :], turned_q, preferred_element_type=F32)
            gp = jnp.dot(vbuf[at, :], turned_g, preferred_element_type=F32)
            first = t * KEYS_TILE
            s = jnp.where((row <= qpos - first) & (row >= qstart - first), s, FLOOR_SCORE)
            top = jnp.maximum(peak, jnp.max(fold(s, jnp.max), axis=0, keepdims=True))
            p = jnp.exp2((s - top) * (SCALE * LOG2E))
            scores[t] = p
            products[t] = gp
            peaks[t] = jnp.broadcast_to(top, (8, ROWS_TILE))
            shrink = jnp.exp2((peak - top) * (SCALE * LOG2E))
            return top, total * shrink + fold(p, jnp.sum), weighted * shrink + fold(p * gp, jnp.sum)

        zero = jnp.zeros((8, ROWS_TILE), F32)
        floor = jnp.full((1, ROWS_TILE), FLOOR_SCORE, F32)
        peak, total, weighted = lax.fori_loop(low, high, first_pass, (floor, zero, zero))
        inv = 1.0 / jnp.sum(total, axis=0, keepdims=True)
        centre = jnp.sum(weighted, axis=0, keepdims=True) * inv

        def second_pass(t, turned_dq):
            at = pl.ds(pl.multiple_of(t * KEYS_TILE, KEYS_TILE), KEYS_TILE)
            p = scores[t] * (jnp.exp2((peaks[t][0:1] - peak) * (SCALE * LOG2E)) * inv)
            ds = (p * (products[t] - centre)).astype(BF16)
            dk[at, :] += jnp.dot(ds, rows_q, preferred_element_type=F32)
            dv[at, :] += jnp.dot(p.astype(BF16), rows_g, preferred_element_type=F32)
            return turned_dq + jnp.dot(kturned[t], ds, preferred_element_type=F32)

        zero = jnp.zeros((HEAD_DIM, ROWS_TILE), F32)
        turned_dq = lax.fori_loop(low, high, second_pass, zero)
        rows = (turned_dq * SCALE).T.astype(BF16)
        for u in range(4):
            dq[block_at(4 * i + u)] = rows[64 * u : 64 * u + 64]
        return 0

    lax.fori_loop(0, Q_TILES, query_tile, 0)

    def leave(base, target, target_send, order):
        for b in range(GROUP):
            s = order(b)
            for at_core, ref in ((core, target), (1 - core, target_send)):
                at = pl.ds(pl.multiple_of(base + TOK * b + 64 * at_core, 64), 64)
                ref[s, 0:64, :] = (dk[at, :] * SCALE).astype(BF16)
                ref[s, 64:128, :] = dv[at, :].astype(BF16)

    leave(HALF, own, own_send, block_at)

    @pl.when(late)
    def _():
        leave(0, prev, prev_send, lambda b: b)

    @pl.when(jnp.logical_not(late))
    def _():
        prev[...] = jnp.zeros(prev.shape, BF16)
        prev_send[...] = jnp.zeros(prev_send.shape, BF16)


def body(
    hyena_q, hyena_k, hyena_v, hyena_grad, pole_rate, residue, norm_gain, doc_ids,
    attn_q, attn_k, attn_v, attn_grad,
):
    count = 2 * GROUP
    early = list(range(GROUP))
    late = [GROUP + (p ^ 8) for p in early]
    swap_core = [(i, i ^ 1) for i in range(count)]
    up_half = list(zip(early, late))
    down_half = list(zip(late, early))
    swap_half = up_half + down_half

    def exchange(x):
        return lax.all_to_all(x, "ctx", 0, 0, tiled=True, axis_index_groups=[early, late])

    gain = norm_gain.reshape(1, CH)
    sweep = (TOK * CHUNKS, LANES)
    params = (POLES * CHUNKS, LANES)
    vmem = pltpu.VMEM
    hbm = pl.BlockSpec(memory_space=pltpu.HBM)
    send, m, dec, wgt, rate_part = call(
        first_kernel,
        [((GROUP, ROWS_IN, LANES), BF16), (sweep, F32), (params, F32), (params, F32)]
        + [((POLES, LANES), F32)],
        doc_ids, doc_ids.reshape(1, TOK), pole_rate, residue, hyena_k, hyena_v,
        attn_k, attn_v, attn_q, attn_grad,
        smem=(0,), specs={i: hbm for i in range(2, 10)},
        scratch=[vmem(params, F32)] + [vmem((POLES, CH), F32)] * 2 + [vmem((TOK, CH), BF16)] * 2
        + [vmem((TOK, 1024), BF16)] * 4 + [pltpu.SemaphoreType.DMA((8,))],
        flops=40_000_000, nbytes=6_000_000, vmem=60 << 20,
    )
    got = exchange(send)
    head_spec = {0: pl.BlockSpec((GROUP, ROW_K, LANES), lambda i: (0, 0, 0))}
    (mine,) = call(
        half_state_kernel, [((32, LANES), F32)], got, rate_part, specs=head_spec,
        flops=1_000_000, nbytes=300_000,
    )
    kv = got[:, ROW_K:ROW_Q, :]
    kv_core = lax.ppermute(kv, "ctx", swap_core)
    other = lax.ppermute(mine, "ctx", swap_half)
    other, kv = lax.optimization_barrier((other, kv))
    kv_half = lax.ppermute(kv, "ctx", up_half)
    (carry,) = call(
        carry_kernel, [((GROUP, POLES, LANES), F32)], got, rate_part, other, specs=head_spec,
        flops=1_000_000, nbytes=300_000,
    )
    carry = exchange(carry).reshape(params)
    carry, kv_half = lax.optimization_barrier((carry, kv_half))
    kv_half_core = lax.ppermute(kv_half, "ctx", swap_core)
    f, sums = call(
        forward_kernel, [(sweep, F32), ((8, LANES), F32)],
        doc_ids, carry, m, dec, wgt, hyena_q, hyena_grad, gain,
        smem=(0,), flops=40_000_000, nbytes=6_000_000,
    )
    shared = [
        lax.ppermute(sums, "chan", [(i, (i + k) % 4) for i in range(4)]) for k in (1, 2, 3)
    ]
    part = (GROUP, TOK, HEAD_DIM)
    dq, own, own_send, prev, prev_send = call(
        attention_kernel,
        [((GROUP, 64, HEAD_DIM), BF16)] + [(part, BF16)] * 4,
        got, kv_core, kv_half, kv_half_core, mine, other, sums,
        scratch=[
            vmem((2 * HALF, HEAD_DIM), BF16),
            vmem((2 * HALF, HEAD_DIM), BF16),
            vmem((N_TILES, HEAD_DIM, KEYS_TILE), BF16),
            vmem((N_TILES, KEYS_TILE, ROWS_TILE), F32),
            vmem((N_TILES, KEYS_TILE, ROWS_TILE), F32),
            vmem((N_TILES, 8, ROWS_TILE), F32),
            vmem((2 * HALF, HEAD_DIM), F32),
            vmem((2 * HALF, HEAD_DIM), F32),
        ],
        flops=10_000_000_000, nbytes=6_000_000, vmem=40 << 20,
    )
    f, dq = lax.optimization_barrier((f, dq))
    ghq, gf, back_send = call(
        backward_kernel,
        [((TOK, CH), BF16), (sweep, F32), ((GROUP, ROWS_BACK, LANES), F32)],
        doc_ids, sums, *shared, f, m, dec, hyena_q, hyena_grad, gain,
        smem=(0,), scratch=[vmem(params, F32), vmem(params, F32)],
        flops=40_000_000, nbytes=6_000_000,
    )
    back_send, own_send, prev_send = lax.optimization_barrier((back_send, own_send, prev_send))
    prev_got = lax.ppermute(prev_send, "ctx", swap_core)
    own_got = lax.ppermute(own_send, "ctx", swap_core)
    prev_sum = (prev.astype(F32) + prev_got.astype(F32)).astype(BF16)
    prev_home = lax.ppermute(prev_sum, "ctx", down_half)
    back = exchange(back_send)
    (half_mine,) = call(
        half_adjoint_kernel, [((56, LANES), F32)], got, back, rate_part, other, specs=head_spec,
        flops=1_000_000, nbytes=300_000,
    )
    half_other = lax.ppermute(half_mine, "ctx", swap_half)
    (last_send,) = call(
        last_pack_kernel, [((GROUP, ROWS_OUT, LANES), BF16)],
        got, back, rate_part, other, half_mine, half_other, dq, own, own_got, prev_home,
        specs=head_spec, flops=1_000_000, nbytes=3_000_000,
    )
    last = exchange(last_send)
    ghk, ghv, gres, ggain, gaq, gak, gav = call(
        final_kernel,
        [((TOK, CH), BF16), ((TOK, CH), BF16), ((POLES, CH), F32), ((1, CH), F32)]
        + [((TOK, 1024), BF16)] * 3,
        doc_ids, last, gf, dec, wgt, hyena_k, hyena_v,
        smem=(0,), scratch=[vmem(sweep, F32), vmem(params, F32)],
        flops=40_000_000, nbytes=6_000_000,
    )
    return (ghq, ghk, ghv, gres, ggain.reshape(CH), gaq, gak, gav)


def solution(mesh):
    wide, deep, one = P("ctx", "chan"), P(None, "chan"), P("chan")
    return jax.shard_map(
        body,
        mesh=mesh,
        in_specs=(wide,) * 4 + (deep, deep, one, P("ctx")) + (wide,) * 4,
        out_specs=(wide, wide, wide, deep, one, wide, wide, wide),
        check_vma=False,
    )
```

```python
import functools

import jax
import jax.numpy as jnp
from jax import lax
from jax.experimental import pallas as pl
from jax.experimental.pallas import tpu as pltpu
from jax.sharding import PartitionSpec as P

D = 8192
HEAD_DIM = 128
EPSILON = 1e-06
FLOOR_SCORE = -1e30

TOK = 128
CH = 2048
POLES = 16
LANES = 128
CHUNKS = CH // LANES
GROUP = 16
HALF = GROUP * TOK
SPAN = 8
SCALE = HEAD_DIM ** (-0.5)
LOG2E = 1.4426950408889634

HALF_ROWS = POLES * 8
half_shape = (HALF_ROWS, LANES)
ROW_DOC, ROW_K, ROW_V, ROW_Q, ROW_G, ROWS_IN = 128, 144, 208, 272, 336, 400
OUT_RES, OUT_GAIN, OUT_Q, OUT_KV, ROWS_OUT = 16, 48, 64, 128, 256
BACK_SUM, BACK_GAIN, ROWS_BACK = 16, 48, 64

ROWS_TILE = 256
KEYS_TILE = 512
N_TILES = 2 * HALF // KEYS_TILE
HALF_TILES = N_TILES // 2
Q_TILES = 4

F32 = jnp.float32
BF16 = jnp.bfloat16


def call(kernel, outs, *args, scratch=(), smem=(), flops=0, nbytes=0, vmem=24 << 20, specs=None, far=()):
    grid = (1,) if specs else ()
    specs = specs or {}
    ins = [
        pl.BlockSpec(memory_space=pltpu.SMEM) if i in smem
        else specs.get(i, pl.BlockSpec(memory_space=pltpu.VMEM))
        for i in range(len(args))
    ]
    shapes = [jax.ShapeDtypeStruct(shape, kind) for shape, kind in outs]
    return pl.pallas_call(
        kernel,
        out_shape=shapes,
        grid=grid,
        in_specs=ins,
        out_specs=[
            pl.BlockSpec(memory_space=pltpu.HBM if i in far else pltpu.VMEM) for i in range(len(outs))
        ],
        scratch_shapes=list(scratch),
        cost_estimate=pl.CostEstimate(flops=flops, bytes_accessed=nbytes, transcendentals=0),
        compiler_params=pltpu.CompilerParams(vmem_limit_bytes=vmem),
    )(*args)


def every(start, size):
    return pl.ds(start, size, stride=CHUNKS)


def lanes(j):
    return slice(LANES * j, LANES * (j + 1))


def split(value):
    high = value.astype(BF16)
    return high, (value - high.astype(F32)).astype(BF16)


def scaling_of(rate):
    y = 2.0 * rate
    series = 1.0 - y / 6.0
    for k in (5.0, 4.0, 3.0, 2.0):
        series = 1.0 - y / k * series
    return jnp.sqrt(y * series)


def forward_groups(docs, step, state):
    def group(i, state):
        first = i * SPAN

        def plain(state):
            for u in range(SPAN):
                state = step(first + u, state)
            return state

        def cut(state):
            for u in range(SPAN):
                t = first + u
                keep = jnp.where(docs[t] == docs[jnp.maximum(t - 1, 0)], 1.0, 0.0)
                state = step(t, tuple(s * keep for s in state))
            return state

        whole = docs[jnp.maximum(first - 1, 0)] == docs[first + SPAN - 1]
        return lax.cond(whole, plain, cut, state)

    return lax.fori_loop(0, TOK // SPAN, group, state)


def backward_groups(docs, step, state, count):
    def group(i, state):
        first = TOK - SPAN - i * SPAN

        def plain(state):
            for u in reversed(range(SPAN)):
                state = step(first + u, state)
            return state

        def cut(state):
            for u in reversed(range(SPAN)):
                t = first + u
                keep = jnp.where(docs[t] == docs[jnp.minimum(t + 1, TOK - 1)], 1.0, 0.0)
                state = tuple(s * keep for s in state[:count]) + tuple(state[count:])
                state = step(t, state)
            return state

        whole = docs[first] == docs[jnp.minimum(first + SPAN, TOK - 1)]
        return lax.cond(whole, plain, cut, state)

    return lax.fori_loop(0, TOK // SPAN, group, state)


def split(value):
    high = value.astype(BF16)
    return high, (value - high.astype(F32)).astype(BF16)


def pair_rows(row):
    high, low = split(jnp.broadcast_to(row, (8, LANES)))
    return jnp.concatenate([high.astype(F32), low.astype(F32)], axis=0).astype(BF16)


def joined(ref, index, row):
    return ref[index, row : row + 16, :].astype(F32) + ref[index, row + 16 : row + 32, :].astype(F32)


def first_kernel(
    docs, doc_row, rate_hbm, res_hbm, hk_hbm, hv_hbm, ak_hbm, av_hbm, aq_hbm, ag_hbm,
    send, m, dec, wgt, through, rate_part, thr_all, rate, res, hk, hv, ak, av, aq, ag, sems,
):
    pairs = (
        (rate_hbm, rate), (res_hbm, res), (hk_hbm, hk), (hv_hbm, hv),
        (ak_hbm, ak), (av_hbm, av), (aq_hbm, aq), (ag_hbm, ag),
    )
    copies = [
        pltpu.make_async_copy(source, target, sems.at[i])
        for i, (source, target) in enumerate(pairs)
    ]
    for copy in copies:
        copy.start()
    ids = jnp.broadcast_to(doc_row[...].astype(F32), (16, LANES)).astype(BF16)
    for p in range(GROUP):
        send[p, ROW_DOC:ROW_K, :] = ids
    core = core_of()
    copies[0].wait()
    copies[1].wait()
    rates = rate[...]
    start = pl.multiple_of(chunk_of(position()) * LANES, LANES)
    rate_part[...] = rate[:, pl.ds(start, LANES)]
    decay = jnp.exp(-rates)
    weight = res[...] * scaling_of(rates)
    block = jnp.exp(-float(TOK) * rates)
    for j in range(CHUNKS):
        dec[every(j, POLES), :] = decay[:, lanes(j)]
        wgt[every(j, POLES), :] = weight[:, lanes(j)]
        thr_all[every(j, POLES), :] = block[:, lanes(j)]
    for n in range(POLES):
        at = pl.ds(pl.multiple_of(16 * n + 8 * core, 8), 8)
        through[8 * n : 8 * n + 8, :] = thr_all[at, :]
    copies[2].wait()
    copies[3].wait()
    for j in range(CHUNKS):
        m[every(j, TOK), :] = hk[:, lanes(j)].astype(F32) * hv[:, lanes(j)].astype(F32)
    for g in range(2):
        kept = [dec[n * 16 + 8 * g : n * 16 + 8 * g + 8, :] for n in range(POLES)]

        def step(t, state):
            x = m[pl.ds(pl.multiple_of(t * 16 + 8 * g, 8), 8), :]
            return tuple(d * s + x for d, s in zip(kept, state))

        state = forward_groups(docs, step, (jnp.zeros((8, LANES), F32),) * POLES)
        pairs = [jnp.concatenate(state[n : n + 2], axis=0).astype(BF16) for n in range(0, POLES, 2)]
        for p in range(g, GROUP, 2):
            for i, pair in enumerate(pairs):
                send[p, 16 * i : 16 * i + 16, :] = pair
    for copy, row, ref in zip(copies[4:], (ROW_K, ROW_V, ROW_Q, ROW_G), (ak, av, aq, ag)):
        copy.wait()
        for p in range(GROUP):
            part = slice(64 * (p % 2), 64 * (p % 2) + 64)
            send[p, row : row + 64, :] = ref[part, lanes(p // 2)]


def is_late():
    return lax.axis_index("ctx") >= GROUP


def block_at(b):
    return lax.rem(b + jnp.where(is_late(), 8, 0), GROUP)


def position():
    return block_at(lax.rem(lax.axis_index("ctx"), GROUP))


def core_of():
    return lax.rem(lax.axis_index("ctx"), 2)


def chunk_of(p):
    return 8 * (p % 2) + p // 2


def place_of(j):
    return 2 * (j % 8) + j // 8


def block_docs(got):
    rows = [got[block_at(b), ROW_DOC:ROW_K, :].astype(F32)[0:1] for b in range(GROUP)]
    return jnp.concatenate(rows, axis=0)


def spread(value, rows=POLES):
    return jnp.broadcast_to(value, (rows, LANES))


def flags_of(ids, rows=POLES):
    first, last = ids[:, 0:1], ids[:, LANES - 1 : LANES]
    same = [spread((first[b : b + 1] == last[b : b + 1]).astype(F32), rows) for b in range(GROUP)]
    join = [
        spread((last[b : b + 1] == first[b + 1 : b + 2]).astype(F32), rows) for b in range(GROUP - 1)
    ]
    return same, join


def half_state_kernel(got, through, out, local, ends, inside):
    ids = block_docs(got)
    same, join = flags_of(ids, HALF_ROWS)
    thr = through[...]
    state = jnp.zeros(half_shape, F32)
    reach = jnp.ones(half_shape, F32)
    turn = lax.rem(lax.axis_index("ctx"), GROUP)
    column = position() // 2
    for b in range(GROUP):
        inside[b, 0] = state
        inside[b, 1] = reach
        end = got[block_at(b), 0:HALF_ROWS, :].astype(F32)
        inside[b, 2] = end
        hold = same[b] * thr
        state = end + hold * state
        reach = hold * reach
        if b < GROUP - 1:
            state, reach = join[b] * state, join[b] * reach
    out[0:HALF_ROWS, :] = state
    out[HALF_ROWS:ROW_K, :] = ids
    partner = turn + 1 - 2 * core_of()
    local[0] = inside[turn, 0]
    local[1] = inside[turn, 1]
    local[2] = inside[partner, 0]
    local[3] = inside[partner, 1]
    for s in range(8):

        @pl.when(column == s)
        def _():
            for b in range(GROUP):
                ends[b] = inside[b, 2, pl.ds(s, POLES, stride=8), :]


def entry_kernel(local, mine, other, keep, send):
    late = jnp.where(is_late(), 1.0, 0.0)
    met = (other[ROW_K - 1 : ROW_K, LANES - 1 : LANES] == mine[HALF_ROWS : HALF_ROWS + 1, 0:1])
    carry = other[0:HALF_ROWS, :] * spread(met.astype(F32), HALF_ROWS) * late
    keep[...] = local[0] + local[1] * carry
    send[...] = local[2] + local[3] * carry


def keys_kernel(got, kv):
    kv[...] = got[:, ROW_K:ROW_Q, :]


def entry_states(keep, got, g):
    mine = core_of() == g
    return tuple(
        jnp.where(mine, keep[8 * n : 8 * n + 8, :], got[8 * n : 8 * n + 8, :]) for n in range(POLES)
    )


def forward_kernel(docs, keep, got, m, dec, wgt, hq, hg, gain, f, sums):
    for g in range(2):
        kept = [dec[n * 16 + 8 * g : n * 16 + 8 * g + 8, :] for n in range(POLES)]
        weights = [wgt[n * 16 + 8 * g : n * 16 + 8 * g + 8, :] for n in range(POLES)]

        def step(t, state):
            at = pl.ds(pl.multiple_of(t * 16 + 8 * g, 8), 8)
            x = m[at, :]
            state = tuple(d * s + x for d, s in zip(kept, state))
            terms = [w * s for w, s in zip(weights, state)]
            while len(terms) > 1:
                terms = [a + b for a, b in zip(terms[::2], terms[1::2])]
            f[at, :] = terms[0]
            return state

        forward_groups(docs, step, entry_states(keep, got, g))
    squares = jnp.zeros((TOK, LANES), F32)
    along = jnp.zeros((TOK, LANES), F32)
    for j in range(CHUNKS):
        out_y = hq[:, lanes(j)].astype(F32) * f[every(j, TOK), :]
        squares = squares + out_y * out_y
        along = along + hg[:, lanes(j)].astype(F32) * gain[:, lanes(j)] * out_y
    sums[0:1, :] = jnp.sum(squares.T, axis=0, keepdims=True)
    sums[1:2, :] = jnp.sum(along.T, axis=0, keepdims=True)
    sums[2:8, :] = jnp.zeros((6, LANES), F32)


def backward_kernel(docs, s0, s1, s2, s3, f, m, dec, hq, hg, gain, ghq, gf, send, starts, totals):
    total = s0[...] + s1[...] + s2[...] + s3[...]
    inv = lax.rsqrt(total[0:1, :] / D + EPSILON)
    slope = inv * inv * inv * total[1:2, :] / D
    inv = jnp.broadcast_to(inv, (TOK, LANES)).T
    slope = jnp.broadcast_to(slope, (TOK, LANES)).T
    for j in range(CHUNKS):
        q = hq[:, lanes(j)].astype(F32)
        back = hg[:, lanes(j)].astype(F32)
        row = f[every(j, TOK), :]
        out_y = q * row
        grad_y = inv * (back * gain[:, lanes(j)]) - out_y * slope
        ghq[:, lanes(j)] = (grad_y * row).astype(BF16)
        gf[every(j, TOK), :] = grad_y * q
        gain_part = jnp.sum(back * out_y * inv, axis=0, keepdims=True)
        send[place_of(j), BACK_GAIN:ROWS_BACK, :] = pair_rows(gain_part)
    for g in range(2):
        kept = [dec[n * 16 + 8 * g : n * 16 + 8 * g + 8, :] for n in range(POLES)]

        def step(t, carry):
            at = pl.ds(pl.multiple_of(t * 16 + 8 * g, 8), 8)
            x, feed = gf[at, :], m[at, :]
            state = tuple(d * s + x for d, s in zip(kept, carry[:POLES]))
            return state + tuple(k + feed * s for k, s in zip(carry[POLES:], state))

        zero = (jnp.zeros((8, LANES), F32),) * (2 * POLES)
        carry = backward_groups(docs, step, zero, POLES)
        for n in range(POLES):
            starts[n * 16 + 8 * g : n * 16 + 8 * g + 8, :] = carry[n]
            totals[n * 16 + 8 * g : n * 16 + 8 * g + 8, :] = carry[POLES + n]
    for p in range(GROUP):
        send[p, 0:16, :] = starts[every(chunk_of(p), POLES), :].astype(BF16)
        high, low = split(totals[every(chunk_of(p), POLES), :])
        send[p, BACK_SUM : BACK_SUM + 16, :] = high
        send[p, BACK_SUM + 16 : BACK_GAIN, :] = low


def half_adjoint_kernel(docs_mine, ends, back, rate, docs_other, out):
    ids, other = docs_mine[HALF_ROWS:ROW_K, :], docs_other[HALF_ROWS:ROW_K, :]
    same, join = flags_of(ids)
    rates = rate[...]
    through = jnp.exp(-float(TOK) * rates)
    decay = jnp.exp(-rates)
    early = jnp.where(is_late(), 0.0, 1.0)
    met = spread((other[0:1, 0:1] == ids[15:16, LANES - 1 : LANES]).astype(F32)) * early
    total = jnp.zeros((POLES, LANES), F32)
    reach = jnp.zeros((POLES, LANES), F32)
    gains = jnp.zeros((8, LANES), F32)
    carry = jnp.zeros((POLES, LANES), F32)
    unit = met
    for b in reversed(range(GROUP)):
        end = decay * ends[b]
        total = total + joined(back, block_at(b), BACK_SUM) + end * carry
        reach = reach + end * unit
        pair = back[block_at(b), BACK_GAIN:ROWS_BACK, :].astype(F32)
        gains = gains + pair[0:8] + pair[8:16]
        carry = back[block_at(b), 0:16, :].astype(F32) + same[b] * through * carry
        unit = same[b] * through * unit
        if b > 0:
            carry = join[b - 1] * carry
            unit = join[b - 1] * unit
    out[0:16, :] = carry
    out[16:32, :] = total
    out[32:48, :] = reach
    out[48:56, :] = gains


def last_pack_kernel(
    docs_mine, back, rate, docs_other, mine, theirs, dq, own, own_got, prev_got, send
):
    ids, other = docs_mine[HALF_ROWS:ROW_K, :], docs_other[HALF_ROWS:ROW_K, :]
    same, join = flags_of(ids)
    rates = rate[...]
    through = jnp.exp(-float(TOK) * rates)
    early = jnp.where(is_late(), 0.0, 1.0)
    met = spread((other[0:1, 0:1] == ids[15:16, LANES - 1 : LANES]).astype(F32)) * early
    late_start = mine[0:16, :] * (1.0 - early) + theirs[0:16, :] * early
    early_reach = mine[32:48, :] * early + theirs[32:48, :] * (1.0 - early)
    residue = mine[16:32, :] + theirs[16:32, :] + late_start * early_reach
    res_high, res_low = split(scaling_of(rates) * residue)
    pair = pair_rows((mine[48:56, :] + theirs[48:56, :])[0:1])
    carry = theirs[0:16, :] * met
    for b in reversed(range(GROUP)):
        at = block_at(b)
        send[at, 0:OUT_RES, :] = carry.astype(BF16)
        send[at, OUT_RES : OUT_RES + 16, :] = res_high
        send[at, OUT_RES + 16 : OUT_GAIN, :] = res_low
        send[at, OUT_GAIN:OUT_Q, :] = pair
        send[at, OUT_Q:OUT_KV, :] = dq[at]
        kv = own[at].astype(F32) + own_got[at].astype(F32) + prev_got[at].astype(F32) * early
        send[at, OUT_KV:ROWS_OUT, :] = kv.astype(BF16)
        if b > 0:
            carry = join[b - 1] * (back[at, 0:16, :].astype(F32) + same[b] * through * carry)


def final_kernel(
    docs, got, gf, dec, wgt, hk, hv, ghk, ghv, gres, ggain, gaq, gak, gav, gm, entry
):
    for p in range(GROUP):
        j = chunk_of(p)
        entry[16 * j : 16 * j + 16, :] = got[p, 0:OUT_RES, :].astype(F32)
        gres[:, lanes(j)] = joined(got, p, OUT_RES)
        pair = got[p, OUT_GAIN:OUT_Q, :].astype(F32)
        ggain[:, lanes(j)] = pair[0:1] + pair[8:9]
        rows = slice(64 * (p % 2), 64 * (p % 2) + 64)
        gaq[rows, lanes(p // 2)] = got[p, OUT_Q:OUT_KV, :]
        gak[rows, lanes(p // 2)] = got[p, OUT_KV : OUT_KV + 64, :]
        gav[rows, lanes(p // 2)] = got[p, OUT_KV + 64 : ROWS_OUT, :]
    for g in range(2):
        kept = [dec[n * 16 + 8 * g : n * 16 + 8 * g + 8, :] for n in range(POLES)]
        weights = [wgt[n * 16 + 8 * g : n * 16 + 8 * g + 8, :] for n in range(POLES)]

        def step(t, state):
            at = pl.ds(pl.multiple_of(t * 16 + 8 * g, 8), 8)
            x = gf[at, :]
            state = tuple(d * s + x for d, s in zip(kept, state))
            terms = [w * s for w, s in zip(weights, state)]
            while len(terms) > 1:
                terms = [a + b for a, b in zip(terms[::2], terms[1::2])]
            gm[at, :] = terms[0]
            return state

        start = tuple(entry[every(8 * g * 16 + n, 8), :] for n in range(POLES))
        backward_groups(docs, step, start, POLES)
    for j in range(CHUNKS):
        row = gm[every(j, TOK), :]
        ghk[:, lanes(j)] = (row * hv[:, lanes(j)].astype(F32)).astype(BF16)
        ghv[:, lanes(j)] = (row * hk[:, lanes(j)].astype(F32)).astype(BF16)


def place(keys, values, b, at_core, key_rows, value_rows):
    at = pl.ds(pl.multiple_of(TOK * b + 64 * at_core, 64), 64)
    keys[at, :] = key_rows
    values[at, :] = value_rows


def turn_keys(keys, turned):
    def one(t, _):
        at = pl.ds(pl.multiple_of(t * KEYS_TILE, KEYS_TILE), KEYS_TILE)
        turned[t] = keys[at, :].astype(F32).T.astype(BF16)
        return 0

    lax.fori_loop(0, HALF_TILES, one, 0)


def own_keys_kernel(kv, kv_core, keys, values, turned):
    core = core_of()
    for b in range(GROUP):
        s = block_at(b)
        place(keys, values, b, core, kv[s, 0:64, :], kv[s, 64:128, :])
        place(keys, values, b, 1 - core, kv_core[s, 0:64, :], kv_core[s, 64:128, :])
    turn_keys(keys, turned)


def send_keys_kernel(kv, after, out):
    out[...] = kv[...]


def attention_kernel(
    got, own_k, own_v, own_turned, kv_half, kv_half_core, ids_mine, ids_other, after,
    dq, own, own_send, prev, prev_send,
    prev_k, prev_v, prev_turned, scores, products, peaks, dk, dv,
):
    core = core_of()
    late = is_late()

    @pl.when(late)
    def _():
        for b in range(GROUP):
            place(prev_k, prev_v, b, core, kv_half[b, 0:64, :], kv_half[b, 64:128, :])
            place(
                prev_k, prev_v, b, 1 - core, kv_half_core[b, 0:64, :], kv_half_core[b, 64:128, :]
            )
        turn_keys(prev_k, prev_turned)

    def clear(t, _):
        at = pl.ds(pl.multiple_of(t * KEYS_TILE, KEYS_TILE), KEYS_TILE)
        dk[at, :] = jnp.zeros((KEYS_TILE, HEAD_DIM), F32)
        dv[at, :] = jnp.zeros((KEYS_TILE, HEAD_DIM), F32)
        return 0

    lax.fori_loop(jnp.where(late, 0, HALF_TILES), N_TILES, clear, 0)

    own_ids, other_ids = ids_mine[HALF_ROWS:ROW_K, :], ids_other[HALF_ROWS:ROW_K, :]
    base = jnp.where(late, 0, HALF)
    starts = []
    for d in (1, 2, 3):
        before = jnp.sum((own_ids < d).astype(F32)).astype(jnp.int32)
        behind = jnp.sum((other_ids < d).astype(F32)).astype(jnp.int32)
        starts.append(before + jnp.where(late, behind, HALF))

    def start_of(pos):
        result = jnp.where(pos >= starts[0], starts[0], base)
        for start in starts[1:]:
            result = jnp.where(pos >= start, start, result)
        return result

    def query_tile(i, _):
        rows_q = jnp.concatenate([got[block_at(4 * i + u), ROW_Q:ROW_G, :] for u in range(4)], axis=0)
        rows_g = jnp.concatenate([got[block_at(4 * i + u), ROW_G:ROWS_IN, :] for u in range(4)], axis=0)
        turned_q = rows_q.astype(F32).T.astype(BF16)
        turned_g = rows_g.astype(F32).T.astype(BF16)
        lane = lax.broadcasted_iota(jnp.int32, (1, ROWS_TILE), 1)
        qpos = HALF + 512 * i + 128 * (lane // 64) + 64 * core + lax.rem(lane, 64)
        qstart = start_of(qpos)
        low = start_of(HALF + 512 * i + 64 * core) // KEYS_TILE
        high = HALF // KEYS_TILE + i + 1
        row = lax.broadcasted_iota(jnp.int32, (KEYS_TILE, ROWS_TILE), 0)

        def fold(value, by):
            return by(value.reshape(KEYS_TILE // 8, 8, ROWS_TILE), axis=0)

        def first_pass(keys, values, base, t, carry):
            peak, total, weighted = carry
            at = pl.ds(pl.multiple_of((t - base) * KEYS_TILE, KEYS_TILE), KEYS_TILE)
            s = jnp.dot(keys[at, :], turned_q, preferred_element_type=F32)
            gp = jnp.dot(values[at, :], turned_g, preferred_element_type=F32)
            first = t * KEYS_TILE
            s = jnp.where((row <= qpos - first) & (row >= qstart - first), s, FLOOR_SCORE)
            top = jnp.maximum(peak, jnp.max(fold(s, jnp.max), axis=0, keepdims=True))
            p = jnp.exp2((s - top) * (SCALE * LOG2E))
            scores[t] = p
            products[t] = gp
            peaks[t] = jnp.broadcast_to(top, (8, ROWS_TILE))
            shrink = jnp.exp2((peak - top) * (SCALE * LOG2E))
            return top, total * shrink + fold(p, jnp.sum), weighted * shrink + fold(p * gp, jnp.sum)

        zero = jnp.zeros((8, ROWS_TILE), F32)
        floor = jnp.full((1, ROWS_TILE), FLOOR_SCORE, F32)
        ahead = functools.partial(first_pass, prev_k, prev_v, 0)
        carry = lax.fori_loop(low, HALF_TILES, ahead, (floor, zero, zero))
        within = functools.partial(first_pass, own_k, own_v, HALF_TILES)
        middle = jnp.maximum(low, HALF_TILES)
        peak, total, weighted = lax.fori_loop(middle, high, within, carry)
        inv = 1.0 / jnp.sum(total, axis=0, keepdims=True)
        centre = jnp.sum(weighted, axis=0, keepdims=True) * inv

        def second_pass(turned, base, t, turned_dq):
            at = pl.ds(pl.multiple_of(t * KEYS_TILE, KEYS_TILE), KEYS_TILE)
            p = scores[t] * (jnp.exp2((peaks[t][0:1] - peak) * (SCALE * LOG2E)) * inv)
            ds = (p * (products[t] - centre)).astype(BF16)
            dk[at, :] += jnp.dot(ds, rows_q, preferred_element_type=F32)
            dv[at, :] += jnp.dot(p.astype(BF16), rows_g, preferred_element_type=F32)
            return turned_dq + jnp.dot(turned[t - base], ds, preferred_element_type=F32)

        zero = jnp.zeros((HEAD_DIM, ROWS_TILE), F32)
        ahead = functools.partial(second_pass, prev_turned, 0)
        turned_dq = lax.fori_loop(low, HALF_TILES, ahead, zero)
        within = functools.partial(second_pass, own_turned, HALF_TILES)
        turned_dq = lax.fori_loop(middle, high, within, turned_dq)
        rows = (turned_dq * SCALE).T.astype(BF16)
        for u in range(4):
            dq[block_at(4 * i + u)] = rows[64 * u : 64 * u + 64]
        return 0

    lax.fori_loop(0, Q_TILES, query_tile, 0)

    def leave(base, target, target_send, order):
        for b in range(GROUP):
            s = order(b)
            for at_core, ref in ((core, target), (1 - core, target_send)):
                at = pl.ds(pl.multiple_of(base + TOK * b + 64 * at_core, 64), 64)
                ref[s, 0:64, :] = (dk[at, :] * SCALE).astype(BF16)
                ref[s, 64:128, :] = dv[at, :].astype(BF16)

    leave(HALF, own, own_send, block_at)

    @pl.when(late)
    def _():
        leave(0, prev, prev_send, lambda b: b)

    @pl.when(jnp.logical_not(late))
    def _():
        prev[...] = jnp.zeros(prev.shape, BF16)
        prev_send[...] = jnp.zeros(prev_send.shape, BF16)


def body(
    hyena_q, hyena_k, hyena_v, hyena_grad, pole_rate, residue, norm_gain, doc_ids,
    attn_q, attn_k, attn_v, attn_grad,
):
    count = 2 * GROUP
    early = list(range(GROUP))
    late = [GROUP + (p ^ 8) for p in early]
    swap_core = [(i, i ^ 1) for i in range(count)]
    up_half = list(zip(early, late))
    down_half = list(zip(late, early))
    swap_half = up_half + down_half

    def exchange(x):
        return lax.all_to_all(x, "ctx", 0, 0, tiled=True, axis_index_groups=[early, late])

    gain = norm_gain.reshape(1, CH)
    sweep = (TOK * CHUNKS, LANES)
    params = (POLES * CHUNKS, LANES)
    vmem = pltpu.VMEM
    hbm = pl.BlockSpec(memory_space=pltpu.HBM)
    send, m, dec, wgt, through, rate_part = call(
        first_kernel,
        [((GROUP, ROWS_IN, LANES), BF16), (sweep, F32), (params, F32), (params, F32)]
        + [(half_shape, F32), ((POLES, LANES), F32)],
        doc_ids, doc_ids.reshape(1, TOK), pole_rate, residue, hyena_k, hyena_v,
        attn_k, attn_v, attn_q, attn_grad,
        smem=(0,), specs={i: hbm for i in range(2, 10)},
        scratch=[vmem(params, F32)] + [vmem((POLES, CH), F32)] * 2 + [vmem((TOK, CH), BF16)] * 2
        + [vmem((TOK, 1024), BF16)] * 4 + [pltpu.SemaphoreType.DMA((8,))],
        flops=40_000_000, nbytes=6_000_000, vmem=60 << 20,
    )
    got = exchange(send)
    mine, local, ends = call(
        half_state_kernel,
        [((ROW_K, LANES), F32), ((4,) + half_shape, F32), ((GROUP, POLES, LANES), F32)],
        got, through, scratch=[vmem((GROUP, 3) + half_shape, F32)],
        flops=1_000_000, nbytes=300_000,
    )
    other = lax.ppermute(mine, "ctx", swap_half)
    part = (GROUP, TOK, HEAD_DIM)
    (kv,) = call(keys_kernel, [(part, BF16)], got, flops=1000, nbytes=1_000_000)
    kv_core = lax.ppermute(kv, "ctx", swap_core)
    (kv_later,) = call(
        send_keys_kernel, [(part, BF16)], kv, other, flops=1000, nbytes=1_000_000
    )
    kv_half = lax.ppermute(kv_later, "ctx", up_half)
    flat = (HALF, HEAD_DIM)
    turned = (HALF_TILES, HEAD_DIM, KEYS_TILE)
    own_k, own_v, own_turned = call(
        own_keys_kernel, [(flat, BF16), (flat, BF16), (turned, BF16)], kv, kv_core,
        flops=1_000_000, nbytes=4_000_000,
    )
    carry, carry_send = call(
        entry_kernel, [(half_shape, F32)] * 2, local, mine, other, flops=100_000, nbytes=300_000
    )
    carry_got = lax.ppermute(carry_send, "ctx", swap_core)
    f, sums = call(
        forward_kernel, [(sweep, F32), ((8, LANES), F32)],
        doc_ids, carry, carry_got, m, dec, wgt, hyena_q, hyena_grad, gain,
        smem=(0,), flops=40_000_000, nbytes=6_000_000,
    )
    shared = [
        lax.ppermute(sums, "chan", [(i, (i + k) % 4) for i in range(4)]) for k in (1, 2, 3)
    ]
    shared[0], kv_half = lax.optimization_barrier((shared[0], kv_half))
    kv_half_core = lax.ppermute(kv_half, "ctx", swap_core)
    dq, own, own_send, prev, prev_send = call(
        attention_kernel,
        [((GROUP, 64, HEAD_DIM), BF16)] + [(part, BF16)] * 4,
        got, own_k, own_v, own_turned, kv_half, kv_half_core, mine, other, sums,
        scratch=[
            vmem(flat, BF16),
            vmem(flat, BF16),
            vmem(turned, BF16),
            vmem((N_TILES, KEYS_TILE, ROWS_TILE), F32),
            vmem((N_TILES, KEYS_TILE, ROWS_TILE), F32),
            vmem((N_TILES, 8, ROWS_TILE), F32),
            vmem((2 * HALF, HEAD_DIM), F32),
            vmem((2 * HALF, HEAD_DIM), F32),
        ],
        flops=10_000_000_000, nbytes=6_000_000, vmem=28 << 20,
    )
    f, dq = lax.optimization_barrier((f, dq))
    ghq, gf, back_send = call(
        backward_kernel,
        [((TOK, CH), BF16), (sweep, F32), ((GROUP, ROWS_BACK, LANES), BF16)],
        doc_ids, sums, *shared, f, m, dec, hyena_q, hyena_grad, gain,
        smem=(0,), scratch=[vmem(params, F32), vmem(params, F32)],
        flops=40_000_000, nbytes=6_000_000,
    )
    back_send, own_send, prev_send = lax.optimization_barrier((back_send, own_send, prev_send))
    prev_got = lax.ppermute(prev_send, "ctx", swap_core)
    own_got = lax.ppermute(own_send, "ctx", swap_core)
    prev_sum = (prev.astype(F32) + prev_got.astype(F32)).astype(BF16)
    prev_home = lax.ppermute(prev_sum, "ctx", down_half)
    back = exchange(back_send)
    (half_mine,) = call(
        half_adjoint_kernel, [((56, LANES), F32)], mine, ends, back, rate_part, other,
        flops=1_000_000, nbytes=300_000,
    )
    half_other = lax.ppermute(half_mine, "ctx", swap_half)
    (last_send,) = call(
        last_pack_kernel, [((GROUP, ROWS_OUT, LANES), BF16)],
        mine, back, rate_part, other, half_mine, half_other, dq, own, own_got, prev_home,
        flops=1_000_000, nbytes=3_000_000,
    )
    last = exchange(last_send)
    ghk, ghv, gres, ggain, gaq, gak, gav = call(
        final_kernel,
        [((TOK, CH), BF16), ((TOK, CH), BF16), ((POLES, CH), F32), ((1, CH), F32)]
        + [((TOK, 1024), BF16)] * 3,
        doc_ids, last, gf, dec, wgt, hyena_k, hyena_v,
        smem=(0,), scratch=[vmem(sweep, F32), vmem(params, F32)],
        flops=40_000_000, nbytes=6_000_000,
    )
    return (ghq, ghk, ghv, gres, ggain.reshape(CH), gaq, gak, gav)


def solution(mesh):
    wide, deep, one = P("ctx", "chan"), P(None, "chan"), P("chan")
    return jax.shard_map(
        body,
        mesh=mesh,
        in_specs=(wide,) * 4 + (deep, deep, one, P("ctx")) + (wide,) * 4,
        out_specs=(wide, wide, wide, deep, one, wide, wide, wide),
        check_vma=False,
    )
```

```python
import functools

import jax
import jax.numpy as jnp
from jax import lax
from jax.experimental import pallas as pl
from jax.experimental.pallas import tpu as pltpu
from jax.sharding import PartitionSpec as P

D = 8192
HEAD_DIM = 128
EPSILON = 1e-06
FLOOR_SCORE = -1e30

TOK = 128
CH = 2048
POLES = 16
LANES = 128
CHUNKS = CH // LANES
GROUP = 16
HALF = GROUP * TOK
SPAN = 32
SCALE = HEAD_DIM ** (-0.5)
LOG2E = 1.4426950408889634

HALF_ROWS = POLES * 8
half_shape = (HALF_ROWS, LANES)
ROW_DOC, ROW_K, ROW_V, ROW_Q, ROW_G, ROWS_IN = 128, 144, 208, 272, 336, 400
OUT_RES, OUT_GAIN, OUT_Q, OUT_KV, ROWS_OUT = 16, 48, 64, 128, 256
BACK_SUM, BACK_GAIN, ROWS_BACK = 16, 48, 64

ROWS_TILE = 256
KEYS_TILE = 512
N_TILES = 2 * HALF // KEYS_TILE
HALF_TILES = N_TILES // 2
CHUNK = 256
STEP = 256
Q_TILES = 4

F32 = jnp.float32
BF16 = jnp.bfloat16


def call(kernel, outs, *args, scratch=(), smem=(), flops=0, nbytes=0, vmem=24 << 20, specs=None, far=()):
    grid = (1,) if specs else ()
    specs = specs or {}
    ins = [
        pl.BlockSpec(memory_space=pltpu.SMEM) if i in smem
        else specs.get(i, pl.BlockSpec(memory_space=pltpu.VMEM))
        for i in range(len(args))
    ]
    shapes = [jax.ShapeDtypeStruct(shape, kind) for shape, kind in outs]
    return pl.pallas_call(
        kernel,
        out_shape=shapes,
        grid=grid,
        in_specs=ins,
        out_specs=[
            pl.BlockSpec(memory_space=pltpu.HBM if i in far else pltpu.VMEM) for i in range(len(outs))
        ],
        scratch_shapes=list(scratch),
        cost_estimate=pl.CostEstimate(flops=flops, bytes_accessed=nbytes, transcendentals=0),
        compiler_params=pltpu.CompilerParams(vmem_limit_bytes=vmem),
    )(*args)


def every(start, size):
    return pl.ds(start, size, stride=CHUNKS)


def lanes(j):
    return slice(LANES * j, LANES * (j + 1))


def split(value):
    high = value.astype(BF16)
    return high, (value - high.astype(F32)).astype(BF16)


def scaling_of(rate):
    y = 2.0 * rate
    series = 1.0 - y / 6.0
    for k in (5.0, 4.0, 3.0, 2.0):
        series = 1.0 - y / k * series
    return jnp.sqrt(y * series)


def forward_groups(docs, step, state):
    def group(i, state):
        first = i * SPAN

        def plain(state):
            for u in range(SPAN):
                state = step(first + u, state)
            return state

        def cut(state):
            for u in range(SPAN):
                t = first + u
                keep = jnp.where(docs[t] == docs[jnp.maximum(t - 1, 0)], 1.0, 0.0)
                state = step(t, tuple(s * keep for s in state))
            return state

        whole = docs[jnp.maximum(first - 1, 0)] == docs[first + SPAN - 1]
        return lax.cond(whole, plain, cut, state)

    return lax.fori_loop(0, TOK // SPAN, group, state)


def backward_groups(docs, step, state, count):
    def group(i, state):
        first = TOK - SPAN - i * SPAN

        def plain(state):
            for u in reversed(range(SPAN)):
                state = step(first + u, state)
            return state

        def cut(state):
            for u in reversed(range(SPAN)):
                t = first + u
                keep = jnp.where(docs[t] == docs[jnp.minimum(t + 1, TOK - 1)], 1.0, 0.0)
                state = tuple(s * keep for s in state[:count]) + tuple(state[count:])
                state = step(t, state)
            return state

        whole = docs[first] == docs[jnp.minimum(first + SPAN, TOK - 1)]
        return lax.cond(whole, plain, cut, state)

    return lax.fori_loop(0, TOK // SPAN, group, state)


def split(value):
    high = value.astype(BF16)
    return high, (value - high.astype(F32)).astype(BF16)


def pair_rows(row):
    high, low = split(jnp.broadcast_to(row, (8, LANES)))
    return jnp.concatenate([high.astype(F32), low.astype(F32)], axis=0).astype(BF16)


def joined(ref, index, row):
    return ref[index, row : row + 16, :].astype(F32) + ref[index, row + 16 : row + 32, :].astype(F32)


def first_kernel(
    docs, doc_row, rate_hbm, res_hbm, hk_hbm, hv_hbm, ak_hbm, av_hbm, aq_hbm, ag_hbm,
    send, m_out, dec, wgt, through, rate_part,
    thr_all, rate, res, hk, hv, ak, av, aq, ag, m, sems,
):
    pairs = (
        (rate_hbm, rate), (res_hbm, res), (hk_hbm, hk), (hv_hbm, hv),
        (ak_hbm, ak), (av_hbm, av), (aq_hbm, aq), (ag_hbm, ag),
    )
    copies = [
        pltpu.make_async_copy(source, target, sems.at[i])
        for i, (source, target) in enumerate(pairs)
    ]
    for copy in copies:
        copy.start()
    ids = jnp.broadcast_to(doc_row[...].astype(F32), (16, LANES)).astype(BF16)
    for p in range(GROUP):
        send[p, ROW_DOC:ROW_K, :] = ids
    core = core_of()
    copies[0].wait()
    copies[1].wait()
    rates = rate[...]
    start = pl.multiple_of(chunk_of(position()) * LANES, LANES)
    rate_part[...] = rate[:, pl.ds(start, LANES)]
    decay = jnp.exp(-rates)
    weight = res[...] * scaling_of(rates)
    block = jnp.exp(-float(TOK) * rates)
    for j in range(CHUNKS):
        dec[every(j, POLES), :] = decay[:, lanes(j)]
        wgt[every(j, POLES), :] = weight[:, lanes(j)]
        thr_all[every(j, POLES), :] = block[:, lanes(j)]
    for n in range(POLES):
        at = pl.ds(pl.multiple_of(16 * n + 8 * core, 8), 8)
        through[8 * n : 8 * n + 8, :] = thr_all[at, :]
    copies[2].wait()
    copies[3].wait()
    for j in range(CHUNKS):
        m[every(j, TOK), :] = hk[:, lanes(j)].astype(F32) * hv[:, lanes(j)].astype(F32)
    leaving = pltpu.make_async_copy(m, m_out, sems.at[8])
    leaving.start()
    for g in range(2):
        kept = [dec[n * 16 + 8 * g : n * 16 + 8 * g + 8, :] for n in range(POLES)]

        def step(t, state):
            x = m[pl.ds(pl.multiple_of(t * 16 + 8 * g, 8), 8), :]
            return tuple(d * s + x for d, s in zip(kept, state))

        state = forward_groups(docs, step, (jnp.zeros((8, LANES), F32),) * POLES)
        pairs = [jnp.concatenate(state[n : n + 2], axis=0).astype(BF16) for n in range(0, POLES, 2)]
        for p in range(g, GROUP, 2):
            for i, pair in enumerate(pairs):
                send[p, 16 * i : 16 * i + 16, :] = pair
    for copy, row, ref in zip(copies[4:], (ROW_K, ROW_V, ROW_Q, ROW_G), (ak, av, aq, ag)):
        copy.wait()
        for p in range(GROUP):
            part = slice(64 * (p % 2), 64 * (p % 2) + 64)
            send[p, row : row + 64, :] = ref[part, lanes(p // 2)]
    leaving.wait()


def is_late():
    return lax.axis_index("ctx") >= GROUP


def block_at(b):
    return lax.rem(b + jnp.where(is_late(), 8, 0), GROUP)


def position():
    return block_at(lax.rem(lax.axis_index("ctx"), GROUP))


def core_of():
    return lax.rem(lax.axis_index("ctx"), 2)


def chunk_of(p):
    return 8 * (p % 2) + p // 2


def place_of(j):
    return 2 * (j % 8) + j // 8


def block_docs(got):
    rows = [got[block_at(b), ROW_DOC:ROW_K, :].astype(F32)[0:1] for b in range(GROUP)]
    return jnp.concatenate(rows, axis=0)


def spread(value, rows=POLES):
    return jnp.broadcast_to(value, (rows, LANES))


def flags_of(ids, rows=POLES):
    first, last = ids[:, 0:1], ids[:, LANES - 1 : LANES]
    same = [spread((first[b : b + 1] == last[b : b + 1]).astype(F32), rows) for b in range(GROUP)]
    join = [
        spread((last[b : b + 1] == first[b + 1 : b + 2]).astype(F32), rows) for b in range(GROUP - 1)
    ]
    return same, join


def half_state_kernel(got, through, out, local, ends, inside):
    ids = block_docs(got)
    same, join = flags_of(ids, HALF_ROWS)
    thr = through[...]
    state = jnp.zeros(half_shape, F32)
    reach = jnp.ones(half_shape, F32)
    turn = lax.rem(lax.axis_index("ctx"), GROUP)
    column = position() // 2
    for b in range(GROUP):
        inside[b, 0] = state
        inside[b, 1] = reach
        end = got[block_at(b), 0:HALF_ROWS, :].astype(F32)
        inside[b, 2] = end
        hold = same[b] * thr
        state = end + hold * state
        reach = hold * reach
        if b < GROUP - 1:
            state, reach = join[b] * state, join[b] * reach
    out[0:HALF_ROWS, :] = state
    out[HALF_ROWS:ROW_K, :] = ids
    partner = turn + 1 - 2 * core_of()
    local[0] = inside[turn, 0]
    local[1] = inside[turn, 1]
    local[2] = inside[partner, 0]
    local[3] = inside[partner, 1]
    for s in range(8):

        @pl.when(column == s)
        def _():
            for b in range(GROUP):
                ends[b] = inside[b, 2, pl.ds(s, POLES, stride=8), :]


def entry_kernel(local, mine, other, keep, send):
    late = jnp.where(is_late(), 1.0, 0.0)
    met = (other[ROW_K - 1 : ROW_K, LANES - 1 : LANES] == mine[HALF_ROWS : HALF_ROWS + 1, 0:1])
    carry = other[0:HALF_ROWS, :] * spread(met.astype(F32), HALF_ROWS) * late
    keep[...] = local[0] + local[1] * carry
    send[...] = local[2] + local[3] * carry


def keys_kernel(got, kv):
    kv[...] = got[:, ROW_K:ROW_Q, :]


def entry_states(keep, got, g):
    mine = core_of() == g
    return tuple(
        jnp.where(mine, keep[8 * n : 8 * n + 8, :], got[8 * n : 8 * n + 8, :]) for n in range(POLES)
    )


def forward_kernel(docs, keep, got, m, dec, wgt, hq, hg, gain, f, sums):
    for g in range(2):
        kept = [dec[n * 16 + 8 * g : n * 16 + 8 * g + 8, :] for n in range(POLES)]
        weights = [wgt[n * 16 + 8 * g : n * 16 + 8 * g + 8, :] for n in range(POLES)]

        def step(t, state):
            at = pl.ds(pl.multiple_of(t * 16 + 8 * g, 8), 8)
            x = m[at, :]
            state = tuple(d * s + x for d, s in zip(kept, state))
            terms = [w * s for w, s in zip(weights, state)]
            while len(terms) > 1:
                terms = [a + b for a, b in zip(terms[::2], terms[1::2])]
            f[at, :] = terms[0]
            return state

        forward_groups(docs, step, entry_states(keep, got, g))
    squares = jnp.zeros((TOK, LANES), F32)
    along = jnp.zeros((TOK, LANES), F32)
    for j in range(CHUNKS):
        out_y = hq[:, lanes(j)].astype(F32) * f[every(j, TOK), :]
        squares = squares + out_y * out_y
        along = along + hg[:, lanes(j)].astype(F32) * gain[:, lanes(j)] * out_y
    sums[0:1, :] = jnp.sum(squares.T, axis=0, keepdims=True)
    sums[1:2, :] = jnp.sum(along.T, axis=0, keepdims=True)
    sums[2:8, :] = jnp.zeros((6, LANES), F32)


def backward_kernel(docs, sums, after, f, m, dec, hq, hg, gain, ghq, gf, send, starts, totals):
    total = sums[...]
    inv = lax.rsqrt(total[0:1, :] / D + EPSILON)
    slope = inv * inv * inv * total[1:2, :] / D
    inv = jnp.broadcast_to(inv, (TOK, LANES)).T
    slope = jnp.broadcast_to(slope, (TOK, LANES)).T
    for j in range(CHUNKS):
        q = hq[:, lanes(j)].astype(F32)
        back = hg[:, lanes(j)].astype(F32)
        row = f[every(j, TOK), :]
        out_y = q * row
        grad_y = inv * (back * gain[:, lanes(j)]) - out_y * slope
        ghq[:, lanes(j)] = (grad_y * row).astype(BF16)
        gf[every(j, TOK), :] = grad_y * q
        gain_part = jnp.sum(back * out_y * inv, axis=0, keepdims=True)
        send[place_of(j), BACK_GAIN:ROWS_BACK, :] = pair_rows(gain_part)
    for g in range(2):
        kept = [dec[n * 16 + 8 * g : n * 16 + 8 * g + 8, :] for n in range(POLES)]

        def step(t, carry):
            at = pl.ds(pl.multiple_of(t * 16 + 8 * g, 8), 8)
            x, feed = gf[at, :], m[at, :]
            state = tuple(d * s + x for d, s in zip(kept, carry[:POLES]))
            return state + tuple(k + feed * s for k, s in zip(carry[POLES:], state))

        zero = (jnp.zeros((8, LANES), F32),) * (2 * POLES)
        carry = backward_groups(docs, step, zero, POLES)
        for n in range(POLES):
            starts[n * 16 + 8 * g : n * 16 + 8 * g + 8, :] = carry[n]
            totals[n * 16 + 8 * g : n * 16 + 8 * g + 8, :] = carry[POLES + n]
    for p in range(GROUP):
        send[p, 0:16, :] = starts[every(chunk_of(p), POLES), :].astype(BF16)
        high, low = split(totals[every(chunk_of(p), POLES), :])
        send[p, BACK_SUM : BACK_SUM + 16, :] = high
        send[p, BACK_SUM + 16 : BACK_GAIN, :] = low


def half_adjoint_kernel(docs_mine, ends, back, rate, docs_other, out):
    ids, other = docs_mine[HALF_ROWS:ROW_K, :], docs_other[HALF_ROWS:ROW_K, :]
    same, join = flags_of(ids)
    rates = rate[...]
    through = jnp.exp(-float(TOK) * rates)
    decay = jnp.exp(-rates)
    early = jnp.where(is_late(), 0.0, 1.0)
    met = spread((other[0:1, 0:1] == ids[15:16, LANES - 1 : LANES]).astype(F32)) * early
    total = jnp.zeros((POLES, LANES), F32)
    reach = jnp.zeros((POLES, LANES), F32)
    gains = jnp.zeros((8, LANES), F32)
    carry = jnp.zeros((POLES, LANES), F32)
    unit = met
    for b in reversed(range(GROUP)):
        end = decay * ends[b]
        total = total + joined(back, block_at(b), BACK_SUM) + end * carry
        reach = reach + end * unit
        pair = back[block_at(b), BACK_GAIN:ROWS_BACK, :].astype(F32)
        gains = gains + pair[0:8] + pair[8:16]
        carry = back[block_at(b), 0:16, :].astype(F32) + same[b] * through * carry
        unit = same[b] * through * unit
        if b > 0:
            carry = join[b - 1] * carry
            unit = join[b - 1] * unit
    out[0:16, :] = carry
    out[16:32, :] = total
    out[32:48, :] = reach
    out[48:56, :] = gains


def last_pack_kernel(
    docs_mine, back, rate, docs_other, mine, theirs, dq, own, own_got, prev_got, send
):
    ids, other = docs_mine[HALF_ROWS:ROW_K, :], docs_other[HALF_ROWS:ROW_K, :]
    same, join = flags_of(ids)
    rates = rate[...]
    through = jnp.exp(-float(TOK) * rates)
    early = jnp.where(is_late(), 0.0, 1.0)
    met = spread((other[0:1, 0:1] == ids[15:16, LANES - 1 : LANES]).astype(F32)) * early
    late_start = mine[0:16, :] * (1.0 - early) + theirs[0:16, :] * early
    early_reach = mine[32:48, :] * early + theirs[32:48, :] * (1.0 - early)
    residue = mine[16:32, :] + theirs[16:32, :] + late_start * early_reach
    res_high, res_low = split(scaling_of(rates) * residue)
    pair = pair_rows((mine[48:56, :] + theirs[48:56, :])[0:1])
    carry = theirs[0:16, :] * met
    for b in reversed(range(GROUP)):
        at = block_at(b)
        send[at, 0:OUT_RES, :] = carry.astype(BF16)
        send[at, OUT_RES : OUT_RES + 16, :] = res_high
        send[at, OUT_RES + 16 : OUT_GAIN, :] = res_low
        send[at, OUT_GAIN:OUT_Q, :] = pair
        send[at, OUT_Q:OUT_KV, :] = dq[at]
        kv = own[at].astype(F32) + own_got[at].astype(F32) + prev_got[at].astype(F32) * early
        send[at, OUT_KV:ROWS_OUT, :] = kv.astype(BF16)
        if b > 0:
            carry = join[b - 1] * (back[at, 0:16, :].astype(F32) + same[b] * through * carry)


def final_kernel(
    docs, got, gf, dec, wgt, hk, hv, ghk, ghv, gres, ggain, gaq, gak, gav, gm, entry
):
    for p in range(GROUP):
        j = chunk_of(p)
        entry[16 * j : 16 * j + 16, :] = got[p, 0:OUT_RES, :].astype(F32)
        gres[:, lanes(j)] = joined(got, p, OUT_RES)
        pair = got[p, OUT_GAIN:OUT_Q, :].astype(F32)
        ggain[:, lanes(j)] = pair[0:1] + pair[8:9]
        rows = slice(64 * (p % 2), 64 * (p % 2) + 64)
        gaq[rows, lanes(p // 2)] = got[p, OUT_Q:OUT_KV, :]
        gak[rows, lanes(p // 2)] = got[p, OUT_KV : OUT_KV + 64, :]
        gav[rows, lanes(p // 2)] = got[p, OUT_KV + 64 : ROWS_OUT, :]
    for g in range(2):
        kept = [dec[n * 16 + 8 * g : n * 16 + 8 * g + 8, :] for n in range(POLES)]
        weights = [wgt[n * 16 + 8 * g : n * 16 + 8 * g + 8, :] for n in range(POLES)]

        def step(t, state):
            at = pl.ds(pl.multiple_of(t * 16 + 8 * g, 8), 8)
            x = gf[at, :]
            state = tuple(d * s + x for d, s in zip(kept, state))
            terms = [w * s for w, s in zip(weights, state)]
            while len(terms) > 1:
                terms = [a + b for a, b in zip(terms[::2], terms[1::2])]
            gm[at, :] = terms[0]
            return state

        start = tuple(entry[every(8 * g * 16 + n, 8), :] for n in range(POLES))
        backward_groups(docs, step, start, POLES)
    for j in range(CHUNKS):
        row = gm[every(j, TOK), :]
        ghk[:, lanes(j)] = (row * hv[:, lanes(j)].astype(F32)).astype(BF16)
        ghv[:, lanes(j)] = (row * hk[:, lanes(j)].astype(F32)).astype(BF16)


def place(keys, values, b, at_core, key_rows, value_rows):
    at = pl.ds(pl.multiple_of(TOK * b + 64 * at_core, 64), 64)
    keys[at, :] = key_rows
    values[at, :] = value_rows


def turn_keys(keys, turned):
    def one(t, _):
        at = pl.ds(pl.multiple_of(t * KEYS_TILE, KEYS_TILE), KEYS_TILE)
        turned[t] = keys[at, :].astype(F32).T.astype(BF16)
        return 0

    lax.fori_loop(0, HALF_TILES, one, 0)


def own_keys_kernel(got, kv, kv_core, keys, values, turned, rows_q, rows_g, turned_q, turned_g):
    core = core_of()
    for i in range(Q_TILES):
        for u in range(4):
            part = slice(64 * u, 64 * u + 64)
            rows_q[i, part, :] = got[block_at(4 * i + u), ROW_Q:ROW_G, :]
            rows_g[i, part, :] = got[block_at(4 * i + u), ROW_G:ROWS_IN, :]
        turned_q[i] = rows_q[i].astype(F32).T.astype(BF16)
        turned_g[i] = rows_g[i].astype(F32).T.astype(BF16)
    for b in range(GROUP):
        s = block_at(b)
        place(keys, values, b, core, kv[s, 0:64, :], kv[s, 64:128, :])
        place(keys, values, b, 1 - core, kv_core[s, 0:64, :], kv_core[s, 64:128, :])
    turn_keys(keys, turned)


def sums_kernel(s0, s1, s2, s3, total):
    total[...] = s0[...] + s1[...] + s2[...] + s3[...]


def send_keys_kernel(kv, after, out):
    out[...] = kv[...]


def attention_kernel(
    all_q, all_g, all_turned_q, all_turned_g, own_k, own_v, own_turned, kv_half, kv_half_core,
    ids_mine, ids_other, after,
    dq, own, own_send, prev, prev_send, token,
    prev_k, prev_v, prev_turned, scores, products, peaks, dk, dv,
):
    core = core_of()
    late = is_late()
    token[...] = jnp.zeros((8, LANES), F32)

    @pl.when(late)
    def _():
        for b in range(GROUP):
            place(prev_k, prev_v, b, core, kv_half[b, 0:64, :], kv_half[b, 64:128, :])
            place(
                prev_k, prev_v, b, 1 - core, kv_half_core[b, 0:64, :], kv_half_core[b, 64:128, :]
            )
        turn_keys(prev_k, prev_turned)

    def clear(t, _):
        at = pl.ds(pl.multiple_of(t * KEYS_TILE, KEYS_TILE), KEYS_TILE)
        dk[at, :] = jnp.zeros((KEYS_TILE, HEAD_DIM), F32)
        dv[at, :] = jnp.zeros((KEYS_TILE, HEAD_DIM), F32)
        return 0

    lax.fori_loop(jnp.where(late, 0, HALF_TILES), N_TILES, clear, 0)

    own_ids, other_ids = ids_mine[HALF_ROWS:ROW_K, :], ids_other[HALF_ROWS:ROW_K, :]
    base = jnp.where(late, 0, HALF)
    starts = []
    for d in (1, 2, 3):
        before = jnp.sum((own_ids < d).astype(F32)).astype(jnp.int32)
        behind = jnp.sum((other_ids < d).astype(F32)).astype(jnp.int32)
        starts.append(before + jnp.where(late, behind, HALF))

    def start_of(pos):
        result = jnp.where(pos >= starts[0], starts[0], base)
        for start in starts[1:]:
            result = jnp.where(pos >= start, start, result)
        return result

    def query_tile(i, _):
        rows_q, rows_g = all_q[i], all_g[i]
        turned_q, turned_g = all_turned_q[i], all_turned_g[i]
        lane = lax.broadcasted_iota(jnp.int32, (1, ROWS_TILE), 1)
        qpos = HALF + 512 * i + 128 * (lane // 64) + 64 * core + lax.rem(lane, 64)
        qstart = start_of(qpos)
        low = start_of(HALF + 512 * i + 64 * core) // KEYS_TILE
        high = HALF // KEYS_TILE + i + 1
        row = lax.broadcasted_iota(jnp.int32, (CHUNK, ROWS_TILE), 0)

        def fold(value, by):
            return by(value.reshape(CHUNK // 8, 8, ROWS_TILE), axis=0)

        def first_pass(keys, values, base, t, carry):
            peak, total, weighted = carry
            for u in range(KEYS_TILE // CHUNK):
                first = t * KEYS_TILE + u * CHUNK
                at = pl.ds(pl.multiple_of(first - base * KEYS_TILE, CHUNK), CHUNK)
                s = jnp.dot(keys[at, :], turned_q, preferred_element_type=F32)
                gp = jnp.dot(values[at, :], turned_g, preferred_element_type=F32)
                s = jnp.where((row <= qpos - first) & (row >= qstart - first), s, FLOOR_SCORE)
                top = jnp.maximum(peak, jnp.max(fold(s, jnp.max), axis=0, keepdims=True))
                p = jnp.exp2((s - top) * (SCALE * LOG2E))
                scores[t, u * CHUNK : u * CHUNK + CHUNK, :] = p
                products[t, u * CHUNK : u * CHUNK + CHUNK, :] = gp
                peaks[t, u : u + 1, :] = top
                shrink = jnp.exp2((peak - top) * (SCALE * LOG2E))
                total = total * shrink + fold(p, jnp.sum)
                weighted = weighted * shrink + fold(p * gp, jnp.sum)
                peak = top
            return peak, total, weighted

        zero = jnp.zeros((8, ROWS_TILE), F32)
        floor = jnp.full((1, ROWS_TILE), FLOOR_SCORE, F32)
        ahead = functools.partial(first_pass, prev_k, prev_v, 0)
        carry = lax.fori_loop(low, HALF_TILES, ahead, (floor, zero, zero))
        within = functools.partial(first_pass, own_k, own_v, HALF_TILES)
        middle = jnp.maximum(low, HALF_TILES)
        peak, total, weighted = lax.fori_loop(middle, high, within, carry)
        inv = 1.0 / jnp.sum(total, axis=0, keepdims=True)
        centre = jnp.sum(weighted, axis=0, keepdims=True) * inv

        def second_pass(turned, base, t, turned_dq):
            for v in range(KEYS_TILE // STEP):
                parts = []
                for u in range(v * STEP // CHUNK, (v + 1) * STEP // CHUNK):
                    rows = slice(u * CHUNK, u * CHUNK + CHUNK)
                    fall = jnp.exp2((peaks[t, u : u + 1, :] - peak) * (SCALE * LOG2E)) * inv
                    p = scores[t, rows, :] * fall
                    parts.append((p.astype(BF16), (p * (products[t, rows, :] - centre)).astype(BF16)))
                p = jnp.concatenate([one for one, _ in parts], axis=0)
                ds = jnp.concatenate([one for _, one in parts], axis=0)
                at = pl.ds(pl.multiple_of(t * KEYS_TILE + v * STEP, STEP), STEP)
                dk[at, :] += jnp.dot(ds, rows_q, preferred_element_type=F32)
                dv[at, :] += jnp.dot(p, rows_g, preferred_element_type=F32)
                part = turned[t - base, :, v * STEP : v * STEP + STEP]
                turned_dq = turned_dq + jnp.dot(part, ds, preferred_element_type=F32)
            return turned_dq

        zero = jnp.zeros((HEAD_DIM, ROWS_TILE), F32)
        ahead = functools.partial(second_pass, prev_turned, 0)
        turned_dq = lax.fori_loop(low, HALF_TILES, ahead, zero)
        within = functools.partial(second_pass, own_turned, HALF_TILES)
        turned_dq = lax.fori_loop(middle, high, within, turned_dq)
        rows = (turned_dq * SCALE).T.astype(BF16)
        for u in range(4):
            dq[block_at(4 * i + u)] = rows[64 * u : 64 * u + 64]
        return 0

    lax.fori_loop(0, Q_TILES, query_tile, 0)

    def leave(base, target, target_send, order):
        for b in range(GROUP):
            s = order(b)
            for at_core, ref in ((core, target), (1 - core, target_send)):
                at = pl.ds(pl.multiple_of(base + TOK * b + 64 * at_core, 64), 64)
                ref[s, 0:64, :] = (dk[at, :] * SCALE).astype(BF16)
                ref[s, 64:128, :] = dv[at, :].astype(BF16)

    leave(HALF, own, own_send, block_at)

    @pl.when(late)
    def _():
        leave(0, prev, prev_send, lambda b: b)

    @pl.when(jnp.logical_not(late))
    def _():
        prev[...] = jnp.zeros(prev.shape, BF16)
        prev_send[...] = jnp.zeros(prev_send.shape, BF16)


def body(
    hyena_q, hyena_k, hyena_v, hyena_grad, pole_rate, residue, norm_gain, doc_ids,
    attn_q, attn_k, attn_v, attn_grad,
):
    count = 2 * GROUP
    early = list(range(GROUP))
    late = [GROUP + (p ^ 8) for p in early]
    swap_core = [(i, i ^ 1) for i in range(count)]
    up_half = list(zip(early, late))
    down_half = list(zip(late, early))
    swap_half = up_half + down_half

    def exchange(x):
        return lax.all_to_all(x, "ctx", 0, 0, tiled=True, axis_index_groups=[early, late])

    gain = norm_gain.reshape(1, CH)
    sweep = (TOK * CHUNKS, LANES)
    params = (POLES * CHUNKS, LANES)
    vmem = pltpu.VMEM
    hbm = pl.BlockSpec(memory_space=pltpu.HBM)
    send, m, dec, wgt, through, rate_part = call(
        first_kernel,
        [((GROUP, ROWS_IN, LANES), BF16), (sweep, F32), (params, F32), (params, F32)]
        + [(half_shape, F32), ((POLES, LANES), F32)],
        doc_ids, doc_ids.reshape(1, TOK), pole_rate, residue, hyena_k, hyena_v,
        attn_k, attn_v, attn_q, attn_grad,
        smem=(0,), specs={i: hbm for i in range(2, 10)}, far=(1,),
        scratch=[vmem(params, F32)] + [vmem((POLES, CH), F32)] * 2 + [vmem((TOK, CH), BF16)] * 2
        + [vmem((TOK, 1024), BF16)] * 4 + [vmem(sweep, F32), pltpu.SemaphoreType.DMA((9,))],
        flops=40_000_000, nbytes=6_000_000, vmem=60 << 20,
    )
    got = exchange(send)
    mine, local, ends = call(
        half_state_kernel,
        [((ROW_K, LANES), F32), ((4,) + half_shape, F32), ((GROUP, POLES, LANES), F32)],
        got, through, scratch=[vmem((GROUP, 3) + half_shape, F32)],
        flops=1_000_000, nbytes=300_000,
    )
    other = lax.ppermute(mine, "ctx", swap_half)
    part = (GROUP, TOK, HEAD_DIM)
    (kv,) = call(keys_kernel, [(part, BF16)], got, flops=1000, nbytes=1_000_000)
    kv_core = lax.ppermute(kv, "ctx", swap_core)
    (kv_later,) = call(
        send_keys_kernel, [(part, BF16)], kv, other, flops=1000, nbytes=1_000_000
    )
    kv_half = lax.ppermute(kv_later, "ctx", up_half)
    flat = (HALF, HEAD_DIM)
    turned = (HALF_TILES, HEAD_DIM, KEYS_TILE)
    tall, wide = (Q_TILES, ROWS_TILE, HEAD_DIM), (Q_TILES, HEAD_DIM, ROWS_TILE)
    own_k, own_v, own_turned, *query_parts = call(
        own_keys_kernel,
        [(flat, BF16), (flat, BF16), (turned, BF16)] + [(tall, BF16)] * 2 + [(wide, BF16)] * 2,
        got, kv, kv_core,
        flops=1_000_000, nbytes=4_000_000,
    )
    carry, carry_send = call(
        entry_kernel, [(half_shape, F32)] * 2, local, mine, other, flops=100_000, nbytes=300_000
    )
    carry_got = lax.ppermute(carry_send, "ctx", swap_core)
    f, sums = call(
        forward_kernel, [(sweep, F32), ((8, LANES), F32)],
        doc_ids, carry, carry_got, m, dec, wgt, hyena_q, hyena_grad, gain,
        smem=(0,), flops=40_000_000, nbytes=6_000_000,
    )
    shared = [
        lax.ppermute(sums, "chan", [(i, (i + k) % 4) for i in range(4)]) for k in (1, 2, 3)
    ]
    (sums,) = call(
        sums_kernel, [((8, LANES), F32)], sums, *shared, flops=1000, nbytes=10_000
    )
    (kv_half,) = call(
        send_keys_kernel, [(part, BF16)], kv_half, sums, flops=1000, nbytes=1_000_000
    )
    kv_half_core = lax.ppermute(kv_half, "ctx", swap_core)
    dq, own, own_send, prev, prev_send, after = call(
        attention_kernel,
        [((GROUP, 64, HEAD_DIM), BF16)] + [(part, BF16)] * 4 + [((8, LANES), F32)],
        *query_parts, own_k, own_v, own_turned, kv_half, kv_half_core, mine, other, sums,
        scratch=[
            vmem(flat, BF16),
            vmem(flat, BF16),
            vmem(turned, BF16),
            vmem((N_TILES, KEYS_TILE, ROWS_TILE), F32),
            vmem((N_TILES, KEYS_TILE, ROWS_TILE), F32),
            vmem((N_TILES, 8, ROWS_TILE), F32),
            vmem((2 * HALF, HEAD_DIM), F32),
            vmem((2 * HALF, HEAD_DIM), F32),
        ],
        flops=10_000_000_000, nbytes=6_000_000, vmem=28 << 20,
    )
    ghq, gf, back_send = call(
        backward_kernel,
        [((TOK, CH), BF16), (sweep, F32), ((GROUP, ROWS_BACK, LANES), BF16)],
        doc_ids, sums, after, f, m, dec, hyena_q, hyena_grad, gain,
        smem=(0,), scratch=[vmem(params, F32), vmem(params, F32)],
        flops=40_000_000, nbytes=6_000_000,
    )
    prev_got = lax.ppermute(prev_send, "ctx", swap_core)
    own_got = lax.ppermute(own_send, "ctx", swap_core)
    back_send, prev_got = lax.optimization_barrier((back_send, prev_got))
    prev_sum = (prev.astype(F32) + prev_got.astype(F32)).astype(BF16)
    prev_home = lax.ppermute(prev_sum, "ctx", down_half)
    back = exchange(back_send)
    (half_mine,) = call(
        half_adjoint_kernel, [((56, LANES), F32)], mine, ends, back, rate_part, other,
        flops=1_000_000, nbytes=300_000,
    )
    half_other = lax.ppermute(half_mine, "ctx", swap_half)
    (last_send,) = call(
        last_pack_kernel, [((GROUP, ROWS_OUT, LANES), BF16)],
        mine, back, rate_part, other, half_mine, half_other, dq, own, own_got, prev_home,
        flops=1_000_000, nbytes=3_000_000,
    )
    last = exchange(last_send)
    ghk, ghv, gres, ggain, gaq, gak, gav = call(
        final_kernel,
        [((TOK, CH), BF16), ((TOK, CH), BF16), ((POLES, CH), F32), ((1, CH), F32)]
        + [((TOK, 1024), BF16)] * 3,
        doc_ids, last, gf, dec, wgt, hyena_k, hyena_v,
        smem=(0,), scratch=[vmem(sweep, F32), vmem(params, F32)],
        flops=40_000_000, nbytes=6_000_000,
    )
    return (ghq, ghk, ghv, gres, ggain.reshape(CH), gaq, gak, gav)


def solution(mesh):
    wide, deep, one = P("ctx", "chan"), P(None, "chan"), P("chan")
    return jax.shard_map(
        body,
        mesh=mesh,
        in_specs=(wide,) * 4 + (deep, deep, one, P("ctx")) + (wide,) * 4,
        out_specs=(wide, wide, wide, deep, one, wide, wide, wide),
        check_vma=False,
    )
```

```python
import functools

import jax
import jax.numpy as jnp
from jax import lax
from jax.experimental import pallas as pl
from jax.experimental.pallas import tpu as pltpu
from jax.sharding import PartitionSpec as P

D = 8192
HEAD_DIM = 128
EPSILON = 1e-06
FLOOR_SCORE = -1e30

TOK = 128
CH = 2048
POLES = 16
LANES = 128
CHUNKS = CH // LANES
GROUP = 16
HALF = GROUP * TOK
SPAN = 64
SCALE = HEAD_DIM ** (-0.5)
LOG2E = 1.4426950408889634

HALF_ROWS = POLES * 8
half_shape = (HALF_ROWS, LANES)
ROW_DOC, ROW_K, ROW_V, ROW_Q, ROW_G, ROWS_IN = 128, 144, 208, 272, 336, 400
OUT_RES, OUT_GAIN, OUT_Q, OUT_KV, ROWS_OUT = 16, 32, 48, 112, 240
BACK_SUM, BACK_GAIN, ROWS_BACK = 16, 32, 48

ROWS_TILE = 256
KEYS_TILE = 512
N_TILES = 2 * HALF // KEYS_TILE
HALF_TILES = N_TILES // 2
CHUNK = 256
STEP = 256
Q_TILES = 4

F32 = jnp.float32
BF16 = jnp.bfloat16


def call(kernel, outs, *args, scratch=(), smem=(), flops=0, nbytes=0, vmem=24 << 20, specs=None, far=()):
    grid = (1,) if specs else ()
    specs = specs or {}
    ins = [
        pl.BlockSpec(memory_space=pltpu.SMEM) if i in smem
        else specs.get(i, pl.BlockSpec(memory_space=pltpu.VMEM))
        for i in range(len(args))
    ]
    shapes = [jax.ShapeDtypeStruct(shape, kind) for shape, kind in outs]
    return pl.pallas_call(
        kernel,
        out_shape=shapes,
        grid=grid,
        in_specs=ins,
        out_specs=[
            pl.BlockSpec(memory_space=pltpu.HBM if i in far else pltpu.VMEM) for i in range(len(outs))
        ],
        scratch_shapes=list(scratch),
        cost_estimate=pl.CostEstimate(flops=flops, bytes_accessed=nbytes, transcendentals=0),
        compiler_params=pltpu.CompilerParams(vmem_limit_bytes=vmem),
    )(*args)


def every(start, size):
    return pl.ds(start, size, stride=CHUNKS)


def lanes(j):
    return slice(LANES * j, LANES * (j + 1))


def split(value):
    high = value.astype(BF16)
    return high, (value - high.astype(F32)).astype(BF16)


def scaling_of(rate):
    y = 2.0 * rate
    series = 1.0 - y / 6.0
    for k in (5.0, 4.0, 3.0, 2.0):
        series = 1.0 - y / k * series
    return jnp.sqrt(y * series)


def forward_groups(docs, step, state):
    def group(i, state):
        first = i * SPAN

        def plain(state):
            for u in range(SPAN):
                state = step(first + u, state)
            return state

        def cut(state):
            for u in range(SPAN):
                t = first + u
                keep = jnp.where(docs[t] == docs[jnp.maximum(t - 1, 0)], 1.0, 0.0)
                state = step(t, tuple(s * keep for s in state))
            return state

        whole = docs[jnp.maximum(first - 1, 0)] == docs[first + SPAN - 1]
        return lax.cond(whole, plain, cut, state)

    return lax.fori_loop(0, TOK // SPAN, group, state)


def backward_groups(docs, step, state, count):
    def group(i, state):
        first = TOK - SPAN - i * SPAN

        def plain(state):
            for u in reversed(range(SPAN)):
                state = step(first + u, state)
            return state

        def cut(state):
            for u in reversed(range(SPAN)):
                t = first + u
                keep = jnp.where(docs[t] == docs[jnp.minimum(t + 1, TOK - 1)], 1.0, 0.0)
                state = tuple(s * keep for s in state[:count]) + tuple(state[count:])
                state = step(t, state)
            return state

        whole = docs[first] == docs[jnp.minimum(first + SPAN, TOK - 1)]
        return lax.cond(whole, plain, cut, state)

    return lax.fori_loop(0, TOK // SPAN, group, state)


def split(value):
    high = value.astype(BF16)
    return high, (value - high.astype(F32)).astype(BF16)


def pair_rows(row):
    high, low = split(jnp.broadcast_to(row, (8, LANES)))
    return jnp.concatenate([high.astype(F32), low.astype(F32)], axis=0).astype(BF16)


def first_kernel(
    docs, doc_row, rate_hbm, res_hbm, hk_hbm, hv_hbm, ak_hbm, av_hbm, aq_hbm, ag_hbm,
    send, m_out, dec, wgt, through, rate_part,
    thr_all, rate, res, hk, hv, ak, av, aq, ag, m, sems,
):
    pairs = (
        (rate_hbm, rate), (res_hbm, res), (hk_hbm, hk), (hv_hbm, hv),
        (ak_hbm, ak), (av_hbm, av), (aq_hbm, aq), (ag_hbm, ag),
    )
    copies = [
        pltpu.make_async_copy(source, target, sems.at[i])
        for i, (source, target) in enumerate(pairs)
    ]
    for copy in copies:
        copy.start()
    ids = jnp.broadcast_to(doc_row[...].astype(F32), (16, LANES)).astype(BF16)
    for p in range(GROUP):
        send[p, ROW_DOC:ROW_K, :] = ids
    core = core_of()
    copies[0].wait()
    copies[1].wait()
    rates = rate[...]
    start = pl.multiple_of(chunk_of(position()) * LANES, LANES)
    rate_part[...] = rate[:, pl.ds(start, LANES)]
    decay = jnp.exp(-rates)
    weight = res[...] * scaling_of(rates)
    block = jnp.exp(-float(TOK) * rates)
    for j in range(CHUNKS):
        dec[every(j, POLES), :] = decay[:, lanes(j)]
        wgt[every(j, POLES), :] = weight[:, lanes(j)]
        thr_all[every(j, POLES), :] = block[:, lanes(j)]
    for n in range(POLES):
        at = pl.ds(pl.multiple_of(16 * n + 8 * core, 8), 8)
        through[8 * n : 8 * n + 8, :] = thr_all[at, :]
    copies[2].wait()
    copies[3].wait()
    for j in range(CHUNKS):
        m[every(j, TOK), :] = hk[:, lanes(j)].astype(F32) * hv[:, lanes(j)].astype(F32)
    leaving = pltpu.make_async_copy(m, m_out, sems.at[8])
    leaving.start()
    for g in range(2):
        kept = [dec[n * 16 + 8 * g : n * 16 + 8 * g + 8, :] for n in range(POLES)]

        def step(t, state):
            x = m[pl.ds(pl.multiple_of(t * 16 + 8 * g, 8), 8), :]
            return tuple(d * s + x for d, s in zip(kept, state))

        state = forward_groups(docs, step, (jnp.zeros((8, LANES), F32),) * POLES)
        pairs = [jnp.concatenate(state[n : n + 2], axis=0).astype(BF16) for n in range(0, POLES, 2)]
        for p in range(g, GROUP, 2):
            for i, pair in enumerate(pairs):
                send[p, 16 * i : 16 * i + 16, :] = pair
    for copy, row, ref in zip(copies[4:], (ROW_K, ROW_V, ROW_Q, ROW_G), (ak, av, aq, ag)):
        copy.wait()
        for p in range(GROUP):
            part = slice(64 * (p % 2), 64 * (p % 2) + 64)
            send[p, row : row + 64, :] = ref[part, lanes(p // 2)]
    leaving.wait()


def is_late():
    return lax.axis_index("ctx") >= GROUP


def block_at(b):
    return lax.rem(b + jnp.where(is_late(), 8, 0), GROUP)


def position():
    return block_at(lax.rem(lax.axis_index("ctx"), GROUP))


def core_of():
    return lax.rem(lax.axis_index("ctx"), 2)


def chunk_of(p):
    return 8 * (p % 2) + p // 2


def place_of(j):
    return 2 * (j % 8) + j // 8


def block_docs(got):
    rows = [got[block_at(b), ROW_DOC:ROW_K, :].astype(F32)[0:1] for b in range(GROUP)]
    return jnp.concatenate(rows, axis=0)


def spread(value, rows=POLES):
    return jnp.broadcast_to(value, (rows, LANES))


def flags_of(ids, rows=POLES):
    first, last = ids[:, 0:1], ids[:, LANES - 1 : LANES]
    same = [spread((first[b : b + 1] == last[b : b + 1]).astype(F32), rows) for b in range(GROUP)]
    join = [
        spread((last[b : b + 1] == first[b + 1 : b + 2]).astype(F32), rows) for b in range(GROUP - 1)
    ]
    return same, join


def half_state_kernel(got, through, out, local, ends, inside):
    ids = block_docs(got)
    same, join = flags_of(ids, HALF_ROWS)
    thr = through[...]
    state = jnp.zeros(half_shape, F32)
    reach = jnp.ones(half_shape, F32)
    turn = lax.rem(lax.axis_index("ctx"), GROUP)
    column = position() // 2
    for b in range(GROUP):
        inside[b, 0] = state
        inside[b, 1] = reach
        end = got[block_at(b), 0:HALF_ROWS, :].astype(F32)
        inside[b, 2] = end
        hold = same[b] * thr
        state = end + hold * state
        reach = hold * reach
        if b < GROUP - 1:
            state, reach = join[b] * state, join[b] * reach
    out[0:HALF_ROWS, :] = state
    out[HALF_ROWS:ROW_K, :] = ids
    partner = turn + 1 - 2 * core_of()
    local[0] = inside[turn, 0]
    local[1] = inside[turn, 1]
    local[2] = inside[partner, 0]
    local[3] = inside[partner, 1]
    for s in range(8):

        @pl.when(column == s)
        def _():
            for b in range(GROUP):
                ends[b] = inside[b, 2, pl.ds(s, POLES, stride=8), :]


def entry_kernel(local, mine, other, keep, send):
    late = jnp.where(is_late(), 1.0, 0.0)
    met = (other[ROW_K - 1 : ROW_K, LANES - 1 : LANES] == mine[HALF_ROWS : HALF_ROWS + 1, 0:1])
    carry = other[0:HALF_ROWS, :] * spread(met.astype(F32), HALF_ROWS) * late
    keep[...] = local[0] + local[1] * carry
    send[...] = local[2] + local[3] * carry


def keys_kernel(got, kv):
    kv[...] = got[:, ROW_K:ROW_Q, :]


def entry_states(keep, got, g):
    mine = core_of() == g
    return tuple(
        jnp.where(mine, keep[8 * n : 8 * n + 8, :], got[8 * n : 8 * n + 8, :]) for n in range(POLES)
    )


def forward_kernel(docs, keep, got, m, dec, wgt, hq, hg, gain, f, sums):
    for g in range(2):
        kept = [dec[n * 16 + 8 * g : n * 16 + 8 * g + 8, :] for n in range(POLES)]
        weights = [wgt[n * 16 + 8 * g : n * 16 + 8 * g + 8, :] for n in range(POLES)]

        def step(t, state):
            at = pl.ds(pl.multiple_of(t * 16 + 8 * g, 8), 8)
            x = m[at, :]
            state = tuple(d * s + x for d, s in zip(kept, state))
            terms = [w * s for w, s in zip(weights, state)]
            while len(terms) > 1:
                terms = [a + b for a, b in zip(terms[::2], terms[1::2])]
            f[at, :] = terms[0]
            return state

        forward_groups(docs, step, entry_states(keep, got, g))
    squares = jnp.zeros((TOK, LANES), F32)
    along = jnp.zeros((TOK, LANES), F32)
    for j in range(CHUNKS):
        out_y = hq[:, lanes(j)].astype(F32) * f[every(j, TOK), :]
        squares = squares + out_y * out_y
        along = along + hg[:, lanes(j)].astype(F32) * gain[:, lanes(j)] * out_y
    sums[0:1, :] = jnp.sum(squares.T, axis=0, keepdims=True)
    sums[1:2, :] = jnp.sum(along.T, axis=0, keepdims=True)
    sums[2:8, :] = jnp.zeros((6, LANES), F32)


def backward_kernel(docs, sums, after, f, m, dec, hq, hg, gain, ghq, gf, send, starts, totals):
    total = sums[...]
    inv = lax.rsqrt(total[0:1, :] / D + EPSILON)
    slope = inv * inv * inv * total[1:2, :] / D
    inv = jnp.broadcast_to(inv, (TOK, LANES)).T
    slope = jnp.broadcast_to(slope, (TOK, LANES)).T
    for j in range(CHUNKS):
        q = hq[:, lanes(j)].astype(F32)
        back = hg[:, lanes(j)].astype(F32)
        row = f[every(j, TOK), :]
        out_y = q * row
        grad_y = inv * (back * gain[:, lanes(j)]) - out_y * slope
        ghq[:, lanes(j)] = (grad_y * row).astype(BF16)
        gf[every(j, TOK), :] = grad_y * q
        gain_part = jnp.sum(back * out_y * inv, axis=0, keepdims=True)
        send[place_of(j), BACK_GAIN:ROWS_BACK, :] = pair_rows(gain_part)
    for g in range(2):
        kept = [dec[n * 16 + 8 * g : n * 16 + 8 * g + 8, :] for n in range(POLES)]

        def step(t, carry):
            at = pl.ds(pl.multiple_of(t * 16 + 8 * g, 8), 8)
            x, feed = gf[at, :], m[at, :]
            state = tuple(d * s + x for d, s in zip(kept, carry[:POLES]))
            return state + tuple(k + feed * s for k, s in zip(carry[POLES:], state))

        zero = (jnp.zeros((8, LANES), F32),) * (2 * POLES)
        carry = backward_groups(docs, step, zero, POLES)
        for n in range(POLES):
            starts[n * 16 + 8 * g : n * 16 + 8 * g + 8, :] = carry[n]
            totals[n * 16 + 8 * g : n * 16 + 8 * g + 8, :] = carry[POLES + n]
    for p in range(GROUP):
        send[p, 0:16, :] = starts[every(chunk_of(p), POLES), :].astype(BF16)
        send[p, BACK_SUM:BACK_GAIN, :] = totals[every(chunk_of(p), POLES), :].astype(BF16)


def half_adjoint_kernel(docs_mine, ends, back, rate, docs_other, out):
    ids, other = docs_mine[HALF_ROWS:ROW_K, :], docs_other[HALF_ROWS:ROW_K, :]
    same, join = flags_of(ids)
    rates = rate[...]
    through = jnp.exp(-float(TOK) * rates)
    decay = jnp.exp(-rates)
    early = jnp.where(is_late(), 0.0, 1.0)
    met = spread((other[0:1, 0:1] == ids[15:16, LANES - 1 : LANES]).astype(F32)) * early
    total = jnp.zeros((POLES, LANES), F32)
    reach = jnp.zeros((POLES, LANES), F32)
    gains = jnp.zeros((8, LANES), F32)
    carry = jnp.zeros((POLES, LANES), F32)
    unit = met
    for b in reversed(range(GROUP)):
        end = decay * ends[b]
        total = total + back[block_at(b), BACK_SUM:BACK_GAIN, :].astype(F32) + end * carry
        reach = reach + end * unit
        pair = back[block_at(b), BACK_GAIN:ROWS_BACK, :].astype(F32)
        gains = gains + pair[0:8] + pair[8:16]
        carry = back[block_at(b), 0:16, :].astype(F32) + same[b] * through * carry
        unit = same[b] * through * unit
        if b > 0:
            carry = join[b - 1] * carry
            unit = join[b - 1] * unit
    out[0:16, :] = carry
    out[16:32, :] = total
    out[32:48, :] = reach
    out[48:56, :] = gains


def last_pack_kernel(
    docs_mine, back, rate, docs_other, mine, theirs, dq, own, own_got, prev_got, send
):
    ids, other = docs_mine[HALF_ROWS:ROW_K, :], docs_other[HALF_ROWS:ROW_K, :]
    same, join = flags_of(ids)
    rates = rate[...]
    through = jnp.exp(-float(TOK) * rates)
    early = jnp.where(is_late(), 0.0, 1.0)
    met = spread((other[0:1, 0:1] == ids[15:16, LANES - 1 : LANES]).astype(F32)) * early
    late_start = mine[0:16, :] * (1.0 - early) + theirs[0:16, :] * early
    early_reach = mine[32:48, :] * early + theirs[32:48, :] * (1.0 - early)
    residue = mine[16:32, :] + theirs[16:32, :] + late_start * early_reach
    residue = (scaling_of(rates) * residue).astype(BF16)
    pair = pair_rows((mine[48:56, :] + theirs[48:56, :])[0:1])
    carry = theirs[0:16, :] * met
    for b in reversed(range(GROUP)):
        at = block_at(b)
        send[at, 0:OUT_RES, :] = carry.astype(BF16)
        send[at, OUT_RES:OUT_GAIN, :] = residue
        send[at, OUT_GAIN:OUT_Q, :] = pair
        send[at, OUT_Q:OUT_KV, :] = dq[at]
        kv = own[at].astype(F32) + own_got[at].astype(F32) + prev_got[at].astype(F32) * early
        send[at, OUT_KV:ROWS_OUT, :] = kv.astype(BF16)
        if b > 0:
            carry = join[b - 1] * (back[at, 0:16, :].astype(F32) + same[b] * through * carry)


def final_kernel(
    docs, got, gf, dec, wgt, hk, hv, ghk, ghv, gres, ggain, gaq, gak, gav, gm, entry
):
    for p in range(GROUP):
        j = chunk_of(p)
        entry[16 * j : 16 * j + 16, :] = got[p, 0:OUT_RES, :].astype(F32)
        gres[:, lanes(j)] = got[p, OUT_RES:OUT_GAIN, :].astype(F32)
        pair = got[p, OUT_GAIN:OUT_Q, :].astype(F32)
        ggain[:, lanes(j)] = pair[0:1] + pair[8:9]
        rows = slice(64 * (p % 2), 64 * (p % 2) + 64)
        gaq[rows, lanes(p // 2)] = got[p, OUT_Q:OUT_KV, :]
        gak[rows, lanes(p // 2)] = got[p, OUT_KV : OUT_KV + 64, :]
        gav[rows, lanes(p // 2)] = got[p, OUT_KV + 64 : ROWS_OUT, :]
    for g in range(2):
        kept = [dec[n * 16 + 8 * g : n * 16 + 8 * g + 8, :] for n in range(POLES)]
        weights = [wgt[n * 16 + 8 * g : n * 16 + 8 * g + 8, :] for n in range(POLES)]

        def step(t, state):
            at = pl.ds(pl.multiple_of(t * 16 + 8 * g, 8), 8)
            x = gf[at, :]
            state = tuple(d * s + x for d, s in zip(kept, state))
            terms = [w * s for w, s in zip(weights, state)]
            while len(terms) > 1:
                terms = [a + b for a, b in zip(terms[::2], terms[1::2])]
            gm[at, :] = terms[0]
            return state

        start = tuple(entry[every(8 * g * 16 + n, 8), :] for n in range(POLES))
        backward_groups(docs, step, start, POLES)
    for j in range(CHUNKS):
        row = gm[every(j, TOK), :]
        ghk[:, lanes(j)] = (row * hv[:, lanes(j)].astype(F32)).astype(BF16)
        ghv[:, lanes(j)] = (row * hk[:, lanes(j)].astype(F32)).astype(BF16)


def place(keys, values, b, at_core, key_rows, value_rows):
    at = pl.ds(pl.multiple_of(TOK * b + 64 * at_core, 64), 64)
    keys[at, :] = key_rows
    values[at, :] = value_rows


def turn_keys(keys, turned):
    def one(t, _):
        at = pl.ds(pl.multiple_of(t * KEYS_TILE, KEYS_TILE), KEYS_TILE)
        turned[t] = keys[at, :].astype(F32).T.astype(BF16)
        return 0

    lax.fori_loop(0, HALF_TILES, one, 0)


def own_keys_kernel(got, kv, kv_core, keys, values, turned, rows_q, rows_g, turned_q, turned_g):
    core = core_of()
    for i in range(Q_TILES):
        for u in range(4):
            part = slice(64 * u, 64 * u + 64)
            rows_q[i, part, :] = got[block_at(4 * i + u), ROW_Q:ROW_G, :]
            rows_g[i, part, :] = got[block_at(4 * i + u), ROW_G:ROWS_IN, :]
        turned_q[i] = rows_q[i].astype(F32).T.astype(BF16)
        turned_g[i] = rows_g[i].astype(F32).T.astype(BF16)
    for b in range(GROUP):
        s = block_at(b)
        place(keys, values, b, core, kv[s, 0:64, :], kv[s, 64:128, :])
        place(keys, values, b, 1 - core, kv_core[s, 0:64, :], kv_core[s, 64:128, :])
    turn_keys(keys, turned)


def sums_kernel(s0, s1, s2, s3, total):
    total[...] = s0[...] + s1[...] + s2[...] + s3[...]


def send_keys_kernel(kv, after, out):
    out[...] = kv[...]


def attention_kernel(
    all_q, all_g, all_turned_q, all_turned_g, own_k, own_v, own_turned, kv_half, kv_half_core,
    ids_mine, ids_other, after,
    dq, own, own_send, prev, prev_send, token,
    prev_k, prev_v, prev_turned, scores, products, peaks, dk, dv,
):
    core = core_of()
    late = is_late()
    token[...] = jnp.zeros((8, LANES), F32)

    @pl.when(late)
    def _():
        for b in range(GROUP):
            place(prev_k, prev_v, b, core, kv_half[b, 0:64, :], kv_half[b, 64:128, :])
            place(
                prev_k, prev_v, b, 1 - core, kv_half_core[b, 0:64, :], kv_half_core[b, 64:128, :]
            )
        turn_keys(prev_k, prev_turned)

    def clear(t, _):
        at = pl.ds(pl.multiple_of(t * KEYS_TILE, KEYS_TILE), KEYS_TILE)
        dk[at, :] = jnp.zeros((KEYS_TILE, HEAD_DIM), F32)
        dv[at, :] = jnp.zeros((KEYS_TILE, HEAD_DIM), F32)
        return 0

    lax.fori_loop(jnp.where(late, 0, HALF_TILES), N_TILES, clear, 0)

    own_ids, other_ids = ids_mine[HALF_ROWS:ROW_K, :], ids_other[HALF_ROWS:ROW_K, :]
    base = jnp.where(late, 0, HALF)
    starts = []
    for d in (1, 2, 3):
        before = jnp.sum((own_ids < d).astype(F32)).astype(jnp.int32)
        behind = jnp.sum((other_ids < d).astype(F32)).astype(jnp.int32)
        starts.append(before + jnp.where(late, behind, HALF))

    def start_of(pos):
        result = jnp.where(pos >= starts[0], starts[0], base)
        for start in starts[1:]:
            result = jnp.where(pos >= start, start, result)
        return result

    def query_tile(i, _):
        rows_q, rows_g = all_q[i], all_g[i]
        turned_q, turned_g = all_turned_q[i], all_turned_g[i]
        lane = lax.broadcasted_iota(jnp.int32, (1, ROWS_TILE), 1)
        qpos = HALF + 512 * i + 128 * (lane // 64) + 64 * core + lax.rem(lane, 64)
        qstart = start_of(qpos)
        low = start_of(HALF + 512 * i + 64 * core) // KEYS_TILE
        high = HALF // KEYS_TILE + i + 1
        row = lax.broadcasted_iota(jnp.int32, (CHUNK, ROWS_TILE), 0)

        def fold(value, by):
            return by(value.reshape(CHUNK // 8, 8, ROWS_TILE), axis=0)

        def first_pass(keys, values, base, t, carry):
            peak, total, weighted = carry
            for u in range(KEYS_TILE // CHUNK):
                first = t * KEYS_TILE + u * CHUNK
                at = pl.ds(pl.multiple_of(first - base * KEYS_TILE, CHUNK), CHUNK)
                s = jnp.dot(keys[at, :], turned_q, preferred_element_type=F32)
                gp = jnp.dot(values[at, :], turned_g, preferred_element_type=F32)
                s = jnp.where((row <= qpos - first) & (row >= qstart - first), s, FLOOR_SCORE)
                top = jnp.maximum(peak, jnp.max(fold(s, jnp.max), axis=0, keepdims=True))
                p = jnp.exp2((s - top) * (SCALE * LOG2E))
                scores[t, u * CHUNK : u * CHUNK + CHUNK, :] = p
                products[t, u * CHUNK : u * CHUNK + CHUNK, :] = gp
                peaks[t, u : u + 1, :] = top
                shrink = jnp.exp2((peak - top) * (SCALE * LOG2E))
                total = total * shrink + fold(p, jnp.sum)
                weighted = weighted * shrink + fold(p * gp, jnp.sum)
                peak = top
            return peak, total, weighted

        zero = jnp.zeros((8, ROWS_TILE), F32)
        floor = jnp.full((1, ROWS_TILE), FLOOR_SCORE, F32)
        ahead = functools.partial(first_pass, prev_k, prev_v, 0)
        carry = lax.fori_loop(low, HALF_TILES, ahead, (floor, zero, zero))
        within = functools.partial(first_pass, own_k, own_v, HALF_TILES)
        middle = jnp.maximum(low, HALF_TILES)
        peak, total, weighted = lax.fori_loop(middle, high, within, carry)
        inv = 1.0 / jnp.sum(total, axis=0, keepdims=True)
        centre = jnp.sum(weighted, axis=0, keepdims=True) * inv

        def second_pass(turned, base, t, turned_dq):
            for v in range(KEYS_TILE // STEP):
                parts = []
                for u in range(v * STEP // CHUNK, (v + 1) * STEP // CHUNK):
                    rows = slice(u * CHUNK, u * CHUNK + CHUNK)
                    fall = jnp.exp2((peaks[t, u : u + 1, :] - peak) * (SCALE * LOG2E)) * inv
                    p = scores[t, rows, :] * fall
                    parts.append((p.astype(BF16), (p * (products[t, rows, :] - centre)).astype(BF16)))
                p = jnp.concatenate([one for one, _ in parts], axis=0)
                ds = jnp.concatenate([one for _, one in parts], axis=0)
                at = pl.ds(pl.multiple_of(t * KEYS_TILE + v * STEP, STEP), STEP)
                dk[at, :] += jnp.dot(ds, rows_q, preferred_element_type=F32)
                dv[at, :] += jnp.dot(p, rows_g, preferred_element_type=F32)
                part = turned[t - base, :, v * STEP : v * STEP + STEP]
                turned_dq = turned_dq + jnp.dot(part, ds, preferred_element_type=F32)
            return turned_dq

        zero = jnp.zeros((HEAD_DIM, ROWS_TILE), F32)
        ahead = functools.partial(second_pass, prev_turned, 0)
        turned_dq = lax.fori_loop(low, HALF_TILES, ahead, zero)
        within = functools.partial(second_pass, own_turned, HALF_TILES)
        turned_dq = lax.fori_loop(middle, high, within, turned_dq)
        rows = (turned_dq * SCALE).T.astype(BF16)
        for u in range(4):
            dq[block_at(4 * i + u)] = rows[64 * u : 64 * u + 64]
        return 0

    lax.fori_loop(0, Q_TILES, query_tile, 0)

    def leave(base, target, target_send, order):
        for b in range(GROUP):
            s = order(b)
            for at_core, ref in ((core, target), (1 - core, target_send)):
                at = pl.ds(pl.multiple_of(base + TOK * b + 64 * at_core, 64), 64)
                ref[s, 0:64, :] = (dk[at, :] * SCALE).astype(BF16)
                ref[s, 64:128, :] = dv[at, :].astype(BF16)

    leave(HALF, own, own_send, block_at)

    @pl.when(late)
    def _():
        leave(0, prev, prev_send, lambda b: b)

    @pl.when(jnp.logical_not(late))
    def _():
        prev[...] = jnp.zeros(prev.shape, BF16)
        prev_send[...] = jnp.zeros(prev_send.shape, BF16)


def body(
    hyena_q, hyena_k, hyena_v, hyena_grad, pole_rate, residue, norm_gain, doc_ids,
    attn_q, attn_k, attn_v, attn_grad,
):
    count = 2 * GROUP
    early = list(range(GROUP))
    late = [GROUP + (p ^ 8) for p in early]
    swap_core = [(i, i ^ 1) for i in range(count)]
    up_half = list(zip(early, late))
    down_half = list(zip(late, early))
    swap_half = up_half + down_half

    def exchange(x):
        return lax.all_to_all(x, "ctx", 0, 0, tiled=True, axis_index_groups=[early, late])

    gain = norm_gain.reshape(1, CH)
    sweep = (TOK * CHUNKS, LANES)
    params = (POLES * CHUNKS, LANES)
    vmem = pltpu.VMEM
    hbm = pl.BlockSpec(memory_space=pltpu.HBM)
    send, m, dec, wgt, through, rate_part = call(
        first_kernel,
        [((GROUP, ROWS_IN, LANES), BF16), (sweep, F32), (params, F32), (params, F32)]
        + [(half_shape, F32), ((POLES, LANES), F32)],
        doc_ids, doc_ids.reshape(1, TOK), pole_rate, residue, hyena_k, hyena_v,
        attn_k, attn_v, attn_q, attn_grad,
        smem=(0,), specs={i: hbm for i in range(2, 10)}, far=(1,),
        scratch=[vmem(params, F32)] + [vmem((POLES, CH), F32)] * 2 + [vmem((TOK, CH), BF16)] * 2
        + [vmem((TOK, 1024), BF16)] * 4 + [vmem(sweep, F32), pltpu.SemaphoreType.DMA((9,))],
        flops=40_000_000, nbytes=6_000_000, vmem=60 << 20,
    )
    got = exchange(send)
    mine, local, ends = call(
        half_state_kernel,
        [((ROW_K, LANES), F32), ((4,) + half_shape, F32), ((GROUP, POLES, LANES), F32)],
        got, through, scratch=[vmem((GROUP, 3) + half_shape, F32)],
        flops=1_000_000, nbytes=300_000,
    )
    other = lax.ppermute(mine, "ctx", swap_half)
    part = (GROUP, TOK, HEAD_DIM)
    (kv,) = call(keys_kernel, [(part, BF16)], got, flops=1000, nbytes=1_000_000)
    kv_core = lax.ppermute(kv, "ctx", swap_core)
    (kv_later,) = call(
        send_keys_kernel, [(part, BF16)], kv, other, flops=1000, nbytes=1_000_000
    )
    kv_half = lax.ppermute(kv_later, "ctx", up_half)
    flat = (HALF, HEAD_DIM)
    turned = (HALF_TILES, HEAD_DIM, KEYS_TILE)
    tall, wide = (Q_TILES, ROWS_TILE, HEAD_DIM), (Q_TILES, HEAD_DIM, ROWS_TILE)
    own_k, own_v, own_turned, *query_parts = call(
        own_keys_kernel,
        [(flat, BF16), (flat, BF16), (turned, BF16)] + [(tall, BF16)] * 2 + [(wide, BF16)] * 2,
        got, kv, kv_core,
        flops=1_000_000, nbytes=4_000_000,
    )
    carry, carry_send = call(
        entry_kernel, [(half_shape, F32)] * 2, local, mine, other, flops=100_000, nbytes=300_000
    )
    carry_got = lax.ppermute(carry_send, "ctx", swap_core)
    f, sums = call(
        forward_kernel, [(sweep, F32), ((8, LANES), F32)],
        doc_ids, carry, carry_got, m, dec, wgt, hyena_q, hyena_grad, gain,
        smem=(0,), flops=40_000_000, nbytes=6_000_000,
    )
    shared = [
        lax.ppermute(sums, "chan", [(i, (i + k) % 4) for i in range(4)]) for k in (1, 2, 3)
    ]
    (sums,) = call(
        sums_kernel, [((8, LANES), F32)], sums, *shared, flops=1000, nbytes=10_000
    )
    (kv_half,) = call(
        send_keys_kernel, [(part, BF16)], kv_half, sums, flops=1000, nbytes=1_000_000
    )
    kv_half_core = lax.ppermute(kv_half, "ctx", swap_core)
    dq, own, own_send, prev, prev_send, after = call(
        attention_kernel,
        [((GROUP, 64, HEAD_DIM), BF16)] + [(part, BF16)] * 4 + [((8, LANES), F32)],
        *query_parts, own_k, own_v, own_turned, kv_half, kv_half_core, mine, other, sums,
        scratch=[
            vmem(flat, BF16),
            vmem(flat, BF16),
            vmem(turned, BF16),
            vmem((N_TILES, KEYS_TILE, ROWS_TILE), F32),
            vmem((N_TILES, KEYS_TILE, ROWS_TILE), F32),
            vmem((N_TILES, 8, ROWS_TILE), F32),
            vmem((2 * HALF, HEAD_DIM), F32),
            vmem((2 * HALF, HEAD_DIM), F32),
        ],
        flops=10_000_000_000, nbytes=6_000_000, vmem=28 << 20,
    )
    ghq, gf, back_send = call(
        backward_kernel,
        [((TOK, CH), BF16), (sweep, F32), ((GROUP, ROWS_BACK, LANES), BF16)],
        doc_ids, sums, after, f, m, dec, hyena_q, hyena_grad, gain,
        smem=(0,), scratch=[vmem(params, F32), vmem(params, F32)],
        flops=40_000_000, nbytes=6_000_000,
    )
    prev_got = lax.ppermute(prev_send, "ctx", swap_core)
    own_got = lax.ppermute(own_send, "ctx", swap_core)
    back_send, prev_got = lax.optimization_barrier((back_send, prev_got))
    prev_sum = (prev.astype(F32) + prev_got.astype(F32)).astype(BF16)
    prev_home = lax.ppermute(prev_sum, "ctx", down_half)
    back = exchange(back_send)
    (half_mine,) = call(
        half_adjoint_kernel, [((56, LANES), F32)], mine, ends, back, rate_part, other,
        flops=1_000_000, nbytes=300_000,
    )
    half_other = lax.ppermute(half_mine, "ctx", swap_half)
    (last_send,) = call(
        last_pack_kernel, [((GROUP, ROWS_OUT, LANES), BF16)],
        mine, back, rate_part, other, half_mine, half_other, dq, own, own_got, prev_home,
        flops=1_000_000, nbytes=3_000_000,
    )
    last = exchange(last_send)
    ghk, ghv, gres, ggain, gaq, gak, gav = call(
        final_kernel,
        [((TOK, CH), BF16), ((TOK, CH), BF16), ((POLES, CH), F32), ((1, CH), F32)]
        + [((TOK, 1024), BF16)] * 3,
        doc_ids, last, gf, dec, wgt, hyena_k, hyena_v,
        smem=(0,), scratch=[vmem(sweep, F32), vmem(params, F32)],
        flops=40_000_000, nbytes=6_000_000,
    )
    return (ghq, ghk, ghv, gres, ggain.reshape(CH), gaq, gak, gav)


def solution(mesh):
    wide, deep, one = P("ctx", "chan"), P(None, "chan"), P("chan")
    return jax.shard_map(
        body,
        mesh=mesh,
        in_specs=(wide,) * 4 + (deep, deep, one, P("ctx")) + (wide,) * 4,
        out_specs=(wide, wide, wide, deep, one, wide, wide, wide),
        check_vma=False,
    )
```

```python
import functools

import jax
import jax.numpy as jnp
from jax import lax
from jax.experimental import pallas as pl
from jax.experimental.pallas import tpu as pltpu
from jax.sharding import PartitionSpec as P

D = 8192
HEAD_DIM = 128
EPSILON = 1e-06
FLOOR_SCORE = -1e30

TOK = 128
CH = 2048
POLES = 16
LANES = 128
CHUNKS = CH // LANES
GROUP = 16
HALF = GROUP * TOK
SPAN = 64
SCALE = HEAD_DIM ** (-0.5)
LOG2E = 1.4426950408889634

HALF_ROWS = POLES * 8
half_shape = (HALF_ROWS, LANES)
ROW_DOC, ROW_K, ROW_V, ROW_Q, ROW_G, ROWS_IN = 128, 144, 208, 272, 336, 400
OUT_RES, OUT_GAIN, OUT_Q, OUT_KV, ROWS_OUT = 16, 32, 48, 112, 240
BACK_SUM, BACK_GAIN, ROWS_BACK = 16, 32, 48

ROWS_TILE = 256
KEYS_TILE = 512
N_TILES = 2 * HALF // KEYS_TILE
HALF_TILES = N_TILES // 2
CHUNK = 256
STEP = 256
Q_TILES = 4

F32 = jnp.float32
BF16 = jnp.bfloat16


def call(kernel, outs, *args, scratch=(), smem=(), flops=0, nbytes=0, vmem=24 << 20, specs=None, far=()):
    grid = (1,) if specs else ()
    specs = specs or {}
    ins = [
        pl.BlockSpec(memory_space=pltpu.SMEM) if i in smem
        else specs.get(i, pl.BlockSpec(memory_space=pltpu.VMEM))
        for i in range(len(args))
    ]
    shapes = [jax.ShapeDtypeStruct(shape, kind) for shape, kind in outs]
    return pl.pallas_call(
        kernel,
        out_shape=shapes,
        grid=grid,
        in_specs=ins,
        out_specs=[
            pl.BlockSpec(memory_space=pltpu.HBM if i in far else pltpu.VMEM) for i in range(len(outs))
        ],
        scratch_shapes=list(scratch),
        cost_estimate=pl.CostEstimate(flops=flops, bytes_accessed=nbytes, transcendentals=0),
        compiler_params=pltpu.CompilerParams(vmem_limit_bytes=vmem),
    )(*args)


def every(start, size):
    return pl.ds(start, size, stride=CHUNKS)


def lanes(j):
    return slice(LANES * j, LANES * (j + 1))


def split(value):
    high = value.astype(BF16)
    return high, (value - high.astype(F32)).astype(BF16)


def scaling_of(rate):
    y = 2.0 * rate
    series = 1.0 - y / 6.0
    for k in (5.0, 4.0, 3.0, 2.0):
        series = 1.0 - y / k * series
    return jnp.sqrt(y * series)


def forward_groups(docs, step, state):
    def group(i, state):
        first = i * SPAN

        def plain(state):
            for u in range(SPAN):
                state = step(first + u, state)
            return state

        def cut(state):
            for u in range(SPAN):
                t = first + u
                keep = jnp.where(docs[t] == docs[jnp.maximum(t - 1, 0)], 1.0, 0.0)
                state = step(t, tuple(s * keep for s in state))
            return state

        whole = docs[jnp.maximum(first - 1, 0)] == docs[first + SPAN - 1]
        return lax.cond(whole, plain, cut, state)

    return lax.fori_loop(0, TOK // SPAN, group, state)


def backward_groups(docs, step, state, count):
    def group(i, state):
        first = TOK - SPAN - i * SPAN

        def plain(state):
            for u in reversed(range(SPAN)):
                state = step(first + u, state)
            return state

        def cut(state):
            for u in reversed(range(SPAN)):
                t = first + u
                keep = jnp.where(docs[t] == docs[jnp.minimum(t + 1, TOK - 1)], 1.0, 0.0)
                state = tuple(s * keep for s in state[:count]) + tuple(state[count:])
                state = step(t, state)
            return state

        whole = docs[first] == docs[jnp.minimum(first + SPAN, TOK - 1)]
        return lax.cond(whole, plain, cut, state)

    return lax.fori_loop(0, TOK // SPAN, group, state)


def split(value):
    high = value.astype(BF16)
    return high, (value - high.astype(F32)).astype(BF16)


def pair_rows(row):
    high, low = split(jnp.broadcast_to(row, (8, LANES)))
    return jnp.concatenate([high.astype(F32), low.astype(F32)], axis=0).astype(BF16)


def first_kernel(
    docs, doc_row, rate_hbm, res_hbm, hk_hbm, hv_hbm, ak_hbm, av_hbm, aq_hbm, ag_hbm,
    send, m_out, dec, wgt, through, rate_part,
    thr_all, rate, res, hk, hv, ak, av, aq, ag, m, states, heads, sems,
):
    pairs = (
        (rate_hbm, rate), (res_hbm, res), (hk_hbm, hk), (hv_hbm, hv),
        (ak_hbm, ak), (av_hbm, av), (aq_hbm, aq), (ag_hbm, ag),
    )
    copies = [
        pltpu.make_async_copy(source, target, sems.at[i])
        for i, (source, target) in enumerate(pairs)
    ]
    for copy in copies:
        copy.start()
    ids = jnp.broadcast_to(doc_row[...].astype(F32), (16, LANES)).astype(BF16)
    for p in range(GROUP):
        heads[p, 0 : ROW_K - ROW_DOC, :] = ids
    core = core_of()
    copies[0].wait()
    copies[1].wait()
    rates = rate[...]
    start = pl.multiple_of(chunk_of(position()) * LANES, LANES)
    rate_part[...] = rate[:, pl.ds(start, LANES)]
    decay = jnp.exp(-rates)
    weight = res[...] * scaling_of(rates)
    block = jnp.exp(-float(TOK) * rates)
    for j in range(CHUNKS):
        dec[every(j, POLES), :] = decay[:, lanes(j)]
        wgt[every(j, POLES), :] = weight[:, lanes(j)]
        thr_all[every(j, POLES), :] = block[:, lanes(j)]
    for n in range(POLES):
        at = pl.ds(pl.multiple_of(16 * n + 8 * core, 8), 8)
        through[8 * n : 8 * n + 8, :] = thr_all[at, :]
    copies[2].wait()
    copies[3].wait()
    for j in range(CHUNKS):
        m[every(j, TOK), :] = hk[:, lanes(j)].astype(F32) * hv[:, lanes(j)].astype(F32)
    leaving = [pltpu.make_async_copy(m, m_out, sems.at[8])]
    leaving[0].start()
    for copy, row, ref in zip(copies[4:], (ROW_K, ROW_V, ROW_Q, ROW_G), (ak, av, aq, ag)):
        copy.wait()
        at = row - ROW_DOC
        for p in range(GROUP):
            part = slice(64 * (p % 2), 64 * (p % 2) + 64)
            heads[p, at : at + 64, :] = ref[part, lanes(p // 2)]
    leaving.append(pltpu.make_async_copy(heads, send.at[:, ROW_DOC:ROWS_IN, :], sems.at[9]))
    leaving[1].start()
    for g in range(2):
        kept = [dec[n * 16 + 8 * g : n * 16 + 8 * g + 8, :] for n in range(POLES)]

        def step(t, state):
            x = m[pl.ds(pl.multiple_of(t * 16 + 8 * g, 8), 8), :]
            return tuple(d * s + x for d, s in zip(kept, state))

        state = forward_groups(docs, step, (jnp.zeros((8, LANES), F32),) * POLES)
        pairs = [jnp.concatenate(state[n : n + 2], axis=0).astype(BF16) for n in range(0, POLES, 2)]
        for p in range(g, GROUP, 2):
            for i, pair in enumerate(pairs):
                states[p, 16 * i : 16 * i + 16, :] = pair
    leaving.append(pltpu.make_async_copy(states, send.at[:, 0:ROW_DOC, :], sems.at[10]))
    leaving[2].start()
    for copy in leaving:
        copy.wait()


def is_late():
    return lax.axis_index("ctx") >= GROUP


def block_at(b):
    return lax.rem(b + jnp.where(is_late(), 8, 0), GROUP)


def position():
    return block_at(lax.rem(lax.axis_index("ctx"), GROUP))


def core_of():
    return lax.rem(lax.axis_index("ctx"), 2)


def chunk_of(p):
    return 8 * (p % 2) + p // 2


def place_of(j):
    return 2 * (j % 8) + j // 8


def block_docs(got):
    rows = [got[block_at(b), ROW_DOC:ROW_K, :].astype(F32)[0:1] for b in range(GROUP)]
    return jnp.concatenate(rows, axis=0)


def spread(value, rows=POLES):
    return jnp.broadcast_to(value, (rows, LANES))


def flags_of(ids, rows=POLES):
    first, last = ids[:, 0:1], ids[:, LANES - 1 : LANES]
    same = [spread((first[b : b + 1] == last[b : b + 1]).astype(F32), rows) for b in range(GROUP)]
    join = [
        spread((last[b : b + 1] == first[b + 1 : b + 2]).astype(F32), rows) for b in range(GROUP - 1)
    ]
    return same, join


def half_state_kernel(got, through, out, local, ends, inside):
    ids = block_docs(got)
    same, join = flags_of(ids, HALF_ROWS)
    thr = through[...]
    state = jnp.zeros(half_shape, F32)
    reach = jnp.ones(half_shape, F32)
    turn = lax.rem(lax.axis_index("ctx"), GROUP)
    column = position() // 2
    for b in range(GROUP):
        inside[b, 0] = state
        inside[b, 1] = reach
        end = got[block_at(b), 0:HALF_ROWS, :].astype(F32)
        inside[b, 2] = end
        hold = same[b] * thr
        state = end + hold * state
        reach = hold * reach
        if b < GROUP - 1:
            state, reach = join[b] * state, join[b] * reach
    out[0:HALF_ROWS, :] = state
    out[HALF_ROWS:ROW_K, :] = ids
    partner = turn + 1 - 2 * core_of()
    local[0] = inside[turn, 0]
    local[1] = inside[turn, 1]
    local[2] = inside[partner, 0]
    local[3] = inside[partner, 1]
    for s in range(8):

        @pl.when(column == s)
        def _():
            for b in range(GROUP):
                ends[b] = inside[b, 2, pl.ds(s, POLES, stride=8), :]


def entry_kernel(local, mine, other, keep, send):
    late = jnp.where(is_late(), 1.0, 0.0)
    met = (other[ROW_K - 1 : ROW_K, LANES - 1 : LANES] == mine[HALF_ROWS : HALF_ROWS + 1, 0:1])
    carry = other[0:HALF_ROWS, :] * spread(met.astype(F32), HALF_ROWS) * late
    keep[...] = local[0] + local[1] * carry
    send[...] = local[2] + local[3] * carry


def keys_kernel(got, kv):
    kv[...] = got[:, ROW_K:ROW_Q, :]


def entry_states(keep, got, g):
    mine = core_of() == g
    return tuple(
        jnp.where(mine, keep[8 * n : 8 * n + 8, :], got[8 * n : 8 * n + 8, :]) for n in range(POLES)
    )


def forward_kernel(docs, keep, got, m, dec, wgt, hq, hg, gain, f, sums):
    for g in range(2):
        kept = [dec[n * 16 + 8 * g : n * 16 + 8 * g + 8, :] for n in range(POLES)]
        weights = [wgt[n * 16 + 8 * g : n * 16 + 8 * g + 8, :] for n in range(POLES)]

        def step(t, state):
            at = pl.ds(pl.multiple_of(t * 16 + 8 * g, 8), 8)
            x = m[at, :]
            state = tuple(d * s + x for d, s in zip(kept, state))
            terms = [w * s for w, s in zip(weights, state)]
            while len(terms) > 1:
                terms = [a + b for a, b in zip(terms[::2], terms[1::2])]
            f[at, :] = terms[0]
            return state

        forward_groups(docs, step, entry_states(keep, got, g))
    squares = jnp.zeros((TOK, LANES), F32)
    along = jnp.zeros((TOK, LANES), F32)
    for j in range(CHUNKS):
        out_y = hq[:, lanes(j)].astype(F32) * f[every(j, TOK), :]
        squares = squares + out_y * out_y
        along = along + hg[:, lanes(j)].astype(F32) * gain[:, lanes(j)] * out_y
    sums[0:1, :] = jnp.sum(squares.T, axis=0, keepdims=True)
    sums[1:2, :] = jnp.sum(along.T, axis=0, keepdims=True)
    sums[2:8, :] = jnp.zeros((6, LANES), F32)


def backward_kernel(docs, sums, after, f, m, dec, hq, hg, gain, ghq, gf, send, starts, totals):
    total = sums[...]
    inv = lax.rsqrt(total[0:1, :] / D + EPSILON)
    slope = inv * inv * inv * total[1:2, :] / D
    inv = jnp.broadcast_to(inv, (TOK, LANES)).T
    slope = jnp.broadcast_to(slope, (TOK, LANES)).T
    for j in range(CHUNKS):
        q = hq[:, lanes(j)].astype(F32)
        back = hg[:, lanes(j)].astype(F32)
        row = f[every(j, TOK), :]
        out_y = q * row
        grad_y = inv * (back * gain[:, lanes(j)]) - out_y * slope
        ghq[:, lanes(j)] = (grad_y * row).astype(BF16)
        gf[every(j, TOK), :] = grad_y * q
        gain_part = jnp.sum(back * out_y * inv, axis=0, keepdims=True)
        send[place_of(j), BACK_GAIN:ROWS_BACK, :] = pair_rows(gain_part)
    for g in range(2):
        kept = [dec[n * 16 + 8 * g : n * 16 + 8 * g + 8, :] for n in range(POLES)]

        def step(t, carry):
            at = pl.ds(pl.multiple_of(t * 16 + 8 * g, 8), 8)
            x, feed = gf[at, :], m[at, :]
            state = tuple(d * s + x for d, s in zip(kept, carry[:POLES]))
            return state + tuple(k + feed * s for k, s in zip(carry[POLES:], state))

        zero = (jnp.zeros((8, LANES), F32),) * (2 * POLES)
        carry = backward_groups(docs, step, zero, POLES)
        for n in range(POLES):
            starts[n * 16 + 8 * g : n * 16 + 8 * g + 8, :] = carry[n]
            totals[n * 16 + 8 * g : n * 16 + 8 * g + 8, :] = carry[POLES + n]
    for p in range(GROUP):
        send[p, 0:16, :] = starts[every(chunk_of(p), POLES), :].astype(BF16)
        send[p, BACK_SUM:BACK_GAIN, :] = totals[every(chunk_of(p), POLES), :].astype(BF16)


def half_adjoint_kernel(docs_mine, ends, back, rate, docs_other, out):
    ids, other = docs_mine[HALF_ROWS:ROW_K, :], docs_other[HALF_ROWS:ROW_K, :]
    same, join = flags_of(ids)
    rates = rate[...]
    through = jnp.exp(-float(TOK) * rates)
    decay = jnp.exp(-rates)
    early = jnp.where(is_late(), 0.0, 1.0)
    met = spread((other[0:1, 0:1] == ids[15:16, LANES - 1 : LANES]).astype(F32)) * early
    total = jnp.zeros((POLES, LANES), F32)
    reach = jnp.zeros((POLES, LANES), F32)
    gains = jnp.zeros((8, LANES), F32)
    carry = jnp.zeros((POLES, LANES), F32)
    unit = met
    for b in reversed(range(GROUP)):
        end = decay * ends[b]
        total = total + back[block_at(b), BACK_SUM:BACK_GAIN, :].astype(F32) + end * carry
        reach = reach + end * unit
        pair = back[block_at(b), BACK_GAIN:ROWS_BACK, :].astype(F32)
        gains = gains + pair[0:8] + pair[8:16]
        carry = back[block_at(b), 0:16, :].astype(F32) + same[b] * through * carry
        unit = same[b] * through * unit
        if b > 0:
            carry = join[b - 1] * carry
            unit = join[b - 1] * unit
    out[0:16, :] = carry
    out[16:32, :] = total
    out[32:48, :] = reach
    out[48:56, :] = gains


def last_pack_kernel(
    docs_mine, back, rate, docs_other, mine, theirs, dq, own, own_got, prev_got, send
):
    ids, other = docs_mine[HALF_ROWS:ROW_K, :], docs_other[HALF_ROWS:ROW_K, :]
    same, join = flags_of(ids)
    rates = rate[...]
    through = jnp.exp(-float(TOK) * rates)
    early = jnp.where(is_late(), 0.0, 1.0)
    met = spread((other[0:1, 0:1] == ids[15:16, LANES - 1 : LANES]).astype(F32)) * early
    late_start = mine[0:16, :] * (1.0 - early) + theirs[0:16, :] * early
    early_reach = mine[32:48, :] * early + theirs[32:48, :] * (1.0 - early)
    residue = mine[16:32, :] + theirs[16:32, :] + late_start * early_reach
    residue = (scaling_of(rates) * residue).astype(BF16)
    pair = pair_rows((mine[48:56, :] + theirs[48:56, :])[0:1])
    carry = theirs[0:16, :] * met
    for b in reversed(range(GROUP)):
        at = block_at(b)
        send[at, 0:OUT_RES, :] = carry.astype(BF16)
        send[at, OUT_RES:OUT_GAIN, :] = residue
        send[at, OUT_GAIN:OUT_Q, :] = pair
        send[at, OUT_Q:OUT_KV, :] = dq[at]
        kv = own[at].astype(F32) + own_got[at].astype(F32) + prev_got[at].astype(F32) * early
        send[at, OUT_KV:ROWS_OUT, :] = kv.astype(BF16)
        if b > 0:
            carry = join[b - 1] * (back[at, 0:16, :].astype(F32) + same[b] * through * carry)


def final_kernel(
    docs, got, gf, dec, wgt, hk, hv, ghk, ghv, gres, ggain, gaq, gak, gav, gm, entry
):
    for p in range(GROUP):
        j = chunk_of(p)
        entry[16 * j : 16 * j + 16, :] = got[p, 0:OUT_RES, :].astype(F32)
        gres[:, lanes(j)] = got[p, OUT_RES:OUT_GAIN, :].astype(F32)
        pair = got[p, OUT_GAIN:OUT_Q, :].astype(F32)
        ggain[:, lanes(j)] = pair[0:1] + pair[8:9]
        rows = slice(64 * (p % 2), 64 * (p % 2) + 64)
        gaq[rows, lanes(p // 2)] = got[p, OUT_Q:OUT_KV, :]
        gak[rows, lanes(p // 2)] = got[p, OUT_KV : OUT_KV + 64, :]
        gav[rows, lanes(p // 2)] = got[p, OUT_KV + 64 : ROWS_OUT, :]
    for g in range(2):
        kept = [dec[n * 16 + 8 * g : n * 16 + 8 * g + 8, :] for n in range(POLES)]
        weights = [wgt[n * 16 + 8 * g : n * 16 + 8 * g + 8, :] for n in range(POLES)]

        def step(t, state):
            at = pl.ds(pl.multiple_of(t * 16 + 8 * g, 8), 8)
            x = gf[at, :]
            state = tuple(d * s + x for d, s in zip(kept, state))
            terms = [w * s for w, s in zip(weights, state)]
            while len(terms) > 1:
                terms = [a + b for a, b in zip(terms[::2], terms[1::2])]
            gm[at, :] = terms[0]
            return state

        start = tuple(entry[every(8 * g * 16 + n, 8), :] for n in range(POLES))
        backward_groups(docs, step, start, POLES)
    for j in range(CHUNKS):
        row = gm[every(j, TOK), :]
        ghk[:, lanes(j)] = (row * hv[:, lanes(j)].astype(F32)).astype(BF16)
        ghv[:, lanes(j)] = (row * hk[:, lanes(j)].astype(F32)).astype(BF16)


def place(keys, values, b, at_core, key_rows, value_rows):
    at = pl.ds(pl.multiple_of(TOK * b + 64 * at_core, 64), 64)
    keys[at, :] = key_rows
    values[at, :] = value_rows


def turn_keys(keys, turned):
    def one(t, _):
        at = pl.ds(pl.multiple_of(t * KEYS_TILE, KEYS_TILE), KEYS_TILE)
        turned[t] = keys[at, :].astype(F32).T.astype(BF16)
        return 0

    lax.fori_loop(0, HALF_TILES, one, 0)


def own_keys_kernel(got, kv, kv_core, keys, values, turned, rows_q, rows_g, turned_q, turned_g):
    core = core_of()
    for i in range(Q_TILES):
        for u in range(4):
            part = slice(64 * u, 64 * u + 64)
            rows_q[i, part, :] = got[block_at(4 * i + u), ROW_Q:ROW_G, :]
            rows_g[i, part, :] = got[block_at(4 * i + u), ROW_G:ROWS_IN, :]
        turned_q[i] = rows_q[i].astype(F32).T.astype(BF16)
        turned_g[i] = rows_g[i].astype(F32).T.astype(BF16)
    for b in range(GROUP):
        s = block_at(b)
        place(keys, values, b, core, kv[s, 0:64, :], kv[s, 64:128, :])
        place(keys, values, b, 1 - core, kv_core[s, 0:64, :], kv_core[s, 64:128, :])
    turn_keys(keys, turned)


def sums_kernel(s0, s1, s2, s3, total):
    total[...] = s0[...] + s1[...] + s2[...] + s3[...]


def send_keys_kernel(kv, after, out):
    out[...] = kv[...]


def attention_kernel(
    all_q, all_g, all_turned_q, all_turned_g, own_k, own_v, own_turned, kv_half, kv_half_core,
    ids_mine, ids_other, after,
    dq, own, own_send, prev, prev_send, token,
    prev_k, prev_v, prev_turned, scores, products, peaks, dk, dv,
):
    core = core_of()
    late = is_late()
    token[...] = jnp.zeros((8, LANES), F32)

    @pl.when(late)
    def _():
        for b in range(GROUP):
            place(prev_k, prev_v, b, core, kv_half[b, 0:64, :], kv_half[b, 64:128, :])
            place(
                prev_k, prev_v, b, 1 - core, kv_half_core[b, 0:64, :], kv_half_core[b, 64:128, :]
            )
        turn_keys(prev_k, prev_turned)

    def clear(t, _):
        at = pl.ds(pl.multiple_of(t * KEYS_TILE, KEYS_TILE), KEYS_TILE)
        dk[at, :] = jnp.zeros((KEYS_TILE, HEAD_DIM), F32)
        dv[at, :] = jnp.zeros((KEYS_TILE, HEAD_DIM), F32)
        return 0

    lax.fori_loop(jnp.where(late, 0, HALF_TILES), N_TILES, clear, 0)

    own_ids, other_ids = ids_mine[HALF_ROWS:ROW_K, :], ids_other[HALF_ROWS:ROW_K, :]
    base = jnp.where(late, 0, HALF)
    starts = []
    for d in (1, 2, 3):
        before = jnp.sum((own_ids < d).astype(F32)).astype(jnp.int32)
        behind = jnp.sum((other_ids < d).astype(F32)).astype(jnp.int32)
        starts.append(before + jnp.where(late, behind, HALF))

    def start_of(pos):
        result = jnp.where(pos >= starts[0], starts[0], base)
        for start in starts[1:]:
            result = jnp.where(pos >= start, start, result)
        return result

    def query_tile(i, _):
        rows_q, rows_g = all_q[i], all_g[i]
        turned_q, turned_g = all_turned_q[i], all_turned_g[i]
        lane = lax.broadcasted_iota(jnp.int32, (1, ROWS_TILE), 1)
        qpos = HALF + 512 * i + 128 * (lane // 64) + 64 * core + lax.rem(lane, 64)
        qstart = start_of(qpos)
        low = start_of(HALF + 512 * i + 64 * core) // KEYS_TILE
        high = HALF // KEYS_TILE + i + 1
        row = lax.broadcasted_iota(jnp.int32, (CHUNK, ROWS_TILE), 0)

        def fold(value, by):
            return by(value.reshape(CHUNK // 8, 8, ROWS_TILE), axis=0)

        def first_pass(keys, values, base, t, carry):
            peak, total, weighted = carry
            for u in range(KEYS_TILE // CHUNK):
                first = t * KEYS_TILE + u * CHUNK
                at = pl.ds(pl.multiple_of(first - base * KEYS_TILE, CHUNK), CHUNK)
                s = jnp.dot(keys[at, :], turned_q, preferred_element_type=F32)
                gp = jnp.dot(values[at, :], turned_g, preferred_element_type=F32)
                s = jnp.where((row <= qpos - first) & (row >= qstart - first), s, FLOOR_SCORE)
                top = jnp.maximum(peak, jnp.max(fold(s, jnp.max), axis=0, keepdims=True))
                p = jnp.exp2((s - top) * (SCALE * LOG2E))
                scores[t, u * CHUNK : u * CHUNK + CHUNK, :] = p
                products[t, u * CHUNK : u * CHUNK + CHUNK, :] = gp
                peaks[t, u : u + 1, :] = top
                shrink = jnp.exp2((peak - top) * (SCALE * LOG2E))
                total = total * shrink + fold(p, jnp.sum)
                weighted = weighted * shrink + fold(p * gp, jnp.sum)
                peak = top
            return peak, total, weighted

        zero = jnp.zeros((8, ROWS_TILE), F32)
        floor = jnp.full((1, ROWS_TILE), FLOOR_SCORE, F32)
        ahead = functools.partial(first_pass, prev_k, prev_v, 0)
        carry = lax.fori_loop(low, HALF_TILES, ahead, (floor, zero, zero))
        within = functools.partial(first_pass, own_k, own_v, HALF_TILES)
        middle = jnp.maximum(low, HALF_TILES)
        peak, total, weighted = lax.fori_loop(middle, high, within, carry)
        inv = 1.0 / jnp.sum(total, axis=0, keepdims=True)
        centre = jnp.sum(weighted, axis=0, keepdims=True) * inv

        def second_pass(turned, base, t, turned_dq):
            for v in range(KEYS_TILE // STEP):
                parts = []
                for u in range(v * STEP // CHUNK, (v + 1) * STEP // CHUNK):
                    rows = slice(u * CHUNK, u * CHUNK + CHUNK)
                    fall = jnp.exp2((peaks[t, u : u + 1, :] - peak) * (SCALE * LOG2E)) * inv
                    p = scores[t, rows, :] * fall
                    parts.append((p.astype(BF16), (p * (products[t, rows, :] - centre)).astype(BF16)))
                p = jnp.concatenate([one for one, _ in parts], axis=0)
                ds = jnp.concatenate([one for _, one in parts], axis=0)
                at = pl.ds(pl.multiple_of(t * KEYS_TILE + v * STEP, STEP), STEP)
                dk[at, :] += jnp.dot(ds, rows_q, preferred_element_type=F32)
                dv[at, :] += jnp.dot(p, rows_g, preferred_element_type=F32)
                part = turned[t - base, :, v * STEP : v * STEP + STEP]
                turned_dq = turned_dq + jnp.dot(part, ds, preferred_element_type=F32)
            return turned_dq

        zero = jnp.zeros((HEAD_DIM, ROWS_TILE), F32)
        ahead = functools.partial(second_pass, prev_turned, 0)
        turned_dq = lax.fori_loop(low, HALF_TILES, ahead, zero)
        within = functools.partial(second_pass, own_turned, HALF_TILES)
        turned_dq = lax.fori_loop(middle, high, within, turned_dq)
        rows = (turned_dq * SCALE).T.astype(BF16)
        for u in range(4):
            dq[block_at(4 * i + u)] = rows[64 * u : 64 * u + 64]
        return 0

    lax.fori_loop(0, Q_TILES, query_tile, 0)

    def leave(base, target, target_send, order):
        for b in range(GROUP):
            s = order(b)
            for at_core, ref in ((core, target), (1 - core, target_send)):
                at = pl.ds(pl.multiple_of(base + TOK * b + 64 * at_core, 64), 64)
                ref[s, 0:64, :] = (dk[at, :] * SCALE).astype(BF16)
                ref[s, 64:128, :] = dv[at, :].astype(BF16)

    leave(HALF, own, own_send, block_at)

    @pl.when(late)
    def _():
        leave(0, prev, prev_send, lambda b: b)


def body(
    hyena_q, hyena_k, hyena_v, hyena_grad, pole_rate, residue, norm_gain, doc_ids,
    attn_q, attn_k, attn_v, attn_grad,
):
    count = 2 * GROUP
    early = list(range(GROUP))
    late = [GROUP + (p ^ 8) for p in early]
    swap_core = [(i, i ^ 1) for i in range(count)]
    up_half = list(zip(early, late))
    down_half = list(zip(late, early))
    swap_half = up_half + down_half

    def exchange(x):
        return lax.all_to_all(x, "ctx", 0, 0, tiled=True, axis_index_groups=[early, late])

    gain = norm_gain.reshape(1, CH)
    sweep = (TOK * CHUNKS, LANES)
    params = (POLES * CHUNKS, LANES)
    vmem = pltpu.VMEM
    hbm = pl.BlockSpec(memory_space=pltpu.HBM)
    send, m, dec, wgt, through, rate_part = call(
        first_kernel,
        [((GROUP, ROWS_IN, LANES), BF16), (sweep, F32), (params, F32), (params, F32)]
        + [(half_shape, F32), ((POLES, LANES), F32)],
        doc_ids, doc_ids.reshape(1, TOK), pole_rate, residue, hyena_k, hyena_v,
        attn_k, attn_v, attn_q, attn_grad,
        smem=(0,), specs={i: hbm for i in range(2, 10)}, far=(0, 1),
        scratch=[vmem(params, F32)] + [vmem((POLES, CH), F32)] * 2 + [vmem((TOK, CH), BF16)] * 2
        + [vmem((TOK, 1024), BF16)] * 4 + [vmem(sweep, F32), vmem((GROUP, HALF_ROWS, LANES), BF16)]
        + [vmem((GROUP, ROWS_IN - ROW_DOC, LANES), BF16), pltpu.SemaphoreType.DMA((11,))],
        flops=40_000_000, nbytes=6_000_000, vmem=60 << 20,
    )
    got = exchange(send)
    mine, local, ends = call(
        half_state_kernel,
        [((ROW_K, LANES), F32), ((4,) + half_shape, F32), ((GROUP, POLES, LANES), F32)],
        got, through, scratch=[vmem((GROUP, 3) + half_shape, F32)],
        flops=1_000_000, nbytes=300_000,
    )
    other = lax.ppermute(mine, "ctx", swap_half)
    part = (GROUP, TOK, HEAD_DIM)
    (kv,) = call(keys_kernel, [(part, BF16)], got, flops=1000, nbytes=1_000_000)
    kv_core = lax.ppermute(kv, "ctx", swap_core)
    (kv_later,) = call(
        send_keys_kernel, [(part, BF16)], kv, other, flops=1000, nbytes=1_000_000
    )
    kv_half = lax.ppermute(kv_later, "ctx", up_half)
    flat = (HALF, HEAD_DIM)
    turned = (HALF_TILES, HEAD_DIM, KEYS_TILE)
    tall, wide = (Q_TILES, ROWS_TILE, HEAD_DIM), (Q_TILES, HEAD_DIM, ROWS_TILE)
    own_k, own_v, own_turned, *query_parts = call(
        own_keys_kernel,
        [(flat, BF16), (flat, BF16), (turned, BF16)] + [(tall, BF16)] * 2 + [(wide, BF16)] * 2,
        got, kv, kv_core,
        flops=1_000_000, nbytes=4_000_000,
    )
    carry, carry_send = call(
        entry_kernel, [(half_shape, F32)] * 2, local, mine, other, flops=100_000, nbytes=300_000
    )
    carry_got = lax.ppermute(carry_send, "ctx", swap_core)
    f, sums = call(
        forward_kernel, [(sweep, F32), ((8, LANES), F32)],
        doc_ids, carry, carry_got, m, dec, wgt, hyena_q, hyena_grad, gain,
        smem=(0,), flops=40_000_000, nbytes=6_000_000,
    )
    shared = [
        lax.ppermute(sums, "chan", [(i, (i + k) % 4) for i in range(4)]) for k in (1, 2, 3)
    ]
    (sums,) = call(
        sums_kernel, [((8, LANES), F32)], sums, *shared, flops=1000, nbytes=10_000
    )
    (kv_half,) = call(
        send_keys_kernel, [(part, BF16)], kv_half, sums, flops=1000, nbytes=1_000_000
    )
    kv_half_core = lax.ppermute(kv_half, "ctx", swap_core)
    dq, own, own_send, prev, prev_send, after = call(
        attention_kernel,
        [((GROUP, 64, HEAD_DIM), BF16)] + [(part, BF16)] * 4 + [((8, LANES), F32)],
        *query_parts, own_k, own_v, own_turned, kv_half, kv_half_core, mine, other, sums,
        scratch=[
            vmem(flat, BF16),
            vmem(flat, BF16),
            vmem(turned, BF16),
            vmem((N_TILES, KEYS_TILE, ROWS_TILE), F32),
            vmem((N_TILES, KEYS_TILE, ROWS_TILE), F32),
            vmem((N_TILES, 8, ROWS_TILE), F32),
            vmem((2 * HALF, HEAD_DIM), F32),
            vmem((2 * HALF, HEAD_DIM), F32),
        ],
        flops=10_000_000_000, nbytes=6_000_000, vmem=28 << 20,
    )
    ghq, gf, back_send = call(
        backward_kernel,
        [((TOK, CH), BF16), (sweep, F32), ((GROUP, ROWS_BACK, LANES), BF16)],
        doc_ids, sums, after, f, m, dec, hyena_q, hyena_grad, gain,
        smem=(0,), scratch=[vmem(params, F32), vmem(params, F32)],
        flops=40_000_000, nbytes=6_000_000,
    )
    prev_got = lax.ppermute(prev_send, "ctx", swap_core)
    own_got = lax.ppermute(own_send, "ctx", swap_core)
    back_send, prev_got = lax.optimization_barrier((back_send, prev_got))
    prev_sum = (prev.astype(F32) + prev_got.astype(F32)).astype(BF16)
    prev_home = lax.ppermute(prev_sum, "ctx", down_half)
    back = exchange(back_send)
    (half_mine,) = call(
        half_adjoint_kernel, [((56, LANES), F32)], mine, ends, back, rate_part, other,
        flops=1_000_000, nbytes=300_000,
    )
    half_other = lax.ppermute(half_mine, "ctx", swap_half)
    (last_send,) = call(
        last_pack_kernel, [((GROUP, ROWS_OUT, LANES), BF16)],
        mine, back, rate_part, other, half_mine, half_other, dq, own, own_got, prev_home,
        flops=1_000_000, nbytes=3_000_000,
    )
    last = exchange(last_send)
    ghk, ghv, gres, ggain, gaq, gak, gav = call(
        final_kernel,
        [((TOK, CH), BF16), ((TOK, CH), BF16), ((POLES, CH), F32), ((1, CH), F32)]
        + [((TOK, 1024), BF16)] * 3,
        doc_ids, last, gf, dec, wgt, hyena_k, hyena_v,
        smem=(0,), scratch=[vmem(sweep, F32), vmem(params, F32)],
        flops=40_000_000, nbytes=6_000_000,
    )
    return (ghq, ghk, ghv, gres, ggain.reshape(CH), gaq, gak, gav)


def solution(mesh):
    wide, deep, one = P("ctx", "chan"), P(None, "chan"), P("chan")
    return jax.shard_map(
        body,
        mesh=mesh,
        in_specs=(wide,) * 4 + (deep, deep, one, P("ctx")) + (wide,) * 4,
        out_specs=(wide, wide, wide, deep, one, wide, wide, wide),
        check_vma=False,
    )
```
